32 devices in a mesh: dp: 8 (over y, x, core), sub: 4 (over z).
Axes of the slice: x: 2, y: 2, z: 4, core: 2. Of those that a mesh axis runs over, the one named last changes fastest.
Arguments:
- frames: bfloat16 [768, 196, 512], P(('dp', 'sub')), may hold values from -6 to 6
- valid: int32 [768, 196], P(('dp', 'sub')), may hold values from 0 to 1, as said below
- memory: bfloat16 [768, 96, 512], P(('dp', 'sub')), may hold values from -6 to 6
- ct_memory: bfloat16 [768, 96, 512], P(('dp', 'sub')), may hold values from -6 to 6
- ct_read: bfloat16 [768, 16, 512], P(('dp', 'sub')), may hold values from -6 to 6
- attn: float32 [4, 512, 512], P(None, ('dp', 'sub')), may hold values from -0.25 to 0.25
- w_in: float32 [512, 2048], P(('dp', 'sub')), may hold values from -0.25 to 0.25
- w_out: float32 [2048, 512], P(('dp', 'sub')), may hold values from -0.125 to 0.125
- s_read: float32 [512, 16], P(('dp', 'sub')), may hold values from -0.25 to 0.25
- s_write: float32 [512, 96], P(('dp', 'sub')), may hold values from -0.25 to 0.25
- gains: float32 [4, 512], P(None, ('dp', 'sub')), may hold values from 0.5 to 1.5
- bias: float32 [2048], P(('dp', 'sub')), may hold values from -3 to 3
- attn_mom: float32 [4, 512, 512], P(None, ('dp', 'sub')), may hold values from -300 to 300
- w_in_mom: float32 [512, 2048], P(('dp', 'sub')), may hold values from -300 to 300
- w_out_mom: float32 [2048, 512], P(('dp', 'sub')), may hold values from -300 to 300
- s_read_mom: float32 [512, 16], P(('dp', 'sub')), may hold values from -300 to 300
- s_write_mom: float32 [512, 96], P(('dp', 'sub')), may hold values from -300 to 300
- gains_first: float32 [4, 512], P(None, ('dp', 'sub')), may hold values from -300 to 300
- gains_second: float32 [4, 512], P(None, ('dp', 'sub')), may hold values from 100 to 10000
- bias_first: float32 [2048], P(('dp', 'sub')), may hold values from -300 to 300
- bias_second: float32 [2048], P(('dp', 'sub')), may hold values from 100 to 10000
Outputs:
- new_memory: bfloat16 [768, 96, 512], P(('dp', 'sub'))
- read_out: bfloat16 [768, 16, 512], P(('dp', 'sub'))
- grad_frames: bfloat16 [768, 196, 512], P(('dp', 'sub'))
- grad_memory: bfloat16 [768, 96, 512], P(('dp', 'sub'))
- grad_attn: float32 [4, 512, 512], P(None, ('dp', 'sub'))
- grad_w_in: float32 [512, 2048], P(('dp', 'sub'))
- grad_w_out: float32 [2048, 512], P(('dp', 'sub'))
- grad_s_read: float32 [512, 16], P(('dp', 'sub'))
- grad_s_write: float32 [512, 96], P(('dp', 'sub'))
- grad_gains: float32 [4, 512], P(None, ('dp', 'sub'))
- grad_bias: float32 [2048], P(('dp', 'sub'))
- next_attn: float32 [4, 512, 512], P(None, ('dp', 'sub'))
- next_w_in: float32 [512, 2048], P(('dp', 'sub'))
- next_w_out: float32 [2048, 512], P(('dp', 'sub'))
- next_s_read: float32 [512, 16], P(('dp', 'sub'))
- next_s_write: float32 [512, 96], P(('dp', 'sub'))
- next_gains: float32 [4, 512], P(None, ('dp', 'sub'))
- next_bias: float32 [2048], P(('dp', 'sub'))
- next_attn_mom: float32 [4, 512, 512], P(None, ('dp', 'sub'))
- next_w_in_mom: float32 [512, 2048], P(('dp', 'sub'))
- next_w_out_mom: float32 [2048, 512], P(('dp', 'sub'))
- next_s_read_mom: float32 [512, 16], P(('dp', 'sub'))
- next_s_write_mom: float32 [512, 96], P(('dp', 'sub'))
- next_gains_first: float32 [4, 512], P(None, ('dp', 'sub'))
- next_gains_second: float32 [4, 512], P(None, ('dp', 'sub'))
- next_bias_first: float32 [2048], P(('dp', 'sub'))
- next_bias_second: float32 [2048], P(('dp', 'sub'))
The draws below stay inside these ranges and needn't reach their ends.
Inputs may be any that keep to these rules, and one draw needn't show every extreme that they name: `valid`: each clip's row is 196 ones, or 100 ones followed by zeros.
All inputs are finite; a program needn't handle non-finite values.
Results may differ from the reference program's by a relative error of at most 0.035.
Values may be sent and summed in bfloat16 or wider, within the bound.
A program may use at most 320 MiB of HBM per device.

```python
import math
import jax
import jax.numpy as jnp
from jax import lax

D = 512
HEADS = 8
HEAD_DIM = 64
FF = 2048
MEM = 96
READ = 16
TOKS = 196
SHORT = 100
CLIPS = 768


def draw_valid(key, part):
    coins = jax.random.randint(key, (CLIPS,), 0, 2)
    lengths = jnp.where(coins > 0, TOKS, SHORT)
    positions = jnp.arange(TOKS)
    return (positions[None, :] < lengths[:, None]).astype(jnp.int32)


def block_levels(rng, dims, shards, least, top_value):
    level = 1.0
    for dim, parts in shards:
        steps = jax.random.uniform(jax.random.fold_in(jax.random.fold_in(rng, 6), dim), (parts,), jnp.float32, least / len(shards), top_value / len(shards))
        level = level * jnp.repeat(jnp.exp(steps), dims[dim] // parts).reshape((-1,) + (1,) * (len(dims) - 1 - dim))
    return level


def bell_draw(stream_key, extent, spread, most, cuts=(), kind=jnp.bfloat16):
    level = block_levels(stream_key, extent, cuts, -0.22, 0.18) if cuts else 1.0
    entries = jax.random.normal(stream_key, extent, jnp.float32) * spread * level
    return jnp.minimum(jnp.maximum(entries, -most), most).astype(kind)


def setup_inputs(seed: int = 0) -> dict:
    splits = jax.random.split(jax.random.key(seed), 22)
    return {
        "frames": bell_draw(splits[0], (CLIPS, TOKS, D), 1.0, 6.0, ((0, 32),)),
        "valid": draw_valid(jax.random.fold_in(splits[21], 71), 0),
        "memory": bell_draw(splits[2], (CLIPS, MEM, D), 1.0, 6.0, ((0, 32),)),
        "ct_memory": bell_draw(splits[3], (CLIPS, MEM, D), 1.0, 6.0, ((0, 32),)),
        "ct_read": bell_draw(splits[4], (CLIPS, READ, D), 1.0, 6.0, ((0, 32),)),
        "attn": bell_draw(splits[5], (4, D, D), D ** -0.5, 0.25, ((1, 32),), jnp.float32),
        "w_in": bell_draw(splits[6], (D, FF), D ** -0.5, 0.25, ((0, 32),), jnp.float32),
        "w_out": bell_draw(splits[7], (FF, D), FF ** -0.5, 0.125, ((0, 32),), jnp.float32),
        "s_read": bell_draw(splits[8], (D, READ), D ** -0.5, 0.25, ((0, 32),), jnp.float32),
        "s_write": bell_draw(splits[9], (D, MEM), D ** -0.5, 0.25, ((0, 32),), jnp.float32),
        "gains": jnp.clip(1.0 + 0.1 * jax.random.normal(splits[10], (4, D), jnp.float32), 0.5, 1.5),
        "bias": bell_draw(splits[11], (FF,), 0.5, 3.0, ((0, 32),), jnp.float32),
        "attn_mom": bell_draw(splits[12], (4, D, D), 50.0, 300.0, ((1, 32),), jnp.float32),
        "w_in_mom": bell_draw(splits[13], (D, FF), 50.0, 300.0, ((0, 32),), jnp.float32),
        "w_out_mom": bell_draw(splits[14], (FF, D), 50.0, 300.0, ((0, 32),), jnp.float32),
        "s_read_mom": bell_draw(splits[15], (D, READ), 50.0, 300.0, ((0, 32),), jnp.float32),
        "s_write_mom": bell_draw(splits[16], (D, MEM), 50.0, 300.0, ((0, 32),), jnp.float32),
        "gains_first": bell_draw(splits[17], (4, D), 50.0, 300.0, ((1, 32),), jnp.float32),
        "gains_second": jnp.clip(jnp.exp(math.log(10000.0) - 4.6051702 * jax.random.uniform(splits[18], (4, D), jnp.float32) ** block_levels(splits[18], (4, D), ((1, 32),), -0.2, 0.2)), 100.0, 10000.0),
        "bias_first": bell_draw(splits[19], (FF,), 50.0, 300.0, ((0, 32),), jnp.float32),
        "bias_second": jnp.clip(jnp.exp(math.log(10000.0) - 4.6051702 * jax.random.uniform(splits[20], (FF,), jnp.float32) ** block_levels(splits[20], (FF,), ((0, 32),), -0.2, 0.2)), 100.0, 10000.0),
    }


highest = lax.Precision.HIGHEST
norm_eps = 1e-06
masked_logit = -1000000000.0
ns_first = 3.4445
ns_second = -4.775
ns_third = 2.0315
mom_decay = 0.5
muon_rate = 1.0
adam_decay_first = 0.5
adam_decay_second = 0.5
adam_rate = 0.25
adam_count = 10.0
adam_eps = 1e-08
clip_block = 16

@jax.custom_vjp
def low(v):
    return lax.optimization_barrier(v.astype(jnp.bfloat16)).astype(jnp.float32)

@jax.custom_vjp
def low_back(v):
    return v

def low_keep(v):
    return (low(v), None)

def low_pass(kept, grad):
    return (grad,)

def back_keep(v):
    return (v, None)

def back_low(kept, grad):
    return (low(grad),)
low.defvjp(low_keep, low_pass)
low_back.defvjp(back_keep, back_low)

def rms_norm(values, gain):
    return values * lax.rsqrt(lax.optimization_barrier(jnp.mean(values * values, axis=-1, keepdims=True)) + norm_eps) * gain

def summarize(tokens, live, gain, table):
    normed = low(rms_norm(tokens, gain))
    logits = low_back(jnp.einsum('cnd,dk->cnk', normed, table, precision=highest))
    logits = jnp.where(live[:, :, None], logits, masked_logit)
    weights = low(jax.nn.softmax(logits, axis=1))
    return jnp.einsum('cnk,cnd->ckd', weights, tokens, precision=highest)

def forward(frames, memory, valid, params):
    attn, w_in, w_out, s_read, s_write, gains, bias = [low(item) for item in params]
    clip_count = frames.shape[0]
    frame_live = valid > 0
    memory_live = jnp.ones((clip_count, MEM), dtype=bool)
    read_in = jnp.concatenate([memory, frames], axis=1)
    read_live = jnp.concatenate([memory_live, frame_live], axis=1)
    summary = low_back(summarize(read_in, read_live, gains[0], s_read))
    hidden = low(rms_norm(summary, gains[1]))

    def project(matrix):
        made = jnp.einsum('crd,de->cre', hidden, matrix, precision=highest)
        return low(low_back(made)).reshape(clip_count, READ, HEADS, HEAD_DIM)
    queries = project(attn[0])
    key_rows = project(attn[1])
    value_rows = project(attn[2])
    scores = low_back(jnp.einsum('cqhe,ckhe->chqk', queries, key_rows, precision=highest))
    probs = low(jax.nn.softmax(scores * HEAD_DIM ** (-0.5), axis=-1))
    context = jnp.einsum('chqk,ckhe->cqhe', probs, value_rows, precision=highest).reshape(clip_count, READ, D)
    context = low(low_back(context))
    after_attn = summary + low_back(jnp.einsum('crd,de->cre', context, attn[3], precision=highest))
    normed_mlp = low(rms_norm(after_attn, gains[2]))
    pre_act = low_back(jnp.einsum('crd,df->crf', normed_mlp, w_in, precision=highest) + bias)
    activ = low(jax.nn.gelu(pre_act))
    after_mlp = after_attn + low_back(jnp.einsum('crf,fd->crd', activ, w_out, precision=highest))
    read_out = low(after_mlp)
    write_in = jnp.concatenate([memory, read_out, frames], axis=1)
    write_live = jnp.concatenate([memory_live, jnp.ones((clip_count, READ), dtype=bool), frame_live], axis=1)
    new_memory = summarize(write_in, write_live, gains[3], s_write)
    return (new_memory, read_out)

def orthogonalize(matrix):
    tall = matrix.shape[0] > matrix.shape[1]
    current = matrix.T if tall else matrix
    current = current / (jnp.sqrt(jnp.sum(current * current)) + 1e-07)
    for sweep in range(5):
        square = jnp.dot(current, current.T, precision=highest)
        mixed = ns_second * square + ns_third * jnp.dot(square, square, precision=highest)
        current = ns_first * current + jnp.dot(mixed, current, precision=highest)
    return current.T if tall else current

def muon_step(weight, moment, grad_sum):
    moment_new = mom_decay * moment + grad_sum
    ratio = max(1.0, weight.shape[0] / weight.shape[1]) ** 0.5
    return (weight - muon_rate * ratio * orthogonalize(moment_new), moment_new)

def adam_step(weight, first, second, grad_sum):
    first_new = adam_decay_first * first + (1.0 - adam_decay_first) * grad_sum
    second_new = adam_decay_second * second + (1.0 - adam_decay_second) * grad_sum * grad_sum
    first_hat = first_new / (1.0 - adam_decay_first ** adam_count)
    second_hat = second_new / (1.0 - adam_decay_second ** adam_count)
    return (weight - adam_rate * first_hat / (jnp.sqrt(second_hat) + adam_eps), first_new, second_new)

def reference(frames, valid, memory, ct_memory, ct_read, attn, w_in, w_out, s_read, s_write, gains, bias, attn_mom, w_in_mom, w_out_mom, s_read_mom, s_write_mom, gains_first, gains_second, bias_first, bias_second):
    params = (attn, w_in, w_out, s_read, s_write, gains, bias)
    block_count = frames.shape[0] // clip_block

    def split_blocks(values):
        return values.reshape((block_count, clip_block) + values.shape[1:])

    def merge_blocks(values):
        return values.reshape((block_count * clip_block,) + values.shape[2:])

    def one_block(totals, item):
        frame_blk, valid_blk, memory_blk, ct_mem_blk, ct_read_blk = item

        def run_block(frame_f, memory_f, weights):
            return forward(frame_f, memory_f, valid_blk, weights)
        outputs, back_fn = jax.vjp(run_block, frame_blk.astype(jnp.float32), memory_blk.astype(jnp.float32), params)
        grad_frame, grad_mem, grad_weights = back_fn((ct_mem_blk.astype(jnp.float32), ct_read_blk.astype(jnp.float32)))
        totals = jax.tree.map(jnp.add, totals, grad_weights)
        return (totals, (outputs[0].astype(jnp.bfloat16), outputs[1].astype(jnp.bfloat16), grad_frame.astype(jnp.bfloat16), grad_mem.astype(jnp.bfloat16)))
    zeros_init = jax.tree.map(jnp.zeros_like, params)
    grads, stacked = lax.scan(one_block, zeros_init, (split_blocks(frames), split_blocks(valid), split_blocks(memory), split_blocks(ct_memory), split_blocks(ct_read)))
    new_memory, read_out, grad_frames, grad_memory = [merge_blocks(item) for item in stacked]
    grad_attn, grad_w_in, grad_w_out, grad_s_read, grad_s_write, grad_gains, grad_bias = grads
    attn_results = [muon_step(attn[position], attn_mom[position], grad_attn[position]) for position in range(4)]
    next_attn = jnp.stack([result_pair[0] for result_pair in attn_results])
    next_attn_mom = jnp.stack([result_pair[1] for result_pair in attn_results])
    next_w_in, next_w_in_mom = muon_step(w_in, w_in_mom, grad_w_in)
    next_w_out, next_w_out_mom = muon_step(w_out, w_out_mom, grad_w_out)
    next_s_read, next_s_read_mom = muon_step(s_read, s_read_mom, grad_s_read)
    next_s_write, next_s_write_mom = muon_step(s_write, s_write_mom, grad_s_write)
    next_gains, next_gains_first, next_gains_second = adam_step(gains, gains_first, gains_second, grad_gains)
    next_bias, next_bias_first, next_bias_second = adam_step(bias, bias_first, bias_second, grad_bias)
    return (new_memory, read_out, grad_frames, grad_memory, grad_attn, grad_w_in, grad_w_out, grad_s_read, grad_s_write, grad_gains, grad_bias, next_attn, next_w_in, next_w_out, next_s_read, next_s_write, next_gains, next_bias, next_attn_mom, next_w_in_mom, next_w_out_mom, next_s_read_mom, next_s_write_mom, next_gains_first, next_gains_second, next_bias_first, next_bias_second)
```

```python
import functools
import math

import jax
import jax.numpy as jnp
from jax import lax
from jax.experimental import pallas as pl
from jax.experimental.pallas import tpu as pltpu
from jax.sharding import PartitionSpec as P

f32 = jnp.float32
bf16 = jnp.bfloat16

HEADS = 8
HEAD_DIM = 64
NORM_EPS = 1e-06
MASKED = -1000000000.0
GELU_A = math.sqrt(2.0 / math.pi)
GELU_B = 0.044715

ROWS = 16
PACK = 208
SMALL = 192


def dot(a, b, ca=1, cb=0):
    return lax.dot_general(a, b, (((ca,), (cb,)), ((), ())), preferred_element_type=f32)


def step_kernel(
    clips,
    frames_h,
    valid_ref,
    memory_h,
    ctm_h,
    ctr_ref,
    wpack_h,
    nm_h,
    ro_ref,
    gf_h,
    gm_h,
    gpack_ref,
    zm,
    zf,
    ctm,
    nm,
    wmat,
    wout,
    small,
    table,
    gain,
    bias,
    arm,
    arf,
    aread_m,
    aread_f,
    lread_m,
    lread_f,
    rm_s,
    rf_s,
    cm_s,
    cf_s,
    summary,
    queries,
    keys,
    values,
    probs,
    context,
    after,
    normed,
    dgelu,
    activ,
    gafter,
    gsum,
    acc_w,
    acc_r,
    in_sem,
    w_sem,
    out_sem,
):
    mem, read = memory_h.shape[1], ROWS
    toks = frames_h.shape[1]
    rows = clips * read
    groups = wpack_h.shape[0]
    width = zm.shape[2]
    wide = mem + read

    def in_copies(c):
        return (
            pltpu.make_async_copy(memory_h.at[c], zm.at[c, pl.ds(read, mem)], in_sem.at[0, c]),
            pltpu.make_async_copy(frames_h.at[c], zf.at[c], in_sem.at[1, c]),
        )

    def ct_copy(c):
        return pltpu.make_async_copy(ctm_h.at[c], ctm.at[c], in_sem.at[2, c])

    small_copy = pltpu.make_async_copy(
        wpack_h.at[:, pl.ds(SMALL, ROWS)], small, w_sem.at[9]
    )
    w_copies = [
        pltpu.make_async_copy(
            wpack_h.at[:, pl.ds(ROWS * m, ROWS)], wmat.at[m], w_sem.at[m]
        )
        for m in range(8)
    ] + [pltpu.make_async_copy(wpack_h.at[:, pl.ds(128, 64)], wout, w_sem.at[8])]

    small_copy.start()

    @pl.loop(0, clips)
    def _(c):
        for copy in in_copies(c):
            copy.start()

    for copy in w_copies:
        copy.start()

    @pl.loop(0, clips)
    def _(c):
        ct_copy(c).start()

    small_copy.wait()
    flat = small[:, :, 0:128].reshape(groups * ROWS, 128).astype(f32)
    turned = flat.T
    gain[...] = turned[112:120]
    table[0:mem] = (turned[0:mem] * turned[115:116]).astype(bf16)
    table[mem:wide] = (turned[mem:wide] * turned[112:113]).astype(bf16)
    piece = bias.shape[1] // groups
    for d in range(groups):
        bias[:, piece * d : piece * (d + 1)] = small[d, 0:1, 128 : 128 + piece].astype(f32)

    ones = jnp.ones((8, width), bf16)
    memory_lane = lax.broadcasted_iota(jnp.int32, (1, wide), 1) >= read

    @pl.loop(0, clips)
    def _(c):
        zm[c, 0:read] = jnp.zeros((read, width), bf16)
        for copy in in_copies(c):
            copy.wait()
        z_m, z_f = zm[c], zf[c]
        r_m = lax.rsqrt(dot(ones, z_m * z_m, 1, 1) * (1.0 / width) + NORM_EPS)
        r_f = lax.rsqrt(dot(ones, z_f * z_f, 1, 1) * (1.0 / width) + NORM_EPS)
        rm_s[c], rf_s[c] = r_m, r_f
        tab = table[mem:wide]
        live = valid_ref[pl.ds(c, 1), :] > 0
        l_m = jnp.where(memory_lane, dot(tab, z_m, 1, 1) * r_m[0:1], MASKED)
        l_f = jnp.where(live, dot(tab, z_f, 1, 1) * r_f[0:1], MASKED)
        top = jnp.maximum(
            jnp.max(l_m, axis=1, keepdims=True), jnp.max(l_f, axis=1, keepdims=True)
        )
        e_m, e_f = jnp.exp(l_m - top), jnp.exp(l_f - top)
        inv = 1.0 / (
            jnp.sum(e_m, axis=1, keepdims=True) + jnp.sum(e_f, axis=1, keepdims=True)
        )
        a_m, a_f = e_m * inv, e_f * inv
        lread_m[c], lread_f[c] = l_m, l_f
        aread_m[c], aread_f[c] = a_m, a_f
        h_m, h_f = a_m.astype(bf16), a_f.astype(bf16)
        arm[c, 2 * mem : 2 * mem + read] = h_m
        arf[c, 2 * mem : 2 * mem + read] = h_f
        summary[pl.ds(c * read, read)] = dot(h_m, z_m) + dot(h_f, z_f)

    for copy in w_copies:
        copy.wait()

    def mat(m):
        return wmat[m].reshape(groups * ROWS, width)

    def unit(v):
        return lax.rsqrt(jnp.mean(v * v, axis=-1, keepdims=True) + NORM_EPS)

    summ = summary[...]
    hidden = (summ * unit(summ) * gain[1:2]).astype(bf16)
    normed[...] = hidden
    queries[...] = dot(hidden, mat(0)).astype(bf16)
    keys[...] = dot(hidden, mat(1)).astype(bf16)
    values[...] = dot(hidden, mat(2)).astype(bf16)
    scale = HEAD_DIM**-0.5
    block = 128
    blocks = rows // block
    pairs = HEADS // 2
    row_clip = lax.broadcasted_iota(jnp.int32, (block, block), 0) // read
    col_clip = lax.broadcasted_iota(jnp.int32, (block, block), 1) // read
    same = row_clip == col_clip
    low_lane = lax.broadcasted_iota(jnp.int32, (block, block), 1) < HEAD_DIM

    def half_of(v, side):
        zero = jnp.zeros_like(v)
        return jnp.where(low_lane, v, zero) if side == 0 else jnp.where(low_lane, zero, v)

    @pl.loop(0, blocks)
    def _(b):
        at = pl.ds(pl.multiple_of(b * block, block), block)
        for pair in range(pairs):
            lanes = slice(pair * block, (pair + 1) * block)
            q, k, v = queries[at, lanes], keys[at, lanes], values[at, lanes]
            parts = []
            for side in range(2):
                s = jnp.where(same, dot(half_of(q, side), k, 1, 1) * scale, MASKED)
                e = jnp.exp(s - jnp.max(s, axis=1, keepdims=True))
                p = e * (1.0 / jnp.sum(e, axis=1, keepdims=True))
                probs[b, 2 * pair + side] = p
                parts.append(dot(p.astype(bf16), v))
            context[at, lanes] = jnp.where(low_lane, parts[0], parts[1]).astype(bf16)

    aft = summary[...] + dot(context[...], mat(3))
    after[...] = aft
    fed = (aft * unit(aft) * gain[2:3]).astype(bf16)
    for j in range(4):
        cols = slice(width * j, width * (j + 1))
        pre = dot(fed, mat(4 + j)) + bias[:, cols]
        square = pre * pre
        t = jnp.tanh(GELU_A * pre * (1.0 + GELU_B * square))
        half = 0.5 + 0.5 * t
        activ[:, cols] = (pre * half).astype(bf16)
        dgelu[:, cols] = half + (0.5 * GELU_A) * pre * (1.0 - t * t) * (
            1.0 + (3.0 * GELU_B) * square
        )
    out = after[...]
    per = groups // 4

    def out_mat(j):
        return wout[per * j : per * (j + 1)].reshape(width, width)

    for j in range(4):
        out = out + dot(activ[:, width * j : width * (j + 1)], out_mat(j))
    ro_ref[...] = out.astype(bf16)

    acc_w[...] = jnp.zeros_like(acc_w)

    @pl.loop(0, clips)
    def _(c):
        at = pl.ds(pl.multiple_of(c * read, read), read)
        ct_copy(c).wait()
        zm[c, 0:read] = ro_ref[at]
        z_m, z_f = zm[c], zf[c]
        g = ctm[c]
        r_m = lax.rsqrt(dot(ones, z_m * z_m, 1, 1) * (1.0 / width) + NORM_EPS)
        r_f = rf_s[c]
        rm_s[c] = r_m
        both = jnp.concatenate([table[0:mem], g], axis=0)
        x_m, x_f = dot(both, z_m, 1, 1), dot(both, z_f, 1, 1)
        live = valid_ref[pl.ds(c, 1), :] > 0
        l_m = x_m[0:mem] * r_m[0:1]
        l_f = jnp.where(live, x_f[0:mem] * r_f[0:1], MASKED)
        top = jnp.maximum(
            jnp.max(l_m, axis=1, keepdims=True), jnp.max(l_f, axis=1, keepdims=True)
        )
        e_m, e_f = jnp.exp(l_m - top), jnp.exp(l_f - top)
        inv = 1.0 / (
            jnp.sum(e_m, axis=1, keepdims=True) + jnp.sum(e_f, axis=1, keepdims=True)
        )
        a_m, a_f = e_m * inv, e_f * inv
        d_m, d_f = x_m[mem:], x_f[mem:]
        mean = jnp.sum(d_m * a_m, axis=1, keepdims=True) + jnp.sum(
            d_f * a_f, axis=1, keepdims=True
        )
        b_m, b_f = a_m * (d_m - mean), a_f * (d_f - mean)
        k_m = (r_m * r_m) * (jnp.sum(b_m * l_m, axis=0, keepdims=True) * (1.0 / width))
        k_f = (r_f * r_f) * (jnp.sum(b_f * l_f, axis=0, keepdims=True) * (1.0 / width))
        cm_s[c], cf_s[c] = k_m, k_f
        arm[c, 0:mem] = a_m.astype(bf16)
        arf[c, 0:mem] = a_f.astype(bf16)
        arm[c, mem : 2 * mem] = (b_m * r_m[0:1]).astype(bf16)
        arf[c, mem : 2 * mem] = (b_f * r_f[0:1]).astype(bf16)
        ar_m = arm[c, 0 : 2 * mem]
        made = dot(ar_m, z_m) + dot(arf[c, 0 : 2 * mem], z_f)
        nm[c] = made[0:mem].astype(bf16)
        pltpu.make_async_copy(nm.at[c], nm_h.at[c], out_sem.at[0, c]).start()
        acc_w[...] += made[mem:]
        back = jnp.concatenate([g, table[0:mem]], axis=0)
        k_t = k_m.T
        gafter[at] = (
            dot(ar_m[:, 0:read], back, 0, 0)
            - z_m[0:read].astype(f32) * k_t[0:read, 0:1]
            + ctr_ref[at].astype(f32)
        )

    aft = after[...]
    unit_aft = unit(aft)
    flat_aft = aft * unit_aft
    fed = (flat_aft * gain[2:3]).astype(bf16)
    g_out = gafter[...].astype(bf16)
    d_fed = jnp.zeros((rows, width), f32)
    for j in range(4):
        cols = slice(width * j, width * (j + 1))
        d_pre = dot(g_out, out_mat(j), 1, 1) * dgelu[:, cols]
        d_low = d_pre.astype(bf16)
        bias[:, cols] = jnp.sum(d_low.astype(f32), axis=0, keepdims=True)
        gpack_ref[per * j : per * (j + 1), 128:192] = (
            dot(activ[:, cols], g_out, 0, 0).astype(bf16).reshape(per, 64, width)
        )
        gpack_ref[:, ROWS * (4 + j) : ROWS * (5 + j)] = (
            dot(fed, d_low, 0, 0).astype(bf16).reshape(groups, ROWS, width)
        )
        d_fed = d_fed + dot(d_low, mat(4 + j), 1, 1)
    d_gain_mlp = jnp.sum(d_fed * flat_aft, axis=0, keepdims=True)
    d_flat = d_fed * gain[2:3]
    g_mid = gafter[...] + unit_aft * (
        d_flat - flat_aft * jnp.mean(d_flat * flat_aft, axis=-1, keepdims=True)
    )
    gafter[...] = g_mid
    g_low = g_mid.astype(bf16)
    gpack_ref[:, 3 * ROWS : 4 * ROWS] = (
        dot(context[...], g_low, 0, 0).astype(bf16).reshape(groups, ROWS, width)
    )
    context[...] = dot(g_low, mat(3), 1, 1).astype(bf16)

    @pl.loop(0, blocks)
    def _(b):
        at = pl.ds(pl.multiple_of(b * block, block), block)
        for pair in range(pairs):
            lanes = slice(pair * block, (pair + 1) * block)
            q, k, v, dc = queries[at, lanes], keys[at, lanes], values[at, lanes], context[at, lanes]
            grads = []
            for side in range(2):
                p = probs[b, 2 * pair + side]
                dp = dot(half_of(dc, side), v, 1, 1)
                ds = (
                    scale * p * (dp - jnp.sum(dp * p, axis=1, keepdims=True))
                ).astype(bf16)
                grads.append(
                    (dot(ds, k), dot(ds, q, 0, 0), dot(p.astype(bf16), dc, 0, 0))
                )
            queries[at, lanes] = jnp.where(low_lane, grads[0][0], grads[1][0]).astype(bf16)
            keys[at, lanes] = jnp.where(low_lane, grads[0][1], grads[1][1]).astype(bf16)
            values[at, lanes] = jnp.where(low_lane, grads[0][2], grads[1][2]).astype(bf16)

    hidden = normed[...]
    d_hid = jnp.zeros((rows, width), f32)
    for m, g in enumerate((queries, keys, values)):
        g_now = g[...]
        gpack_ref[:, ROWS * m : ROWS * (m + 1)] = (
            dot(hidden, g_now, 0, 0).astype(bf16).reshape(groups, ROWS, width)
        )
        d_hid = d_hid + dot(g_now, mat(m), 1, 1)
    summ = summary[...]
    unit_sum = unit(summ)
    flat_sum = summ * unit_sum
    d_gain_attn = jnp.sum(d_hid * flat_sum, axis=0, keepdims=True)
    d_flat = d_hid * gain[1:2]
    gsum[...] = (
        gafter[...]
        + unit_sum * (d_flat - flat_sum * jnp.mean(d_flat * flat_sum, axis=-1, keepdims=True))
    ).astype(bf16)

    acc_r[...] = jnp.zeros_like(acc_r)

    @pl.loop(0, clips)
    def _(c):
        at = pl.ds(pl.multiple_of(c * read, read), read)
        z_m, z_f = zm[c], zf[c]
        g = gsum[at]
        d_m, d_f = dot(g, z_m, 1, 1), dot(g, z_f, 1, 1)
        a_m, a_f, l_m, l_f = aread_m[c], aread_f[c], lread_m[c], lread_f[c]
        r_m, r_f = rm_s[c], rf_s[c]
        mean = jnp.sum(d_m * a_m, axis=1, keepdims=True) + jnp.sum(
            d_f * a_f, axis=1, keepdims=True
        )
        b_m, b_f = a_m * (d_m - mean), a_f * (d_f - mean)
        k_m = cm_s[c] + (r_m * r_m) * (jnp.sum(b_m * l_m, axis=0, keepdims=True) * (1.0 / width))
        k_f = cf_s[c] + (r_f * r_f) * (jnp.sum(b_f * l_f, axis=0, keepdims=True) * (1.0 / width))
        h_m = (b_m * r_m[0:1]).astype(bf16)
        h_f = (b_f * r_f[0:1]).astype(bf16)
        acc_r[...] += dot(h_m, z_m) + dot(h_f, z_f)
        arm[c, 2 * mem + read : 2 * wide] = h_m
        arf[c, 2 * mem + read : 2 * wide] = h_f
        back = jnp.concatenate([ctm[c], table[0:mem], g, table[mem:wide]], axis=0)
        t_m, t_f = k_m.T, k_f.T
        zm[c] = (dot(arm[c], back, 0, 0) - z_m.astype(f32) * t_m[:, 0:1]).astype(bf16)
        zf[c] = (dot(arf[c], back, 0, 0) - z_f.astype(f32) * t_f[:, 0:1]).astype(bf16)
        pltpu.make_async_copy(zm.at[c, pl.ds(read, mem)], gm_h.at[c], out_sem.at[1, c]).start()
        pltpu.make_async_copy(zf.at[c], gf_h.at[c], out_sem.at[2, c]).start()

    zero_rows = jnp.zeros((1, width), f32)
    rest = jnp.concatenate(
        [zero_rows, d_gain_attn, d_gain_mlp, zero_rows, jnp.zeros((12, width), f32)], axis=0
    )
    stacked = jnp.concatenate([acc_w[...], acc_r[...], rest], axis=0)
    gpack_ref[:, SMALL:PACK] = jnp.zeros((groups, ROWS, width), bf16)
    gpack_ref[:, SMALL:PACK, 0:128] = stacked.T.astype(bf16).reshape(groups, ROWS, 128)
    for d in range(groups):
        gpack_ref[d, SMALL : SMALL + 1, 128 : 128 + piece] = bias[
            :, piece * d : piece * (d + 1)
        ].astype(bf16)

    @pl.loop(0, clips)
    def _(c):
        pltpu.make_async_copy(nm.at[c], nm_h.at[c], out_sem.at[0, c]).wait()
        pltpu.make_async_copy(zm.at[c, pl.ds(read, mem)], gm_h.at[c], out_sem.at[1, c]).wait()
        pltpu.make_async_copy(zf.at[c], gf_h.at[c], out_sem.at[2, c]).wait()


def run_step(frames, valid, memory, ct_memory, ct_read, wpack):
    clips, toks, width = frames.shape
    mem, read = memory.shape[1], ct_read.shape[1]
    groups = wpack.shape[0]
    rows, wide = clips * read, mem + read
    vm = pltpu.VMEM
    hbm = pl.BlockSpec(memory_space=pl.ANY)
    inside = pl.BlockSpec(memory_space=pltpu.VMEM)
    made = jax.ShapeDtypeStruct
    outs = pl.pallas_call(
        functools.partial(step_kernel, clips),
        out_shape=(
            made(memory.shape, bf16),
            made((rows, width), bf16),
            made(frames.shape, bf16),
            made(memory.shape, bf16),
            made((groups, PACK, width), bf16),
        ),
        in_specs=[hbm, inside, hbm, hbm, inside, hbm],
        out_specs=(hbm, inside, hbm, hbm, inside),
        scratch_shapes=[
            vm((clips, wide, width), bf16),
            vm((clips, toks, width), bf16),
            vm((clips, mem, width), bf16),
            vm((clips, mem, width), bf16),
            vm((8, groups, ROWS, width), bf16),
            vm((groups, 64, width), bf16),
            vm((groups, ROWS, width), bf16),
            vm((wide, width), bf16),
            vm((8, width), f32),
            vm((1, 4 * width), f32),
            vm((clips, 2 * wide, wide), bf16),
            vm((clips, 2 * wide, toks), bf16),
            vm((clips, read, wide), f32),
            vm((clips, read, toks), f32),
            vm((clips, read, wide), f32),
            vm((clips, read, toks), f32),
            vm((clips, 8, wide), f32),
            vm((clips, 8, toks), f32),
            vm((clips, 8, wide), f32),
            vm((clips, 8, toks), f32),
            vm((rows, width), f32),
            vm((rows, width), bf16),
            vm((rows, width), bf16),
            vm((rows, width), bf16),
            vm((rows // 128, HEADS, 128, 128), f32),
            vm((rows, width), bf16),
            vm((rows, width), f32),
            vm((rows, width), bf16),
            vm((rows, 4 * width), f32),
            vm((rows, 4 * width), bf16),
            vm((rows, width), f32),
            vm((rows, width), bf16),
            vm((mem, width), f32),
            vm((read, width), f32),
            pltpu.SemaphoreType.DMA((3, clips)),
            pltpu.SemaphoreType.DMA((10,)),
            pltpu.SemaphoreType.DMA((3, clips)),
        ],
        compiler_params=pltpu.CompilerParams(vmem_limit_bytes=60 * 1024 * 1024),
        cost_estimate=pl.CostEstimate(
            flops=12 * 10**9, bytes_accessed=36 * 10**6, transcendentals=4 * 10**6
        ),
        name="clip_step",
    )(frames, valid, memory, ct_memory, ct_read.reshape(rows, width), wpack)
    new_memory, read_out, grad_frames, grad_memory, gpack = outs
    return new_memory, read_out.reshape(ct_read.shape), grad_frames, grad_memory, gpack


MESH = pl.DeviceIdType.MESH
X, Y, CORE = 2, 4, 1
CUT = 112


def remote(src, dst, send, recv, device):
    return pltpu.make_async_remote_copy(
        src_ref=src, dst_ref=dst, send_sem=send, recv_sem=recv, device_id=device, device_id_type=MESH
    )


def gather_kernel(attn, w_in, w_out, s_read, s_write, gains, bias, out, x_ref, own_sem, up, down, sx, sy, fx, fy, sc, rz, rx, ry, rdx, rdy, rc):
    dp, p = lax.axis_index("dp"), lax.axis_index("sub")
    last = lax.axis_size("sub") - 1
    count = last + 1

    def flip(mask):
        return (jnp.bitwise_xor(dp, mask), p)

    def unit(mask, s):
        return out.at[jnp.bitwise_xor(dp, mask) * count + s]

    barrier = pltpu.get_barrier_semaphore()
    for mask in (X, Y, CORE):
        pl.semaphore_signal(barrier, inc=1, device_id=flip(mask), device_id_type=MESH)

    @pl.when(p < last)
    def _():
        pl.semaphore_signal(barrier, inc=1, device_id=(dp, p + 1), device_id_type=MESH)

    @pl.when(p > 0)
    def _():
        pl.semaphore_signal(barrier, inc=1, device_id=(dp, p - 1), device_id_type=MESH)

    width = x_ref.shape[1]
    for m in range(4):
        x_ref[ROWS * m : ROWS * (m + 1)] = attn[m].astype(bf16)
        x_ref[64 + ROWS * m : 64 + ROWS * (m + 1)] = w_in[:, width * m : width * (m + 1)].astype(bf16)
    x_ref[128:192] = w_out[...].astype(bf16)
    x_ref[SMALL:PACK] = jnp.zeros((ROWS, width), bf16)
    x_ref[SMALL:PACK, 0:96] = s_write[...].astype(bf16)
    x_ref[SMALL:PACK, 96:112] = s_read[...].astype(bf16)
    x_ref[SMALL:PACK, 112:116] = turn_gains(gains[...]).astype(bf16)
    x_ref[SMALL : SMALL + 1, 128:192] = bias[...].astype(bf16)
    own = pltpu.make_async_copy(x_ref, unit(0, p), own_sem)
    own.start()
    pl.semaphore_wait(barrier, 3 + jnp.where(p < last, 1, 0) + jnp.where(p > 0, 1, 0))

    def chain(step, way, s, src):
        sems = up if way > 0 else down
        return remote(src, unit(0, s), sems.at[step], rz.at[s], (dp, p + way))

    def side(mask, s, src):
        send, recv = (sx, rx) if mask == X else (sy, ry)
        return remote(src, unit(0, s), send.at[s], recv.at[s], flip(mask))

    def halves(mask, s):
        other = Y if mask == X else X
        part = pl.ds(0, CUT) if mask == X else pl.ds(CUT, PACK - CUT)
        send, recv = (fy, rdy) if mask == X else (fx, rdx)
        ref = unit(mask, s).at[part]
        return remote(ref, ref, send.at[s], recv.at[s], flip(other))

    def cross(kind, s, src):
        return remote(src, unit((0, X, Y, X + Y)[kind], s), sc.at[kind, s], rc.at[kind, s], flip(CORE))

    def share(s, src):
        side(X, s, src).start()
        side(Y, s, src).start()
        cross(0, s, src).start()

    @pl.when(p < last)
    def _():
        chain(0, 1, p, x_ref).start()

    @pl.when(p > 0)
    def _():
        chain(0, -1, p, x_ref).start()

    share(p, x_ref)

    def arrived(s):
        for mask, kind in ((X, 1), (Y, 2)):
            recv = rx if mask == X else ry
            got = unit(mask, s)
            remote(got, got, recv.at[s], recv.at[s], flip(mask)).wait_recv()
            halves(mask, s).start()
            cross(kind, s, got).start()

    def arrivals(k):
        if k == 0:
            arrived(p)
            return

        @pl.when(p >= k)
        def _():
            arrived(p - k)

        @pl.when(p + k <= last)
        def _():
            arrived(p + k)

    for k in range(1, count):
        for way in (1, -1):

            @pl.when(p >= k if way > 0 else p + k <= last)
            def _():
                s = p - k * way
                got = unit(0, s)
                remote(got, got, rz.at[s], rz.at[s], (dp, p)).wait_recv()
                if k < last:

                    @pl.when(p < last if way > 0 else p > 0)
                    def _():
                        chain(k, way, s, got).start()

                share(s, got)

        arrivals(k - 1)
    arrivals(count - 1)
    for s in range(count):
        for recv, part in ((rdy, pl.ds(0, CUT)), (rdx, pl.ds(CUT, PACK - CUT))):
            got = unit(X + Y, s).at[part]
            remote(got, got, recv.at[s], recv.at[s], flip(X)).wait_recv()
        cross(3, s, unit(X + Y, s)).start()
    for s in range(count):
        for kind in range(4):
            got = unit((CORE, X + CORE, Y + CORE, X + Y + CORE)[kind], s)
            remote(got, got, rc.at[kind, s], rc.at[kind, s], flip(CORE)).wait_recv()
    own.wait()
    for s in range(count):
        for mask in (X, Y):
            side(mask, s, unit(0, s)).wait_send()
            halves(mask, s).wait_send()
        for kind in range(4):
            cross(kind, s, unit((0, X, Y, X + Y)[kind], s)).wait_send()
    for k in range(last):

        @pl.when((p < last) & (p >= k))
        def _():
            chain(k, 1, p - k, unit(0, p - k)).wait_send()

        @pl.when((p > 0) & (p + k <= last))
        def _():
            chain(k, -1, p + k, unit(0, p + k)).wait_send()


def gather_pack(*weights):
    n_dp, n_sub = lax.axis_size("dp"), lax.axis_size("sub")
    width = weights[0].shape[-1]
    sem = pltpu.SemaphoreType.DMA
    return pl.pallas_call(
        gather_kernel,
        out_shape=jax.ShapeDtypeStruct((n_dp * n_sub, PACK, width), bf16),
        in_specs=[pl.BlockSpec(memory_space=pltpu.VMEM)] * len(weights),
        out_specs=pl.BlockSpec(memory_space=pl.ANY),
        scratch_shapes=[
            pltpu.VMEM((PACK, width), bf16),
            sem,
            *[sem((n_sub,))] * 6,
            sem((4, n_sub)),
            *[sem((n_sub,))] * 5,
            sem((4, n_sub)),
        ],
        compiler_params=pltpu.CompilerParams(collective_id=1, has_side_effects=True),
        name="gather_weights",
    )(*weights)


def reduce_kernel(g_h, attn_mom, w_in_mom, w_out_mom, s_read_mom, s_write_mom, gains, out, buf, gl, rc, ra, rb, rx, ry, rz, acc, lsem, cs, cr, as_, ar, bs, br, xs, xr, ys, yr, zs, zr, pk, gsend, grecv, gown):
    dp, p = lax.axis_index("dp"), lax.axis_index("sub")
    count = lax.axis_size("sub")
    masks = (0, X, Y, X + Y)

    def flip(mask):
        return (jnp.bitwise_xor(dp, mask), p)

    def column(mask):
        return g_h.at[pl.ds(jnp.bitwise_xor(dp, mask) * count, count)]

    local = [pltpu.make_async_copy(column(masks[k]), gl.at[k], lsem.at[k]) for k in range(4)]
    for k in (3, 1, 2, 0):
        local[k].start()
    barrier = pltpu.get_barrier_semaphore()
    for mask in (X, Y, CORE):
        pl.semaphore_signal(barrier, inc=1, device_id=flip(mask), device_id_type=MESH)
    for off in range(1, count):
        pl.semaphore_signal(
            barrier, inc=1, device_id=(dp, lax.rem(p + off, count)), device_id_type=MESH
        )
    pl.semaphore_wait(barrier, 3 + count - 1)
    crossed = [
        remote(column(masks[k] + CORE), rc.at[k], cs.at[k], cr.at[k], flip(CORE)) for k in range(4)
    ]
    for k in (3, 1, 2, 0):
        crossed[k].start()
    order = [lax.rem(p + off, count) for off in (2, 1, 3, 0)]
    first, second = pl.ds(0, CUT), pl.ds(CUT, PACK - CUT)

    def ready(k):
        local[k].wait()
        crossed[k].wait_recv()

    def total(k, s):
        return gl[k, s].astype(f32) + rc[k, s].astype(f32)

    sent = [crossed[k] for k in range(4)]

    def push(copy):
        copy.start()
        sent.append(copy)

    ready(3)
    for s in order:
        gl[3, s] = total(3, s).astype(bf16)
        push(remote(gl.at[3, s, first], ra.at[s], as_.at[s], ar.at[s], flip(X)))
        push(remote(gl.at[3, s, second], rb.at[s], bs.at[s], br.at[s], flip(Y)))
    ready(1)
    ready(2)
    for s in order:
        sum_x, sum_y = total(1, s), total(2, s)
        remote(rb.at[s], rb.at[s], bs.at[s], br.at[s], flip(Y)).wait_recv()
        gl[1, s, 0:CUT] = sum_x[0:CUT].astype(bf16)
        gl[1, s, CUT:PACK] = (sum_x[CUT:PACK] + rb[s].astype(f32)).astype(bf16)
        push(remote(gl.at[1, s], rx.at[s], xs.at[s], xr.at[s], flip(X)))
        remote(ra.at[s], ra.at[s], as_.at[s], ar.at[s], flip(X)).wait_recv()
        gl[2, s, 0:CUT] = (sum_y[0:CUT] + ra[s].astype(f32)).astype(bf16)
        gl[2, s, CUT:PACK] = sum_y[CUT:PACK].astype(bf16)
        push(remote(gl.at[2, s], ry.at[s], ys.at[s], yr.at[s], flip(Y)))
    ready(0)
    for i, s in enumerate(order):
        mine = total(0, s)
        remote(rx.at[s], rx.at[s], xs.at[s], xr.at[s], flip(X)).wait_recv()
        remote(ry.at[s], ry.at[s], ys.at[s], yr.at[s], flip(Y)).wait_recv()
        mine = mine + rx[s].astype(f32) + ry[s].astype(f32)
        if i < count - 1:
            gl[0, s] = mine.astype(bf16)
            push(remote(gl.at[0, s], rz.at[i], zs.at[i], zr.at[i], (dp, s)))
        else:
            acc[...] = mine
    for i in range(count - 1):
        remote(rz.at[i], rz.at[i], zs.at[i], zr.at[i], (dp, p)).wait_recv()
        acc[...] += rz[i].astype(f32)
    out[...] = acc[...]
    send_momentum(
        acc, attn_mom, w_in_mom, w_out_mom, s_read_mom, s_write_mom, gains, pk, buf, gsend, grecv, gown
    )
    for copy in sent:
        copy.wait_send()


def reduce_pack(gpack, *state):
    groups, rows, width = gpack.shape
    n = lax.axis_size("sub")
    sem, vm = pltpu.SemaphoreType.DMA, pltpu.VMEM
    anywhere, inside = pl.BlockSpec(memory_space=pl.ANY), pl.BlockSpec(memory_space=pltpu.VMEM)
    return pl.pallas_call(
        reduce_kernel,
        out_shape=(
            jax.ShapeDtypeStruct((rows, width), f32),
            jax.ShapeDtypeStruct((groups, 64, width), bf16),
        ),
        in_specs=[anywhere] + [inside] * len(state),
        out_specs=(inside, anywhere),
        scratch_shapes=[
            vm((4, n, rows, width), bf16),
            vm((4, n, rows, width), bf16),
            vm((n, CUT, width), bf16),
            vm((n, rows - CUT, width), bf16),
            vm((n, rows, width), bf16),
            vm((n, rows, width), bf16),
            vm((n - 1, rows, width), bf16),
            vm((rows, width), f32),
            sem((4,)), sem((4,)), sem((4,)),
            *[sem((n,))] * 10,
            vm((rows, width), bf16),
            sem((len(OWNERS),)),
            sem((groups,)),
            sem,
        ],
        compiler_params=pltpu.CompilerParams(
            collective_id=2, has_side_effects=True, vmem_limit_bytes=60 * 1024 * 1024
        ),
        name="reduce_grads",
    )(gpack, *state)


OWNERS = ((2, 0), (4, 3), (2, 3), (4, 0), (0, 1), (6, 2), (0, 3))
PIECES = ((0, 16), (16, 16), (32, 16), (48, 16), (64, 64), (128, 64), (192, 16))


def is_owner(m):
    return (lax.axis_index("dp") == OWNERS[m][0]) & (lax.axis_index("sub") == OWNERS[m][1])


def turn_gains(g):
    eye = (
        lax.broadcasted_iota(jnp.int32, (4, 4), 0) == lax.broadcasted_iota(jnp.int32, (4, 4), 1)
    ).astype(bf16)
    return lax.dot_general(g.astype(bf16), eye, (((0,), (0,)), ((), ())), preferred_element_type=f32)


def small_grads(red, gains_t):
    return (
        red[SMALL:PACK, 0:96] * gains_t[:, 3:4],
        red[SMALL:PACK, 96:112] * gains_t[:, 0:1],
    )


def send_momentum(acc, attn_mom, w_in_mom, w_out_mom, s_read_mom, s_write_mom, gains, pk, buf, gsend, grecv, gown):
    width = acc.shape[1]
    count = lax.axis_size("sub")
    me = lax.axis_index("dp") * count + lax.axis_index("sub")
    for m in range(4):
        at = slice(ROWS * m, ROWS * (m + 1))
        pk[at] = (0.5 * attn_mom[m] + acc[at]).astype(bf16)
        at = slice(64 + ROWS * m, 64 + ROWS * (m + 1))
        pk[at] = (0.5 * w_in_mom[:, width * m : width * (m + 1)] + acc[at]).astype(bf16)
    pk[128:192] = (0.5 * w_out_mom[...] + acc[128:192]).astype(bf16)
    g_write, g_read = small_grads(acc, turn_gains(gains[...]))
    pk[SMALL:PACK] = jnp.zeros((ROWS, width), bf16)
    pk[SMALL:PACK, 0:96] = (0.5 * s_write_mom[...] + g_write).astype(bf16)
    pk[SMALL:PACK, 96:112] = (0.5 * s_read_mom[...] + g_read).astype(bf16)

    def piece(m):
        start, size = PIECES[m]
        return pk.at[pl.ds(start, size)], buf.at[me, pl.ds(0, size)]

    def away(m):
        src, dst = piece(m)
        return remote(src, dst, gsend.at[m], grecv.at[me], OWNERS[m])

    def home(m):
        src, dst = piece(m)
        return pltpu.make_async_copy(src, dst, gown)

    many = range(len(OWNERS))
    for m in (4, 5, 0, 1, 2, 3, 6):

        @pl.when(jnp.logical_not(is_owner(m)))
        def _():
            away(m).start()

    for m in many:

        @pl.when(is_owner(m))
        def _():
            home(m).start()

            @pl.loop(0, buf.shape[0])
            def _(d):
                @pl.when(d != me)
                def _():
                    got = buf.at[d, pl.ds(0, PIECES[m][1])]
                    remote(got, got, grecv.at[d], grecv.at[d], OWNERS[m]).wait_recv()

            home(m).wait()

        @pl.when(jnp.logical_not(is_owner(m)))
        def _():
            away(m).wait_send()


def iterate(x, low):
    blocks = x.shape[0]
    total = jnp.zeros((1, 1), f32)
    for j in range(blocks):
        total = total + jnp.sum(x[j] * x[j], keepdims=True)
    scale = 1.0 / (jnp.sqrt(total) + 1e-07)
    for j in range(blocks):
        x[j] = x[j] * scale
        low[j] = x[j].astype(bf16)

    @pl.loop(0, 5)
    def _(_):
        q = dot(low[0], low[0], 1, 1)
        for j in range(1, blocks):
            q = q + dot(low[j], low[j], 1, 1)
        q_low = q.astype(bf16)
        mixed = (NS[1] * q + NS[2] * dot(q_low, q_low)).astype(bf16)
        for j in range(blocks):
            new = NS[0] * x[j] + dot(mixed, low[j])
            x[j] = new
            low[j] = new.astype(bf16)


def exact_dot(a, b, ca=1, cb=0):
    return lax.dot_general(a, b, (((ca,), (cb,)), ((), ())), preferred_element_type=f32, precision=highest)


def iterate_small(x, same):
    norm = jnp.sum(x * x, axis=1, keepdims=True)
    total = jnp.sum(jnp.where(same, norm.T, 0.0), axis=1, keepdims=True)
    x = x * (1.0 / (jnp.sqrt(total) + 1e-07))
    for _ in range(5):
        q = jnp.where(same, exact_dot(x, x, 1, 1), 0.0)
        mixed = NS[1] * q + NS[2] * exact_dot(q, q)
        x = NS[0] * x + exact_dot(mixed, x)
    return x


def muon_kernel(
    red, buf, attn_mom, w_in_mom, w_out_mom, s_read_mom, s_write_mom, s_read, s_write,
    gains, gains_first, gains_second, bias, bias_first, bias_second,
    xo, g_attn, g_in, g_out, g_read, g_write, g_gains, g_bias,
    n_gains, n_bias, m_attn, m_in, m_out, m_read, m_write,
    n_gains_first, n_gains_second, n_bias_first, n_bias_second,
    x, low,
):
    width = red.shape[1]
    groups = buf.shape[0]
    for m in range(4):
        lanes = slice(width * m, width * (m + 1))
        g = red[ROWS * m : ROWS * (m + 1)]
        g_attn[m] = g
        m_attn[m] = 0.5 * attn_mom[m] + g
        g = red[64 + ROWS * m : 64 + ROWS * (m + 1)]
        g_in[:, lanes] = g
        m_in[:, lanes] = 0.5 * w_in_mom[:, lanes] + g
    g = red[128:192]
    g_out[...] = g
    m_out[...] = 0.5 * w_out_mom[...] + g
    gains_t = turn_gains(gains[...])
    made_write, made_read = small_grads(red, gains_t)
    g_write[...] = made_write
    g_read[...] = made_read
    m_write[...] = 0.5 * s_write_mom[...] + made_write
    m_read[...] = 0.5 * s_read_mom[...] + made_read
    low_write = s_write[...].astype(bf16).astype(f32)
    low_read = s_read[...].astype(bf16).astype(f32)
    to_read = jnp.sum(low_read * red[SMALL:PACK, 96:112], axis=1, keepdims=True)
    to_write = jnp.sum(low_write * red[SMALL:PACK, 0:96], axis=1, keepdims=True)
    column = lax.broadcasted_iota(jnp.int32, (ROWS, 128), 1)
    wide = jnp.where(
        column == 112, to_read, jnp.where(column == 115, to_write, red[SMALL:PACK, 0:128])
    )
    grad_gains = wide.T[112:116]
    g_gains[...] = grad_gains
    n_gains[...], n_gains_first[...], n_gains_second[...] = adam_step(
        gains[...], gains_first[...], gains_second[...], grad_gains
    )
    grad_bias = red[SMALL : SMALL + 1, 128:192]
    g_bias[...] = grad_bias
    n_bias[...], n_bias_first[...], n_bias_second[...] = adam_step(
        bias[...], bias_first[...], bias_second[...], grad_bias
    )

    @pl.when(is_owner(0) | is_owner(1) | is_owner(2) | is_owner(3))
    def _():
        x[0] = buf[:, 0:ROWS].reshape(width, width).astype(f32)
        iterate(x.at[0:1], low.at[0:1])
        xo[:, 0:ROWS] = low[0].reshape(groups, ROWS, width)

    @pl.when(is_owner(4))
    def _():
        for j in range(4):
            x[j] = buf[:, ROWS * j : ROWS * (j + 1)].reshape(width, width).astype(f32)
        iterate(x, low)
        for j in range(4):
            xo[:, ROWS * j : ROWS * (j + 1)] = low[j].reshape(groups, ROWS, width)

    @pl.when(is_owner(5))
    def _():
        per = groups // 4
        for j in range(4):
            x[j] = buf[per * j : per * (j + 1)].reshape(width, width).astype(f32).T
        iterate(x, low)
        for j in range(4):
            xo[per * j : per * (j + 1)] = x[j].T.astype(bf16).reshape(per, 64, width)

    @pl.when(is_owner(6))
    def _():
        table = buf[:, 0:ROWS, 0:128].reshape(width, 128).astype(f32).T
        row = lax.broadcasted_iota(jnp.int32, (128, 128), 0)
        col = lax.broadcasted_iota(jnp.int32, (128, 128), 1)
        same = ((row < 96) & (col < 96)) | ((row >= 96) & (col >= 96))
        made = iterate_small(table, same)
        xo[:, 0:ROWS, 0:128] = made.T.astype(bf16).reshape(groups, ROWS, 128)


def spread_kernel(xo, xrec, ssem, rsem, osem):
    count = lax.axis_size("sub")
    me = lax.axis_index("dp") * count + lax.axis_index("sub")
    groups = xo.shape[0]
    many = range(len(OWNERS))
    barrier = pltpu.get_barrier_semaphore()
    for m in many:

        @pl.when(jnp.logical_not(is_owner(m)))
        def _():
            pl.semaphore_signal(barrier, inc=1, device_id=OWNERS[m], device_id_type=MESH)

    for m in many:
        start, size = PIECES[m]

        def target(m=m, start=start, size=size):
            return xrec.at[pl.ds(start, size)]

        def away(d, m=m, size=size):
            return remote(
                xo.at[d, pl.ds(0, size)], target(), ssem.at[d], rsem.at[m], (d // count, lax.rem(d, count))
            )

        @pl.when(is_owner(m))
        def _():
            pl.semaphore_wait(barrier, groups - 1)
            home = pltpu.make_async_copy(xo.at[me, pl.ds(0, size)], target(), osem)
            home.start()

            @pl.loop(0, groups)
            def _(d):
                @pl.when(d != me)
                def _():
                    away(d).start()

            home.wait()

            @pl.loop(0, groups)
            def _(d):
                @pl.when(d != me)
                def _():
                    away(d).wait_send()

    for m in many:
        start, size = PIECES[m]

        @pl.when(jnp.logical_not(is_owner(m)))
        def _():
            got = xrec.at[pl.ds(start, size)]
            remote(got, got, rsem.at[m], rsem.at[m], OWNERS[m]).wait_recv()


def finish_kernel(xrec, attn, w_in, w_out, s_read, s_write, n_attn, n_in, n_out, n_read, n_write):
    width = xrec.shape[1]
    for m in range(4):
        lanes = slice(width * m, width * (m + 1))
        n_attn[m] = attn[m] - xrec[ROWS * m : ROWS * (m + 1)].astype(f32)
        n_in[:, lanes] = w_in[:, lanes] - xrec[64 + ROWS * m : 64 + ROWS * (m + 1)].astype(f32)
    n_out[...] = w_out[...] - 2.0 * xrec[128:192].astype(f32)
    small = xrec[SMALL:PACK, 0:128].astype(f32)
    n_write[...] = s_write[...] - math.sqrt(512 / 96) * small[:, 0:96]
    n_read[...] = s_read[...] - math.sqrt(512 / 16) * small[:, 96:112]


highest = lax.Precision.HIGHEST
NS = (3.4445, -4.775, 2.0315)


def canonical(attn, w_in, w_out, s_read, s_write, gains, bias):
    width = attn.shape[2]
    groups = attn.shape[1] // ROWS
    a = attn.astype(bf16).reshape(4, groups, ROWS, width).transpose(1, 0, 2, 3)
    i = w_in.astype(bf16).reshape(groups, ROWS, 4, width).transpose(0, 2, 1, 3)
    o = w_out.astype(bf16).reshape(groups, 64, width)
    s = jnp.concatenate([s_write, s_read, gains.T], axis=1).astype(bf16)
    s = jnp.pad(s, ((0, 0), (0, 128 - s.shape[1]))).reshape(groups, ROWS, 128)
    b = bias.astype(bf16).reshape(groups, 1, 64)
    b = jnp.pad(b, ((0, 0), (0, ROWS - 1), (0, width - 128 - 64)))
    return jnp.concatenate(
        [
            a.reshape(groups, 64, width),
            i.reshape(groups, 64, width),
            o,
            jnp.concatenate([s, b], axis=2),
        ],
        axis=1,
    )


def natural(pack, mem, read):
    groups, _, width = pack.shape
    a = pack[:, 0:64].reshape(groups, 4, ROWS, width).transpose(1, 0, 2, 3)
    i = pack[:, 64:128].reshape(groups, 4, ROWS, width).transpose(0, 2, 1, 3)
    s = pack[:, SMALL:PACK, 0:128].reshape(groups * ROWS, 128)
    return (
        a.reshape(4, groups * ROWS, width),
        i.reshape(groups * ROWS, 4 * width),
        pack[:, 128:192].reshape(groups * 64, width),
        s[:, 0:mem],
        s[:, mem : mem + read],
        s[:, mem + read + 1 : mem + read + 3],
        pack[:, SMALL, 128:192].reshape(groups * 64),
    )


def adam_step(weight, first, second, grad):
    first_new = 0.5 * first + 0.5 * grad
    second_new = 0.5 * second + 0.5 * grad * grad
    part = 1.0 - 0.5**10
    moved = 0.25 * (first_new / part) / (jnp.sqrt(second_new / part) + 1e-08)
    return weight - moved, first_new, second_new


def orthogonalize(matrix):
    tall = matrix.shape[0] > matrix.shape[1]
    x = matrix.T if tall else matrix
    x = x / (jnp.sqrt(jnp.sum(x * x)) + 1e-07)
    for _ in range(5):
        q = jnp.dot(x, x.T, precision=highest)
        mixed = NS[1] * q + NS[2] * jnp.dot(q, q, precision=highest)
        x = NS[0] * x + jnp.dot(mixed, x, precision=highest)
    return x.T if tall else x


def any_slice(
    frames, valid, memory, ct_memory, ct_read,
    attn, w_in, w_out, s_read, s_write, gains, bias,
    attn_mom, w_in_mom, w_out_mom, s_read_mom, s_write_mom,
    gains_first, gains_second, bias_first, bias_second,
):
    axes = ("dp", "sub")
    mem, read = memory.shape[1], ct_read.shape[1]

    def gather(v, axis):
        return lax.all_gather(v.astype(bf16), axes, axis=axis, tiled=True)

    def scatter(v, axis):
        return lax.psum_scatter(v, axes, scatter_dimension=axis, tiled=True)

    wpack = canonical(
        gather(attn, 1), gather(w_in, 0), gather(w_out, 0), gather(s_read, 0),
        gather(s_write, 0), gather(gains, 1), gather(bias, 0),
    )
    new_memory, read_out, grad_frames, grad_memory, gpack = run_step(
        frames, valid, memory, ct_memory, ct_read, wpack
    )
    sums = natural(gpack.astype(f32), mem, read)
    g_attn, g_in, g_out, sum_w, sum_r, g_two, g_bias = (
        scatter(v, axis) for v, axis in zip(sums, (1, 0, 0, 0, 0, 0, 0))
    )
    low_gain = gains.astype(bf16).astype(f32)
    low_w, low_r = s_write.astype(bf16).astype(f32), s_read.astype(bf16).astype(f32)
    g_s_write = low_gain[3][:, None] * sum_w
    g_s_read = low_gain[0][:, None] * sum_r
    g_gains = jnp.stack(
        [jnp.sum(low_r * sum_r, axis=1), g_two[:, 0], g_two[:, 1], jnp.sum(low_w * sum_w, axis=1)]
    )
    moms = (
        0.5 * attn_mom + g_attn,
        0.5 * w_in_mom + g_in,
        0.5 * w_out_mom + g_out,
        0.5 * s_read_mom + g_s_read,
        0.5 * s_write_mom + g_s_write,
    )
    whole = [gather(v, axis).astype(f32) for v, axis in zip(moms, (1, 0, 0, 0, 0))]
    matrices = [whole[0][m] for m in range(4)] + whole[1:]
    rank, count = lax.axis_index(axes), lax.axis_size(axes)
    owned = [
        lax.cond(rank == m * count // 8, orthogonalize, jnp.zeros_like, matrix)
        for m, matrix in enumerate(matrices)
    ]
    ortho = (
        scatter(jnp.stack(owned[:4]), 1), *(scatter(v, 0) for v in owned[4:])
    )
    stepped = []
    for weight, part, full in zip((attn, w_in, w_out, s_read, s_write), ortho, whole):
        ratio = max(1.0, full.shape[-2] / full.shape[-1]) ** 0.5
        stepped.append(weight - ratio * part)
    n_gains = adam_step(gains, gains_first, gains_second, g_gains)
    n_bias = adam_step(bias, bias_first, bias_second, g_bias)
    return (
        new_memory, read_out, grad_frames, grad_memory,
        g_attn, g_in, g_out, g_s_read, g_s_write, g_gains, g_bias,
        *stepped, n_gains[0], n_bias[0], *moms, n_gains[1], n_gains[2], n_bias[1], n_bias[2],
    )


def this_slice(
    frames, valid, memory, ct_memory, ct_read,
    attn, w_in, w_out, s_read, s_write, gains, bias,
    attn_mom, w_in_mom, w_out_mom, s_read_mom, s_write_mom,
    gains_first, gains_second, bias_first, bias_second,
):
    inside, anywhere = pl.BlockSpec(memory_space=pltpu.VMEM), pl.BlockSpec(memory_space=pl.ANY)

    def like(*arrays):
        return tuple(jax.ShapeDtypeStruct(a.shape, f32) for a in arrays)

    def row(v):
        return v.reshape(1, -1)

    wpack = gather_pack(attn, w_in, w_out, s_read, s_write, gains, row(bias))
    new_memory, read_out, grad_frames, grad_memory, gpack = run_step(
        frames, valid, memory, ct_memory, ct_read, wpack
    )
    moms = (attn_mom, w_in_mom, w_out_mom, s_read_mom, s_write_mom)
    weights = (attn, w_in, w_out, s_read, s_write)
    red, buf = reduce_pack(gpack, *moms, gains)
    biases = (row(bias), row(bias_first), row(bias_second))
    groups, width = buf.shape[0], buf.shape[2]
    made = pl.pallas_call(
        muon_kernel,
        out_shape=(
            jax.ShapeDtypeStruct(buf.shape, bf16),
            *like(*weights, gains, biases[0]),
            *like(gains, biases[0]),
            *like(*moms, gains, gains, biases[0], biases[0]),
        ),
        in_specs=[inside] * 15,
        out_specs=(inside,) * 19 ,
        scratch_shapes=[pltpu.VMEM((4, width, width), f32), pltpu.VMEM((4, width, width), bf16)],
        compiler_params=pltpu.CompilerParams(vmem_limit_bytes=60 * 1024 * 1024),
        name="muon",
    )(red, buf, *moms, s_read, s_write, gains, gains_first, gains_second, *biases)
    xo, grads, (n_gains, n_bias), new_moms, adams = made[0], made[1:8], made[8:10], made[10:15], made[15:]
    sem = pltpu.SemaphoreType.DMA
    xrec = pl.pallas_call(
        spread_kernel,
        out_shape=jax.ShapeDtypeStruct((PACK, width), bf16),
        in_specs=[anywhere],
        out_specs=anywhere,
        scratch_shapes=[sem((groups,)), sem((len(OWNERS),)), sem],
        compiler_params=pltpu.CompilerParams(collective_id=3, has_side_effects=True),
        name="spread_ortho",
    )(xo)
    stepped = pl.pallas_call(
        finish_kernel,
        out_shape=like(*weights),
        in_specs=[inside] * 6,
        out_specs=(inside,) * 5,
        name="finish",
    )(xrec, *weights)
    flat = bias.shape
    return (
        new_memory, read_out, grad_frames, grad_memory,
        *grads[:6], grads[6].reshape(flat),
        *stepped, n_gains, n_bias.reshape(flat), *new_moms,
        adams[0], adams[1], adams[2].reshape(flat), adams[3].reshape(flat),
    )


def solution(mesh):
    both = ("dp", "sub")
    rows3, rows2, rows1 = P(both, None, None), P(both, None), P(both)
    mid, last = P(None, both, None), P(None, both)
    weights = (mid, rows2, rows2, rows2, rows2)
    here = (mesh.shape["dp"], mesh.shape["sub"]) == (8, 4)
    return jax.shard_map(
        this_slice if here else any_slice,
        mesh=mesh,
        in_specs=(
            rows3, rows2, rows3, rows3, rows3, *weights, last, rows1, *weights, last, last, rows1, rows1,
        ),
        out_specs=(
            rows3, rows3, rows3, rows3, *weights, last, rows1, *weights, last, rows1, *weights,
            last, last, rows1, rows1,
        ),
        check_vma=False,
    )
```

```python
import functools
import math

import jax
import jax.numpy as jnp
from jax import lax
from jax.experimental import pallas as pl
from jax.experimental.pallas import tpu as pltpu
from jax.sharding import PartitionSpec as P

f32 = jnp.float32
bf16 = jnp.bfloat16

HEADS = 8
HEAD_DIM = 64
NORM_EPS = 1e-06
MASKED = -1000000000.0
GELU_A = math.sqrt(2.0 / math.pi)
GELU_B = 0.044715

ROWS = 16
PACK = 208
SMALL = 192


def dot(a, b, ca=1, cb=0):
    return lax.dot_general(a, b, (((ca,), (cb,)), ((), ())), preferred_element_type=f32)


def step_kernel(
    gather,
    clips,
    frames_h,
    valid_ref,
    memory_h,
    ctm_h,
    ctr_ref,
    wpack_h,
    nm_h,
    ro_ref,
    gf_h,
    gm_h,
    gpack_ref,
    zm,
    zf,
    ctm,
    nm,
    wmat,
    wout,
    small,
    table,
    gain,
    bias,
    arm,
    arf,
    aread_m,
    aread_f,
    lread_m,
    lread_f,
    rm_s,
    rf_s,
    cm_s,
    cf_s,
    summary,
    queries,
    keys,
    values,
    probs,
    context,
    after,
    normed,
    dgelu,
    activ,
    gafter,
    gsum,
    acc_w,
    acc_r,
    in_sem,
    w_sem,
    out_sem,
):
    mem, read = memory_h.shape[1], ROWS
    toks = frames_h.shape[1]
    rows = clips * read
    groups = wpack_h.shape[0]
    width = zm.shape[2]
    wide = mem + read

    def in_copies(c):
        return (
            pltpu.make_async_copy(memory_h.at[c], zm.at[c, pl.ds(read, mem)], in_sem.at[0, c]),
            pltpu.make_async_copy(frames_h.at[c], zf.at[c], in_sem.at[1, c]),
        )

    def ct_copy(c):
        return pltpu.make_async_copy(ctm_h.at[c], ctm.at[c], in_sem.at[2, c])

    small_copy = pltpu.make_async_copy(
        wpack_h.at[:, pl.ds(SMALL, ROWS)], small, w_sem.at[9]
    )
    w_copies = [
        pltpu.make_async_copy(
            wpack_h.at[:, pl.ds(ROWS * m, ROWS)], wmat.at[m], w_sem.at[m]
        )
        for m in range(8)
    ] + [pltpu.make_async_copy(wpack_h.at[:, pl.ds(128, 64)], wout, w_sem.at[8])]

    @pl.loop(0, clips)
    def _(c):
        for copy in in_copies(c):
            copy.start()
        ct_copy(c).start()

    gather()
    small_copy.start()
    for copy in w_copies:
        copy.start()

    small_copy.wait()
    flat = small[:, :, 0:128].reshape(groups * ROWS, 128).astype(f32)
    turned = flat.T
    gain[...] = turned[112:120]
    table[0:mem] = (turned[0:mem] * turned[115:116]).astype(bf16)
    table[mem:wide] = (turned[mem:wide] * turned[112:113]).astype(bf16)
    piece = bias.shape[1] // groups
    for d in range(groups):
        bias[:, piece * d : piece * (d + 1)] = small[d, 0:1, 128 : 128 + piece].astype(f32)

    ones = jnp.ones((8, width), bf16)
    memory_lane = lax.broadcasted_iota(jnp.int32, (1, wide), 1) >= read

    @pl.loop(0, clips)
    def _(c):
        zm[c, 0:read] = jnp.zeros((read, width), bf16)
        for copy in in_copies(c):
            copy.wait()
        z_m, z_f = zm[c], zf[c]
        r_m = lax.rsqrt(dot(ones, z_m * z_m, 1, 1) * (1.0 / width) + NORM_EPS)
        r_f = lax.rsqrt(dot(ones, z_f * z_f, 1, 1) * (1.0 / width) + NORM_EPS)
        rm_s[c], rf_s[c] = r_m, r_f
        tab = table[mem:wide]
        live = valid_ref[pl.ds(c, 1), :] > 0
        l_m = jnp.where(memory_lane, dot(tab, z_m, 1, 1) * r_m[0:1], MASKED)
        l_f = jnp.where(live, dot(tab, z_f, 1, 1) * r_f[0:1], MASKED)
        top = jnp.maximum(
            jnp.max(l_m, axis=1, keepdims=True), jnp.max(l_f, axis=1, keepdims=True)
        )
        e_m, e_f = jnp.exp(l_m - top), jnp.exp(l_f - top)
        inv = 1.0 / (
            jnp.sum(e_m, axis=1, keepdims=True) + jnp.sum(e_f, axis=1, keepdims=True)
        )
        a_m, a_f = e_m * inv, e_f * inv
        lread_m[c], lread_f[c] = l_m, l_f
        aread_m[c], aread_f[c] = a_m, a_f
        h_m, h_f = a_m.astype(bf16), a_f.astype(bf16)
        arm[c, 2 * mem : 2 * mem + read] = h_m
        arf[c, 2 * mem : 2 * mem + read] = h_f
        summary[pl.ds(c * read, read)] = dot(h_m, z_m) + dot(h_f, z_f)

    for copy in w_copies:
        copy.wait()

    def mat(m):
        return wmat[m].reshape(groups * ROWS, width)

    def unit(v):
        return lax.rsqrt(jnp.mean(v * v, axis=-1, keepdims=True) + NORM_EPS)

    summ = summary[...]
    hidden = (summ * unit(summ) * gain[1:2]).astype(bf16)
    normed[...] = hidden
    queries[...] = dot(hidden, mat(0)).astype(bf16)
    keys[...] = dot(hidden, mat(1)).astype(bf16)
    values[...] = dot(hidden, mat(2)).astype(bf16)
    scale = HEAD_DIM**-0.5
    block = 128
    blocks = rows // block
    pairs = HEADS // 2
    row_clip = lax.broadcasted_iota(jnp.int32, (block, block), 0) // read
    col_clip = lax.broadcasted_iota(jnp.int32, (block, block), 1) // read
    same = row_clip == col_clip
    low_lane = lax.broadcasted_iota(jnp.int32, (block, block), 1) < HEAD_DIM

    def half_of(v, side):
        zero = jnp.zeros_like(v)
        return jnp.where(low_lane, v, zero) if side == 0 else jnp.where(low_lane, zero, v)

    @pl.loop(0, blocks)
    def _(b):
        at = pl.ds(pl.multiple_of(b * block, block), block)
        for pair in range(pairs):
            lanes = slice(pair * block, (pair + 1) * block)
            q, k, v = queries[at, lanes], keys[at, lanes], values[at, lanes]
            parts = []
            for side in range(2):
                s = jnp.where(same, dot(half_of(q, side), k, 1, 1) * scale, MASKED)
                e = jnp.exp(s - jnp.max(s, axis=1, keepdims=True))
                p = e * (1.0 / jnp.sum(e, axis=1, keepdims=True))
                probs[b, 2 * pair + side] = p
                parts.append(dot(p.astype(bf16), v))
            context[at, lanes] = jnp.where(low_lane, parts[0], parts[1]).astype(bf16)

    aft = summary[...] + dot(context[...], mat(3))
    after[...] = aft
    fed = (aft * unit(aft) * gain[2:3]).astype(bf16)
    for j in range(4):
        cols = slice(width * j, width * (j + 1))
        pre = dot(fed, mat(4 + j)) + bias[:, cols]
        square = pre * pre
        t = jnp.tanh(GELU_A * pre * (1.0 + GELU_B * square))
        half = 0.5 + 0.5 * t
        activ[:, cols] = (pre * half).astype(bf16)
        dgelu[:, cols] = half + (0.5 * GELU_A) * pre * (1.0 - t * t) * (
            1.0 + (3.0 * GELU_B) * square
        )
    out = after[...]
    per = groups // 4

    def out_mat(j):
        return wout[per * j : per * (j + 1)].reshape(width, width)

    for j in range(4):
        out = out + dot(activ[:, width * j : width * (j + 1)], out_mat(j))
    ro_ref[...] = out.astype(bf16)

    acc_w[...] = jnp.zeros_like(acc_w)

    @pl.loop(0, clips)
    def _(c):
        at = pl.ds(pl.multiple_of(c * read, read), read)
        ct_copy(c).wait()
        zm[c, 0:read] = ro_ref[at]
        z_m, z_f = zm[c], zf[c]
        g = ctm[c]
        r_m = lax.rsqrt(dot(ones, z_m * z_m, 1, 1) * (1.0 / width) + NORM_EPS)
        r_f = rf_s[c]
        rm_s[c] = r_m
        both = jnp.concatenate([table[0:mem], g], axis=0)
        x_m, x_f = dot(both, z_m, 1, 1), dot(both, z_f, 1, 1)
        live = valid_ref[pl.ds(c, 1), :] > 0
        l_m = x_m[0:mem] * r_m[0:1]
        l_f = jnp.where(live, x_f[0:mem] * r_f[0:1], MASKED)
        top = jnp.maximum(
            jnp.max(l_m, axis=1, keepdims=True), jnp.max(l_f, axis=1, keepdims=True)
        )
        e_m, e_f = jnp.exp(l_m - top), jnp.exp(l_f - top)
        inv = 1.0 / (
            jnp.sum(e_m, axis=1, keepdims=True) + jnp.sum(e_f, axis=1, keepdims=True)
        )
        a_m, a_f = e_m * inv, e_f * inv
        d_m, d_f = x_m[mem:], x_f[mem:]
        mean = jnp.sum(d_m * a_m, axis=1, keepdims=True) + jnp.sum(
            d_f * a_f, axis=1, keepdims=True
        )
        b_m, b_f = a_m * (d_m - mean), a_f * (d_f - mean)
        k_m = (r_m * r_m) * (jnp.sum(b_m * l_m, axis=0, keepdims=True) * (1.0 / width))
        k_f = (r_f * r_f) * (jnp.sum(b_f * l_f, axis=0, keepdims=True) * (1.0 / width))
        cm_s[c], cf_s[c] = k_m, k_f
        arm[c, 0:mem] = a_m.astype(bf16)
        arf[c, 0:mem] = a_f.astype(bf16)
        arm[c, mem : 2 * mem] = (b_m * r_m[0:1]).astype(bf16)
        arf[c, mem : 2 * mem] = (b_f * r_f[0:1]).astype(bf16)
        ar_m = arm[c, 0 : 2 * mem]
        made = dot(ar_m, z_m) + dot(arf[c, 0 : 2 * mem], z_f)
        nm[c] = made[0:mem].astype(bf16)
        pltpu.make_async_copy(nm.at[c], nm_h.at[c], out_sem.at[0, c]).start()
        acc_w[...] += made[mem:]
        back = jnp.concatenate([g, table[0:mem]], axis=0)
        k_t = k_m.T
        gafter[at] = (
            dot(ar_m[:, 0:read], back, 0, 0)
            - z_m[0:read].astype(f32) * k_t[0:read, 0:1]
            + ctr_ref[at].astype(f32)
        )

    aft = after[...]
    unit_aft = unit(aft)
    flat_aft = aft * unit_aft
    fed = (flat_aft * gain[2:3]).astype(bf16)
    g_out = gafter[...].astype(bf16)
    d_fed = jnp.zeros((rows, width), f32)
    for j in range(4):
        cols = slice(width * j, width * (j + 1))
        d_pre = dot(g_out, out_mat(j), 1, 1) * dgelu[:, cols]
        d_low = d_pre.astype(bf16)
        bias[:, cols] = jnp.sum(d_low.astype(f32), axis=0, keepdims=True)
        gpack_ref[per * j : per * (j + 1), 128:192] = (
            dot(activ[:, cols], g_out, 0, 0).astype(bf16).reshape(per, 64, width)
        )
        gpack_ref[:, ROWS * (4 + j) : ROWS * (5 + j)] = (
            dot(fed, d_low, 0, 0).astype(bf16).reshape(groups, ROWS, width)
        )
        d_fed = d_fed + dot(d_low, mat(4 + j), 1, 1)
    d_gain_mlp = jnp.sum(d_fed * flat_aft, axis=0, keepdims=True)
    d_flat = d_fed * gain[2:3]
    g_mid = gafter[...] + unit_aft * (
        d_flat - flat_aft * jnp.mean(d_flat * flat_aft, axis=-1, keepdims=True)
    )
    gafter[...] = g_mid
    g_low = g_mid.astype(bf16)
    gpack_ref[:, 3 * ROWS : 4 * ROWS] = (
        dot(context[...], g_low, 0, 0).astype(bf16).reshape(groups, ROWS, width)
    )
    context[...] = dot(g_low, mat(3), 1, 1).astype(bf16)

    @pl.loop(0, blocks)
    def _(b):
        at = pl.ds(pl.multiple_of(b * block, block), block)
        for pair in range(pairs):
            lanes = slice(pair * block, (pair + 1) * block)
            q, k, v, dc = queries[at, lanes], keys[at, lanes], values[at, lanes], context[at, lanes]
            grads = []
            for side in range(2):
                p = probs[b, 2 * pair + side]
                dp = dot(half_of(dc, side), v, 1, 1)
                ds = (
                    scale * p * (dp - jnp.sum(dp * p, axis=1, keepdims=True))
                ).astype(bf16)
                grads.append(
                    (dot(ds, k), dot(ds, q, 0, 0), dot(p.astype(bf16), dc, 0, 0))
                )
            queries[at, lanes] = jnp.where(low_lane, grads[0][0], grads[1][0]).astype(bf16)
            keys[at, lanes] = jnp.where(low_lane, grads[0][1], grads[1][1]).astype(bf16)
            values[at, lanes] = jnp.where(low_lane, grads[0][2], grads[1][2]).astype(bf16)

    hidden = normed[...]
    d_hid = jnp.zeros((rows, width), f32)
    for m, g in enumerate((queries, keys, values)):
        g_now = g[...]
        gpack_ref[:, ROWS * m : ROWS * (m + 1)] = (
            dot(hidden, g_now, 0, 0).astype(bf16).reshape(groups, ROWS, width)
        )
        d_hid = d_hid + dot(g_now, mat(m), 1, 1)
    summ = summary[...]
    unit_sum = unit(summ)
    flat_sum = summ * unit_sum
    d_gain_attn = jnp.sum(d_hid * flat_sum, axis=0, keepdims=True)
    d_flat = d_hid * gain[1:2]
    gsum[...] = (
        gafter[...]
        + unit_sum * (d_flat - flat_sum * jnp.mean(d_flat * flat_sum, axis=-1, keepdims=True))
    ).astype(bf16)

    acc_r[...] = jnp.zeros_like(acc_r)

    @pl.loop(0, clips)
    def _(c):
        at = pl.ds(pl.multiple_of(c * read, read), read)
        z_m, z_f = zm[c], zf[c]
        g = gsum[at]
        d_m, d_f = dot(g, z_m, 1, 1), dot(g, z_f, 1, 1)
        a_m, a_f, l_m, l_f = aread_m[c], aread_f[c], lread_m[c], lread_f[c]
        r_m, r_f = rm_s[c], rf_s[c]
        mean = jnp.sum(d_m * a_m, axis=1, keepdims=True) + jnp.sum(
            d_f * a_f, axis=1, keepdims=True
        )
        b_m, b_f = a_m * (d_m - mean), a_f * (d_f - mean)
        k_m = cm_s[c] + (r_m * r_m) * (jnp.sum(b_m * l_m, axis=0, keepdims=True) * (1.0 / width))
        k_f = cf_s[c] + (r_f * r_f) * (jnp.sum(b_f * l_f, axis=0, keepdims=True) * (1.0 / width))
        h_m = (b_m * r_m[0:1]).astype(bf16)
        h_f = (b_f * r_f[0:1]).astype(bf16)
        acc_r[...] += dot(h_m, z_m) + dot(h_f, z_f)
        arm[c, 2 * mem + read : 2 * wide] = h_m
        arf[c, 2 * mem + read : 2 * wide] = h_f
        back = jnp.concatenate([ctm[c], table[0:mem], g, table[mem:wide]], axis=0)
        t_m, t_f = k_m.T, k_f.T
        zm[c] = (dot(arm[c], back, 0, 0) - z_m.astype(f32) * t_m[:, 0:1]).astype(bf16)
        zf[c] = (dot(arf[c], back, 0, 0) - z_f.astype(f32) * t_f[:, 0:1]).astype(bf16)
        pltpu.make_async_copy(zm.at[c, pl.ds(read, mem)], gm_h.at[c], out_sem.at[1, c]).start()
        pltpu.make_async_copy(zf.at[c], gf_h.at[c], out_sem.at[2, c]).start()

    zero_rows = jnp.zeros((1, width), f32)
    rest = jnp.concatenate(
        [zero_rows, d_gain_attn, d_gain_mlp, zero_rows, jnp.zeros((12, width), f32)], axis=0
    )
    stacked = jnp.concatenate([acc_w[...], acc_r[...], rest], axis=0)
    gpack_ref[:, SMALL:PACK] = jnp.zeros((groups, ROWS, width), bf16)
    gpack_ref[:, SMALL:PACK, 0:128] = stacked.T.astype(bf16).reshape(groups, ROWS, 128)
    for d in range(groups):
        gpack_ref[d, SMALL : SMALL + 1, 128 : 128 + piece] = bias[
            :, piece * d : piece * (d + 1)
        ].astype(bf16)

    @pl.loop(0, clips)
    def _(c):
        pltpu.make_async_copy(nm.at[c], nm_h.at[c], out_sem.at[0, c]).wait()
        pltpu.make_async_copy(zm.at[c, pl.ds(read, mem)], gm_h.at[c], out_sem.at[1, c]).wait()
        pltpu.make_async_copy(zf.at[c], gf_h.at[c], out_sem.at[2, c]).wait()


def run_step(frames, valid, memory, ct_memory, ct_read, wpack, weights=()):
    clips, toks, width = frames.shape
    mem, read = memory.shape[1], ct_read.shape[1]
    groups = width // ROWS
    rows, wide = clips * read, mem + read
    vm, sem = pltpu.VMEM, pltpu.SemaphoreType.DMA
    hbm = pl.BlockSpec(memory_space=pl.ANY)
    inside = pl.BlockSpec(memory_space=pltpu.VMEM)
    made = jax.ShapeDtypeStruct
    packed = made((groups, PACK, width), bf16)
    out_shape = (
        made(memory.shape, bf16),
        made((rows, width), bf16),
        made(frames.shape, bf16),
        made(memory.shape, bf16),
        packed,
    )
    out_specs = (hbm, inside, hbm, hbm, inside)
    in_specs = [hbm, inside, hbm, hbm, inside]
    scratch = [
        vm((clips, wide, width), bf16),
        vm((clips, toks, width), bf16),
        vm((clips, mem, width), bf16),
        vm((clips, mem, width), bf16),
        vm((8, groups, ROWS, width), bf16),
        vm((groups, 64, width), bf16),
        vm((groups, ROWS, width), bf16),
        vm((wide, width), bf16),
        vm((8, width), f32),
        vm((1, 4 * width), f32),
        vm((clips, 2 * wide, wide), bf16),
        vm((clips, 2 * wide, toks), bf16),
        vm((clips, read, wide), f32),
        vm((clips, read, toks), f32),
        vm((clips, read, wide), f32),
        vm((clips, read, toks), f32),
        vm((clips, 8, wide), f32),
        vm((clips, 8, toks), f32),
        vm((clips, 8, wide), f32),
        vm((clips, 8, toks), f32),
        vm((rows, width), f32),
        vm((rows, width), bf16),
        vm((rows, width), bf16),
        vm((rows, width), bf16),
        vm((rows // 128, HEADS, 128, 128), f32),
        vm((rows, width), bf16),
        vm((rows, width), f32),
        vm((rows, width), bf16),
        vm((rows, 4 * width), f32),
        vm((rows, 4 * width), bf16),
        vm((rows, width), f32),
        vm((rows, width), bf16),
        vm((mem, width), f32),
        vm((read, width), f32),
        sem((3, clips)),
        sem((10,)),
        sem((3, clips)),
    ]
    params = dict(vmem_limit_bytes=60 * 1024 * 1024)
    kernel = functools.partial(step_kernel, lambda: None)
    operands = (frames, valid, memory, ct_memory, ct_read.reshape(rows, width))
    if weights:
        n = lax.axis_size("sub")
        kernel = gather_step_kernel
        operands = (*weights, *operands)
        in_specs = [inside] * len(weights) + in_specs
        out_shape, out_specs = (*out_shape, packed), (*out_specs, hbm)
        scratch = [
            vm((PACK, width), bf16), sem, *[sem((n,))] * 6, sem((4, n)), *[sem((n,))] * 5, sem((4, n)), *scratch,
        ]
        params.update(collective_id=1, has_side_effects=True)
    else:
        operands, in_specs = (*operands, wpack), [*in_specs, hbm]
    outs = pl.pallas_call(
        functools.partial(kernel, clips),
        out_shape=out_shape,
        in_specs=in_specs,
        out_specs=out_specs,
        scratch_shapes=scratch,
        compiler_params=pltpu.CompilerParams(**params),
        name="clip_step",
    )(*operands)
    new_memory, read_out, grad_frames, grad_memory, gpack = outs[:5]
    return new_memory, read_out.reshape(ct_read.shape), grad_frames, grad_memory, gpack


def gather_step_kernel(clips, *refs):
    weights, ins, outs, scratch = refs[0:7], refs[7:12], refs[12:18], refs[18:]

    def gather():
        gather_kernel(*weights, outs[5], *scratch[:15])

    step_kernel(gather, clips, *ins, outs[5], *outs[:5], *scratch[15:])


MESH = pl.DeviceIdType.MESH
X, Y, CORE = 2, 4, 1
CUT = 112


def remote(src, dst, send, recv, device):
    return pltpu.make_async_remote_copy(
        src_ref=src, dst_ref=dst, send_sem=send, recv_sem=recv, device_id=device, device_id_type=MESH
    )


def gather_kernel(attn, w_in, w_out, s_read, s_write, gains, bias, out, x_ref, own_sem, up, down, sx, sy, fx, fy, sc, rz, rx, ry, rdx, rdy, rc):
    dp, p = lax.axis_index("dp"), lax.axis_index("sub")
    last = lax.axis_size("sub") - 1
    count = last + 1

    def flip(mask):
        return (jnp.bitwise_xor(dp, mask), p)

    def unit(mask, s):
        return out.at[jnp.bitwise_xor(dp, mask) * count + s]

    barrier = pltpu.get_barrier_semaphore()
    for mask in (X, Y, CORE):
        pl.semaphore_signal(barrier, inc=1, device_id=flip(mask), device_id_type=MESH)

    @pl.when(p < last)
    def _():
        pl.semaphore_signal(barrier, inc=1, device_id=(dp, p + 1), device_id_type=MESH)

    @pl.when(p > 0)
    def _():
        pl.semaphore_signal(barrier, inc=1, device_id=(dp, p - 1), device_id_type=MESH)

    width = x_ref.shape[1]
    for m in range(4):
        x_ref[ROWS * m : ROWS * (m + 1)] = attn[m].astype(bf16)
        x_ref[64 + ROWS * m : 64 + ROWS * (m + 1)] = w_in[:, width * m : width * (m + 1)].astype(bf16)
    x_ref[128:192] = w_out[...].astype(bf16)
    x_ref[SMALL:PACK] = jnp.zeros((ROWS, width), bf16)
    x_ref[SMALL:PACK, 0:96] = s_write[...].astype(bf16)
    x_ref[SMALL:PACK, 96:112] = s_read[...].astype(bf16)
    x_ref[SMALL:PACK, 112:116] = turn_gains(gains[...]).astype(bf16)
    x_ref[SMALL : SMALL + 1, 128:192] = bias[...].astype(bf16)
    own = pltpu.make_async_copy(x_ref, unit(0, p), own_sem)
    own.start()
    pl.semaphore_wait(barrier, 3 + jnp.where(p < last, 1, 0) + jnp.where(p > 0, 1, 0))

    def chain(step, way, s, src):
        sems = up if way > 0 else down
        return remote(src, unit(0, s), sems.at[step], rz.at[s], (dp, p + way))

    def side(mask, s, src):
        send, recv = (sx, rx) if mask == X else (sy, ry)
        return remote(src, unit(0, s), send.at[s], recv.at[s], flip(mask))

    def halves(mask, s):
        other = Y if mask == X else X
        part = pl.ds(0, CUT) if mask == X else pl.ds(CUT, PACK - CUT)
        send, recv = (fy, rdy) if mask == X else (fx, rdx)
        ref = unit(mask, s).at[part]
        return remote(ref, ref, send.at[s], recv.at[s], flip(other))

    def cross(kind, s, src):
        return remote(src, unit((0, X, Y, X + Y)[kind], s), sc.at[kind, s], rc.at[kind, s], flip(CORE))

    def share(s, src):
        side(X, s, src).start()
        side(Y, s, src).start()
        cross(0, s, src).start()

    @pl.when(p < last)
    def _():
        chain(0, 1, p, x_ref).start()

    @pl.when(p > 0)
    def _():
        chain(0, -1, p, x_ref).start()

    share(p, x_ref)

    def arrived(s):
        for mask, kind in ((X, 1), (Y, 2)):
            recv = rx if mask == X else ry
            got = unit(mask, s)
            remote(got, got, recv.at[s], recv.at[s], flip(mask)).wait_recv()
            halves(mask, s).start()
            cross(kind, s, got).start()

    def arrivals(k):
        if k == 0:
            arrived(p)
            return

        @pl.when(p >= k)
        def _():
            arrived(p - k)

        @pl.when(p + k <= last)
        def _():
            arrived(p + k)

    for k in range(1, count):
        for way in (1, -1):

            @pl.when(p >= k if way > 0 else p + k <= last)
            def _():
                s = p - k * way
                got = unit(0, s)
                remote(got, got, rz.at[s], rz.at[s], (dp, p)).wait_recv()
                if k < last:

                    @pl.when(p < last if way > 0 else p > 0)
                    def _():
                        chain(k, way, s, got).start()

                share(s, got)

        arrivals(k - 1)
    arrivals(count - 1)
    for s in range(count):
        for recv, part in ((rdy, pl.ds(0, CUT)), (rdx, pl.ds(CUT, PACK - CUT))):
            got = unit(X + Y, s).at[part]
            remote(got, got, recv.at[s], recv.at[s], flip(X)).wait_recv()
        cross(3, s, unit(X + Y, s)).start()
    for s in range(count):
        for kind in range(4):
            got = unit((CORE, X + CORE, Y + CORE, X + Y + CORE)[kind], s)
            remote(got, got, rc.at[kind, s], rc.at[kind, s], flip(CORE)).wait_recv()
    own.wait()
    for s in range(count):
        for mask in (X, Y):
            side(mask, s, unit(0, s)).wait_send()
            halves(mask, s).wait_send()
        for kind in range(4):
            cross(kind, s, unit((0, X, Y, X + Y)[kind], s)).wait_send()
    for k in range(last):

        @pl.when((p < last) & (p >= k))
        def _():
            chain(k, 1, p - k, unit(0, p - k)).wait_send()

        @pl.when((p > 0) & (p + k <= last))
        def _():
            chain(k, -1, p + k, unit(0, p + k)).wait_send()


def reduce_kernel(g_h, attn_mom, w_in_mom, w_out_mom, s_read_mom, s_write_mom, gains, out, buf, gl, rc, ra, rb, rx, ry, rz, acc, lsem, cs, cr, as_, ar, bs, br, xs, xr, ys, yr, zs, zr, pk, gsend, grecv, gown):
    dp, p = lax.axis_index("dp"), lax.axis_index("sub")
    count = lax.axis_size("sub")
    masks = (0, X, Y, X + Y)

    def flip(mask):
        return (jnp.bitwise_xor(dp, mask), p)

    def column(mask):
        return g_h.at[pl.ds(jnp.bitwise_xor(dp, mask) * count, count)]

    local = [pltpu.make_async_copy(column(masks[k]), gl.at[k], lsem.at[k]) for k in range(4)]
    for k in (3, 1, 2, 0):
        local[k].start()
    barrier = pltpu.get_barrier_semaphore()
    for mask in (X, Y, CORE):
        pl.semaphore_signal(barrier, inc=1, device_id=flip(mask), device_id_type=MESH)
    for off in range(1, count):
        pl.semaphore_signal(
            barrier, inc=1, device_id=(dp, lax.rem(p + off, count)), device_id_type=MESH
        )
    pl.semaphore_wait(barrier, 3 + count - 1)
    crossed = [
        remote(column(masks[k] + CORE), rc.at[k], cs.at[k], cr.at[k], flip(CORE)) for k in range(4)
    ]
    for k in (3, 1, 2, 0):
        crossed[k].start()
    order = [lax.rem(p + off, count) for off in (2, 1, 3, 0)]
    first, second = pl.ds(0, CUT), pl.ds(CUT, PACK - CUT)

    def ready(k):
        local[k].wait()
        crossed[k].wait_recv()

    def total(k, s):
        return gl[k, s].astype(f32) + rc[k, s].astype(f32)

    sent = [crossed[k] for k in range(4)]

    def push(copy):
        copy.start()
        sent.append(copy)

    ready(3)
    for s in order:
        gl[3, s] = total(3, s).astype(bf16)
        push(remote(gl.at[3, s, first], ra.at[s], as_.at[s], ar.at[s], flip(X)))
        push(remote(gl.at[3, s, second], rb.at[s], bs.at[s], br.at[s], flip(Y)))
    ready(1)
    ready(2)
    for s in order:
        sum_x, sum_y = total(1, s), total(2, s)
        remote(rb.at[s], rb.at[s], bs.at[s], br.at[s], flip(Y)).wait_recv()
        gl[1, s, 0:CUT] = sum_x[0:CUT].astype(bf16)
        gl[1, s, CUT:PACK] = (sum_x[CUT:PACK] + rb[s].astype(f32)).astype(bf16)
        push(remote(gl.at[1, s], rx.at[s], xs.at[s], xr.at[s], flip(X)))
        remote(ra.at[s], ra.at[s], as_.at[s], ar.at[s], flip(X)).wait_recv()
        gl[2, s, 0:CUT] = (sum_y[0:CUT] + ra[s].astype(f32)).astype(bf16)
        gl[2, s, CUT:PACK] = sum_y[CUT:PACK].astype(bf16)
        push(remote(gl.at[2, s], ry.at[s], ys.at[s], yr.at[s], flip(Y)))
    ready(0)
    for i, s in enumerate(order):
        mine = total(0, s)
        remote(rx.at[s], rx.at[s], xs.at[s], xr.at[s], flip(X)).wait_recv()
        remote(ry.at[s], ry.at[s], ys.at[s], yr.at[s], flip(Y)).wait_recv()
        mine = mine + rx[s].astype(f32) + ry[s].astype(f32)
        if i < count - 1:
            gl[0, s] = mine.astype(bf16)
            push(remote(gl.at[0, s], rz.at[i], zs.at[i], zr.at[i], (dp, s)))
        else:
            acc[...] = mine
    for i in range(count - 1):
        remote(rz.at[i], rz.at[i], zs.at[i], zr.at[i], (dp, p)).wait_recv()
        acc[...] += rz[i].astype(f32)
    out[...] = acc[...]
    send_momentum(
        acc, attn_mom, w_in_mom, w_out_mom, s_read_mom, s_write_mom, gains, pk, buf, gsend, grecv, gown
    )
    for copy in sent:
        copy.wait_send()


def reduce_pack(gpack, *state):
    groups, rows, width = gpack.shape
    n = lax.axis_size("sub")
    sem, vm = pltpu.SemaphoreType.DMA, pltpu.VMEM
    anywhere, inside = pl.BlockSpec(memory_space=pl.ANY), pl.BlockSpec(memory_space=pltpu.VMEM)
    return pl.pallas_call(
        reduce_kernel,
        out_shape=(
            jax.ShapeDtypeStruct((rows, width), f32),
            jax.ShapeDtypeStruct((groups, 64, width), bf16),
        ),
        in_specs=[anywhere] + [inside] * len(state),
        out_specs=(inside, anywhere),
        scratch_shapes=[
            vm((4, n, rows, width), bf16),
            vm((4, n, rows, width), bf16),
            vm((n, CUT, width), bf16),
            vm((n, rows - CUT, width), bf16),
            vm((n, rows, width), bf16),
            vm((n, rows, width), bf16),
            vm((n - 1, rows, width), bf16),
            vm((rows, width), f32),
            sem((4,)), sem((4,)), sem((4,)),
            *[sem((n,))] * 10,
            vm((rows, width), bf16),
            sem((len(OWNERS),)),
            sem((groups,)),
            sem,
        ],
        compiler_params=pltpu.CompilerParams(
            collective_id=2, has_side_effects=True, vmem_limit_bytes=60 * 1024 * 1024
        ),
        name="reduce_grads",
    )(gpack, *state)


OWNERS = ((2, 0), (4, 3), (2, 3), (4, 0), (0, 1), (6, 2), (0, 3))
PIECES = ((0, 16), (16, 16), (32, 16), (48, 16), (64, 64), (128, 64), (192, 16))


def is_owner(m):
    return (lax.axis_index("dp") == OWNERS[m][0]) & (lax.axis_index("sub") == OWNERS[m][1])


def turn_gains(g):
    eye = (
        lax.broadcasted_iota(jnp.int32, (4, 4), 0) == lax.broadcasted_iota(jnp.int32, (4, 4), 1)
    ).astype(bf16)
    return lax.dot_general(g.astype(bf16), eye, (((0,), (0,)), ((), ())), preferred_element_type=f32)


def small_grads(red, gains_t):
    return (
        red[SMALL:PACK, 0:96] * gains_t[:, 3:4],
        red[SMALL:PACK, 96:112] * gains_t[:, 0:1],
    )


def send_momentum(acc, attn_mom, w_in_mom, w_out_mom, s_read_mom, s_write_mom, gains, pk, buf, gsend, grecv, gown):
    width = acc.shape[1]
    count = lax.axis_size("sub")
    me = lax.axis_index("dp") * count + lax.axis_index("sub")
    for m in range(4):
        at = slice(ROWS * m, ROWS * (m + 1))
        pk[at] = (0.5 * attn_mom[m] + acc[at]).astype(bf16)
        at = slice(64 + ROWS * m, 64 + ROWS * (m + 1))
        pk[at] = (0.5 * w_in_mom[:, width * m : width * (m + 1)] + acc[at]).astype(bf16)
    pk[128:192] = (0.5 * w_out_mom[...] + acc[128:192]).astype(bf16)
    g_write, g_read = small_grads(acc, turn_gains(gains[...]))
    pk[SMALL:PACK] = jnp.zeros((ROWS, width), bf16)
    pk[SMALL:PACK, 0:96] = (0.5 * s_write_mom[...] + g_write).astype(bf16)
    pk[SMALL:PACK, 96:112] = (0.5 * s_read_mom[...] + g_read).astype(bf16)

    def piece(m):
        start, size = PIECES[m]
        return pk.at[pl.ds(start, size)], buf.at[me, pl.ds(0, size)]

    def away(m):
        src, dst = piece(m)
        return remote(src, dst, gsend.at[m], grecv.at[me], OWNERS[m])

    def home(m):
        src, dst = piece(m)
        return pltpu.make_async_copy(src, dst, gown)

    many = range(len(OWNERS))
    for m in (4, 5, 0, 1, 2, 3, 6):

        @pl.when(jnp.logical_not(is_owner(m)))
        def _():
            away(m).start()

    for m in many:

        @pl.when(is_owner(m))
        def _():
            home(m).start()

            @pl.loop(0, buf.shape[0])
            def _(d):
                @pl.when(d != me)
                def _():
                    got = buf.at[d, pl.ds(0, PIECES[m][1])]
                    remote(got, got, grecv.at[d], grecv.at[d], OWNERS[m]).wait_recv()

            home(m).wait()

        @pl.when(jnp.logical_not(is_owner(m)))
        def _():
            away(m).wait_send()


def iterate(x, low):
    blocks = x.shape[0]
    total = jnp.zeros((1, 1), f32)
    for j in range(blocks):
        total = total + jnp.sum(x[j] * x[j], keepdims=True)
    scale = 1.0 / (jnp.sqrt(total) + 1e-07)
    for j in range(blocks):
        x[j] = x[j] * scale
        low[j] = x[j].astype(bf16)

    @pl.loop(0, 5)
    def _(_):
        q = dot(low[0], low[0], 1, 1)
        for j in range(1, blocks):
            q = q + dot(low[j], low[j], 1, 1)
        q_low = q.astype(bf16)
        mixed = (NS[1] * q + NS[2] * dot(q_low, q_low)).astype(bf16)
        for j in range(blocks):
            new = NS[0] * x[j] + dot(mixed, low[j])
            x[j] = new
            low[j] = new.astype(bf16)


def exact_dot(a, b, ca=1, cb=0):
    return lax.dot_general(a, b, (((ca,), (cb,)), ((), ())), preferred_element_type=f32, precision=highest)


def iterate_small(x, same):
    norm = jnp.sum(x * x, axis=1, keepdims=True)
    total = jnp.sum(jnp.where(same, norm.T, 0.0), axis=1, keepdims=True)
    x = x * (1.0 / (jnp.sqrt(total) + 1e-07))
    for _ in range(5):
        q = jnp.where(same, exact_dot(x, x, 1, 1), 0.0)
        mixed = NS[1] * q + NS[2] * exact_dot(q, q)
        x = NS[0] * x + exact_dot(mixed, x)
    return x


def muon_kernel(
    red, buf, attn_mom, w_in_mom, w_out_mom, s_read_mom, s_write_mom, s_read, s_write,
    gains, gains_first, gains_second, bias, bias_first, bias_second,
    xo, g_attn, g_in, g_out, g_read, g_write, g_gains, g_bias,
    n_gains, n_bias, m_attn, m_in, m_out, m_read, m_write,
    n_gains_first, n_gains_second, n_bias_first, n_bias_second,
    x, low,
):
    width = red.shape[1]
    groups = buf.shape[0]
    for m in range(4):
        lanes = slice(width * m, width * (m + 1))
        g = red[ROWS * m : ROWS * (m + 1)]
        g_attn[m] = g
        m_attn[m] = 0.5 * attn_mom[m] + g
        g = red[64 + ROWS * m : 64 + ROWS * (m + 1)]
        g_in[:, lanes] = g
        m_in[:, lanes] = 0.5 * w_in_mom[:, lanes] + g
    g = red[128:192]
    g_out[...] = g
    m_out[...] = 0.5 * w_out_mom[...] + g
    gains_t = turn_gains(gains[...])
    made_write, made_read = small_grads(red, gains_t)
    g_write[...] = made_write
    g_read[...] = made_read
    m_write[...] = 0.5 * s_write_mom[...] + made_write
    m_read[...] = 0.5 * s_read_mom[...] + made_read
    low_write = s_write[...].astype(bf16).astype(f32)
    low_read = s_read[...].astype(bf16).astype(f32)
    to_read = jnp.sum(low_read * red[SMALL:PACK, 96:112], axis=1, keepdims=True)
    to_write = jnp.sum(low_write * red[SMALL:PACK, 0:96], axis=1, keepdims=True)
    column = lax.broadcasted_iota(jnp.int32, (ROWS, 128), 1)
    wide = jnp.where(
        column == 112, to_read, jnp.where(column == 115, to_write, red[SMALL:PACK, 0:128])
    )
    grad_gains = wide.T[112:116]
    g_gains[...] = grad_gains
    n_gains[...], n_gains_first[...], n_gains_second[...] = adam_step(
        gains[...], gains_first[...], gains_second[...], grad_gains
    )
    grad_bias = red[SMALL : SMALL + 1, 128:192]
    g_bias[...] = grad_bias
    n_bias[...], n_bias_first[...], n_bias_second[...] = adam_step(
        bias[...], bias_first[...], bias_second[...], grad_bias
    )

    @pl.when(is_owner(0) | is_owner(1) | is_owner(2) | is_owner(3))
    def _():
        x[0] = buf[:, 0:ROWS].reshape(width, width).astype(f32)
        iterate(x.at[0:1], low.at[0:1])
        xo[:, 0:ROWS] = low[0].reshape(groups, ROWS, width)

    @pl.when(is_owner(4))
    def _():
        for j in range(4):
            x[j] = buf[:, ROWS * j : ROWS * (j + 1)].reshape(width, width).astype(f32)
        iterate(x, low)
        for j in range(4):
            xo[:, ROWS * j : ROWS * (j + 1)] = low[j].reshape(groups, ROWS, width)

    @pl.when(is_owner(5))
    def _():
        per = groups // 4
        for j in range(4):
            x[j] = buf[per * j : per * (j + 1)].reshape(width, width).astype(f32).T
        iterate(x, low)
        for j in range(4):
            xo[per * j : per * (j + 1)] = x[j].T.astype(bf16).reshape(per, 64, width)

    @pl.when(is_owner(6))
    def _():
        table = buf[:, 0:ROWS, 0:128].reshape(width, 128).astype(f32).T
        row = lax.broadcasted_iota(jnp.int32, (128, 128), 0)
        col = lax.broadcasted_iota(jnp.int32, (128, 128), 1)
        same = ((row < 96) & (col < 96)) | ((row >= 96) & (col >= 96))
        made = iterate_small(table, same)
        xo[:, 0:ROWS, 0:128] = made.T.astype(bf16).reshape(groups, ROWS, 128)


def spread_kernel(xo, xrec, ssem, rsem, osem):
    count = lax.axis_size("sub")
    me = lax.axis_index("dp") * count + lax.axis_index("sub")
    groups = xo.shape[0]
    many = range(len(OWNERS))
    barrier = pltpu.get_barrier_semaphore()
    for m in many:

        @pl.when(jnp.logical_not(is_owner(m)))
        def _():
            pl.semaphore_signal(barrier, inc=1, device_id=OWNERS[m], device_id_type=MESH)

    for m in many:
        start, size = PIECES[m]

        def target(m=m, start=start, size=size):
            return xrec.at[pl.ds(start, size)]

        def away(d, m=m, size=size):
            return remote(
                xo.at[d, pl.ds(0, size)], target(), ssem.at[d], rsem.at[m], (d // count, lax.rem(d, count))
            )

        @pl.when(is_owner(m))
        def _():
            pl.semaphore_wait(barrier, groups - 1)
            home = pltpu.make_async_copy(xo.at[me, pl.ds(0, size)], target(), osem)
            home.start()

            @pl.loop(0, groups)
            def _(d):
                @pl.when(d != me)
                def _():
                    away(d).start()

            home.wait()

            @pl.loop(0, groups)
            def _(d):
                @pl.when(d != me)
                def _():
                    away(d).wait_send()

    for m in many:
        start, size = PIECES[m]

        @pl.when(jnp.logical_not(is_owner(m)))
        def _():
            got = xrec.at[pl.ds(start, size)]
            remote(got, got, rsem.at[m], rsem.at[m], OWNERS[m]).wait_recv()


def finish_kernel(xrec, attn, w_in, w_out, s_read, s_write, n_attn, n_in, n_out, n_read, n_write):
    width = xrec.shape[1]
    for m in range(4):
        lanes = slice(width * m, width * (m + 1))
        n_attn[m] = attn[m] - xrec[ROWS * m : ROWS * (m + 1)].astype(f32)
        n_in[:, lanes] = w_in[:, lanes] - xrec[64 + ROWS * m : 64 + ROWS * (m + 1)].astype(f32)
    n_out[...] = w_out[...] - 2.0 * xrec[128:192].astype(f32)
    small = xrec[SMALL:PACK, 0:128].astype(f32)
    n_write[...] = s_write[...] - math.sqrt(512 / 96) * small[:, 0:96]
    n_read[...] = s_read[...] - math.sqrt(512 / 16) * small[:, 96:112]


highest = lax.Precision.HIGHEST
NS = (3.4445, -4.775, 2.0315)


def canonical(attn, w_in, w_out, s_read, s_write, gains, bias):
    width = attn.shape[2]
    groups = attn.shape[1] // ROWS
    a = attn.astype(bf16).reshape(4, groups, ROWS, width).transpose(1, 0, 2, 3)
    i = w_in.astype(bf16).reshape(groups, ROWS, 4, width).transpose(0, 2, 1, 3)
    o = w_out.astype(bf16).reshape(groups, 64, width)
    s = jnp.concatenate([s_write, s_read, gains.T], axis=1).astype(bf16)
    s = jnp.pad(s, ((0, 0), (0, 128 - s.shape[1]))).reshape(groups, ROWS, 128)
    b = bias.astype(bf16).reshape(groups, 1, 64)
    b = jnp.pad(b, ((0, 0), (0, ROWS - 1), (0, width - 128 - 64)))
    return jnp.concatenate(
        [
            a.reshape(groups, 64, width),
            i.reshape(groups, 64, width),
            o,
            jnp.concatenate([s, b], axis=2),
        ],
        axis=1,
    )


def natural(pack, mem, read):
    groups, _, width = pack.shape
    a = pack[:, 0:64].reshape(groups, 4, ROWS, width).transpose(1, 0, 2, 3)
    i = pack[:, 64:128].reshape(groups, 4, ROWS, width).transpose(0, 2, 1, 3)
    s = pack[:, SMALL:PACK, 0:128].reshape(groups * ROWS, 128)
    return (
        a.reshape(4, groups * ROWS, width),
        i.reshape(groups * ROWS, 4 * width),
        pack[:, 128:192].reshape(groups * 64, width),
        s[:, 0:mem],
        s[:, mem : mem + read],
        s[:, mem + read + 1 : mem + read + 3],
        pack[:, SMALL, 128:192].reshape(groups * 64),
    )


def adam_step(weight, first, second, grad):
    first_new = 0.5 * first + 0.5 * grad
    second_new = 0.5 * second + 0.5 * grad * grad
    part = 1.0 - 0.5**10
    moved = 0.25 * (first_new / part) / (jnp.sqrt(second_new / part) + 1e-08)
    return weight - moved, first_new, second_new


def orthogonalize(matrix):
    tall = matrix.shape[0] > matrix.shape[1]
    x = matrix.T if tall else matrix
    x = x / (jnp.sqrt(jnp.sum(x * x)) + 1e-07)
    for _ in range(5):
        q = jnp.dot(x, x.T, precision=highest)
        mixed = NS[1] * q + NS[2] * jnp.dot(q, q, precision=highest)
        x = NS[0] * x + jnp.dot(mixed, x, precision=highest)
    return x.T if tall else x


def any_slice(
    frames, valid, memory, ct_memory, ct_read,
    attn, w_in, w_out, s_read, s_write, gains, bias,
    attn_mom, w_in_mom, w_out_mom, s_read_mom, s_write_mom,
    gains_first, gains_second, bias_first, bias_second,
):
    axes = ("dp", "sub")
    mem, read = memory.shape[1], ct_read.shape[1]

    def gather(v, axis):
        return lax.all_gather(v.astype(bf16), axes, axis=axis, tiled=True)

    def scatter(v, axis):
        return lax.psum_scatter(v, axes, scatter_dimension=axis, tiled=True)

    wpack = canonical(
        gather(attn, 1), gather(w_in, 0), gather(w_out, 0), gather(s_read, 0),
        gather(s_write, 0), gather(gains, 1), gather(bias, 0),
    )
    new_memory, read_out, grad_frames, grad_memory, gpack = run_step(
        frames, valid, memory, ct_memory, ct_read, wpack
    )
    sums = natural(gpack.astype(f32), mem, read)
    g_attn, g_in, g_out, sum_w, sum_r, g_two, g_bias = (
        scatter(v, axis) for v, axis in zip(sums, (1, 0, 0, 0, 0, 0, 0))
    )
    low_gain = gains.astype(bf16).astype(f32)
    low_w, low_r = s_write.astype(bf16).astype(f32), s_read.astype(bf16).astype(f32)
    g_s_write = low_gain[3][:, None] * sum_w
    g_s_read = low_gain[0][:, None] * sum_r
    g_gains = jnp.stack(
        [jnp.sum(low_r * sum_r, axis=1), g_two[:, 0], g_two[:, 1], jnp.sum(low_w * sum_w, axis=1)]
    )
    moms = (
        0.5 * attn_mom + g_attn,
        0.5 * w_in_mom + g_in,
        0.5 * w_out_mom + g_out,
        0.5 * s_read_mom + g_s_read,
        0.5 * s_write_mom + g_s_write,
    )
    whole = [gather(v, axis).astype(f32) for v, axis in zip(moms, (1, 0, 0, 0, 0))]
    matrices = [whole[0][m] for m in range(4)] + whole[1:]
    rank, count = lax.axis_index(axes), lax.axis_size(axes)
    owned = [
        lax.cond(rank == m * count // 8, orthogonalize, jnp.zeros_like, matrix)
        for m, matrix in enumerate(matrices)
    ]
    ortho = (
        scatter(jnp.stack(owned[:4]), 1), *(scatter(v, 0) for v in owned[4:])
    )
    stepped = []
    for weight, part, full in zip((attn, w_in, w_out, s_read, s_write), ortho, whole):
        ratio = max(1.0, full.shape[-2] / full.shape[-1]) ** 0.5
        stepped.append(weight - ratio * part)
    n_gains = adam_step(gains, gains_first, gains_second, g_gains)
    n_bias = adam_step(bias, bias_first, bias_second, g_bias)
    return (
        new_memory, read_out, grad_frames, grad_memory,
        g_attn, g_in, g_out, g_s_read, g_s_write, g_gains, g_bias,
        *stepped, n_gains[0], n_bias[0], *moms, n_gains[1], n_gains[2], n_bias[1], n_bias[2],
    )


def this_slice(
    frames, valid, memory, ct_memory, ct_read,
    attn, w_in, w_out, s_read, s_write, gains, bias,
    attn_mom, w_in_mom, w_out_mom, s_read_mom, s_write_mom,
    gains_first, gains_second, bias_first, bias_second,
):
    inside, anywhere = pl.BlockSpec(memory_space=pltpu.VMEM), pl.BlockSpec(memory_space=pl.ANY)

    def like(*arrays):
        return tuple(jax.ShapeDtypeStruct(a.shape, f32) for a in arrays)

    def row(v):
        return v.reshape(1, -1)

    new_memory, read_out, grad_frames, grad_memory, gpack = run_step(
        frames, valid, memory, ct_memory, ct_read, None,
        (attn, w_in, w_out, s_read, s_write, gains, row(bias)),
    )
    moms = (attn_mom, w_in_mom, w_out_mom, s_read_mom, s_write_mom)
    weights = (attn, w_in, w_out, s_read, s_write)
    red, buf = reduce_pack(gpack, *moms, gains)
    biases = (row(bias), row(bias_first), row(bias_second))
    groups, width = buf.shape[0], buf.shape[2]
    made = pl.pallas_call(
        muon_kernel,
        out_shape=(
            jax.ShapeDtypeStruct(buf.shape, bf16),
            *like(*weights, gains, biases[0]),
            *like(gains, biases[0]),
            *like(*moms, gains, gains, biases[0], biases[0]),
        ),
        in_specs=[inside] * 15,
        out_specs=(inside,) * 19 ,
        scratch_shapes=[pltpu.VMEM((4, width, width), f32), pltpu.VMEM((4, width, width), bf16)],
        compiler_params=pltpu.CompilerParams(vmem_limit_bytes=60 * 1024 * 1024),
        name="muon",
    )(red, buf, *moms, s_read, s_write, gains, gains_first, gains_second, *biases)
    xo, grads, (n_gains, n_bias), new_moms, adams = made[0], made[1:8], made[8:10], made[10:15], made[15:]
    sem = pltpu.SemaphoreType.DMA
    xrec = pl.pallas_call(
        spread_kernel,
        out_shape=jax.ShapeDtypeStruct((PACK, width), bf16),
        in_specs=[anywhere],
        out_specs=anywhere,
        scratch_shapes=[sem((groups,)), sem((len(OWNERS),)), sem],
        compiler_params=pltpu.CompilerParams(collective_id=3, has_side_effects=True),
        name="spread_ortho",
    )(xo)
    stepped = pl.pallas_call(
        finish_kernel,
        out_shape=like(*weights),
        in_specs=[inside] * 6,
        out_specs=(inside,) * 5,
        name="finish",
    )(xrec, *weights)
    flat = bias.shape
    return (
        new_memory, read_out, grad_frames, grad_memory,
        *grads[:6], grads[6].reshape(flat),
        *stepped, n_gains, n_bias.reshape(flat), *new_moms,
        adams[0], adams[1], adams[2].reshape(flat), adams[3].reshape(flat),
    )


def solution(mesh):
    both = ("dp", "sub")
    rows3, rows2, rows1 = P(both, None, None), P(both, None), P(both)
    mid, last = P(None, both, None), P(None, both)
    weights = (mid, rows2, rows2, rows2, rows2)
    here = (mesh.shape["dp"], mesh.shape["sub"]) == (8, 4)
    return jax.shard_map(
        this_slice if here else any_slice,
        mesh=mesh,
        in_specs=(
            rows3, rows2, rows3, rows3, rows3, *weights, last, rows1, *weights, last, last, rows1, rows1,
        ),
        out_specs=(
            rows3, rows3, rows3, rows3, *weights, last, rows1, *weights, last, rows1, *weights,
            last, last, rows1, rows1,
        ),
        check_vma=False,
    )
```

```python
import functools
import math

import jax
import jax.numpy as jnp
from jax import lax
from jax.experimental import pallas as pl
from jax.experimental.pallas import tpu as pltpu
from jax.sharding import PartitionSpec as P

f32 = jnp.float32
bf16 = jnp.bfloat16
MESH = pl.DeviceIdType.MESH

HEADS = 8
HEAD_DIM = 64
NORM_EPS = 1e-06
MASKED = -1000000000.0
GELU_A = math.sqrt(2.0 / math.pi)
GELU_B = 0.044715
VMEM_LIMIT = 60 * 1024 * 1024

ROWS = 16
PACK = 208
SMALL = 192
TINY = 256
X, Y, CORE = 2, 4, 1
PARTS = ((64, 64, 64, 0), (0, 32, 32, 64), (192, 16, 0, 96))


def dot(a, b, ca=1, cb=0):
    return lax.dot_general(a, b, (((ca,), (cb,)), ((), ())), preferred_element_type=f32)


def remote(src, dst, send, recv, device):
    return pltpu.make_async_remote_copy(
        src_ref=src, dst_ref=dst, send_sem=send, recv_sem=recv, device_id=device, device_id_type=MESH
    )


def lockstep(bodies):
    done = object()
    running = [body() for body in bodies]
    while running:
        running = [body for body in running if next(body, done) is not done]


def turn_gains(g):
    eye = (
        lax.broadcasted_iota(jnp.int32, (4, 4), 0) == lax.broadcasted_iota(jnp.int32, (4, 4), 1)
    ).astype(bf16)
    return dot(g.astype(bf16), eye, 0, 0)


def gather_weights(weights, out, tiny, x_ref, x_tiny, tsend, trecv, own_sem, up, down, sx, sy, fx, fy, sc, rz, rx, ry, rdx, rdy, rc):
    attn, w_in, w_out, s_read, s_write, gains, bias = weights
    dp, p = lax.axis_index("dp"), lax.axis_index("sub")
    count = lax.axis_size("sub")
    last = count - 1
    me = dp * count + p
    total = out.shape[0]
    size = x_ref.shape[0]
    cut = size // 2
    width = x_ref.shape[1]

    def device(d):
        return (d // count, lax.rem(d, count))

    def flip(mask):
        return (jnp.bitwise_xor(dp, mask), p)

    def unit(mask, s):
        return out.at[jnp.bitwise_xor(dp, mask) * count + s]

    def others(act):
        @pl.loop(0, total)
        def _(d):
            @pl.when(d != me)
            def _():
                act(d)

    barrier = pltpu.get_barrier_semaphore()
    others(lambda d: pl.semaphore_signal(barrier, inc=1, device_id=device(d), device_id_type=MESH))
    x_tiny[...] = jnp.zeros((ROWS, TINY), bf16)
    x_tiny[:, 0:96] = s_write[...].astype(bf16)
    x_tiny[:, 96:112] = s_read[...].astype(bf16)
    x_tiny[:, 112:116] = turn_gains(gains[...]).astype(bf16)
    x_tiny[0:1, 128:192] = bias[...].astype(bf16)
    for m in range(4):
        x_ref[ROWS * m : ROWS * (m + 1)] = attn[m].astype(bf16)
        x_ref[64 + ROWS * m : 64 + ROWS * (m + 1)] = w_in[:, width * m : width * (m + 1)].astype(bf16)
    x_ref[128:192] = w_out[...].astype(bf16)
    own = pltpu.make_async_copy(x_ref, unit(0, p), own_sem.at[0])
    own_tiny = pltpu.make_async_copy(x_tiny, tiny.at[me], own_sem.at[1])
    own.start()
    own_tiny.start()
    pl.semaphore_wait(barrier, total - 1)

    def tiny_copy(d, place):
        return remote(x_tiny, tiny.at[place], tsend.at[d], trecv.at[place], device(d))

    def chain(step, way, s, src):
        sems = up if way > 0 else down
        return remote(src, unit(0, s), sems.at[step], rz.at[s], (dp, p + way))

    def side(mask, s, src):
        send, recv = (sx, rx) if mask == X else (sy, ry)
        return remote(src, unit(0, s), send.at[s], recv.at[s], flip(mask))

    def halves(mask, s):
        other = Y if mask == X else X
        part = pl.ds(0, cut) if mask == X else pl.ds(cut, size - cut)
        send, recv = (fy, rdy) if mask == X else (fx, rdx)
        ref = unit(mask, s).at[part]
        return remote(ref, ref, send.at[s], recv.at[s], flip(other))

    def cross(kind, s, src):
        return remote(src, unit((0, X, Y, X + Y)[kind], s), sc.at[kind, s], rc.at[kind, s], flip(CORE))

    def share(s, src):
        side(X, s, src).start()
        side(Y, s, src).start()
        cross(0, s, src).start()

    others(lambda d: tiny_copy(d, me).start())

    @pl.when(p < last)
    def _():
        chain(0, 1, p, x_ref).start()

    @pl.when(p > 0)
    def _():
        chain(0, -1, p, x_ref).start()

    share(p, x_ref)

    def arrived(s):
        for mask, kind in ((X, 1), (Y, 2)):
            recv = rx if mask == X else ry
            got = unit(mask, s)
            remote(got, got, recv.at[s], recv.at[s], flip(mask)).wait_recv()
            halves(mask, s).start()
            cross(kind, s, got).start()

    def arrivals(k):
        if k == 0:
            arrived(p)
            return

        @pl.when(p >= k)
        def _():
            arrived(p - k)

        @pl.when(p + k <= last)
        def _():
            arrived(p + k)

    yield
    for k in range(1, count):
        for way in (1, -1):

            @pl.when(p >= k if way > 0 else p + k <= last)
            def _():
                s = p - k * way
                got = unit(0, s)
                remote(got, got, rz.at[s], rz.at[s], (dp, p)).wait_recv()
                if k < last:

                    @pl.when(p < last if way > 0 else p > 0)
                    def _():
                        chain(k, way, s, got).start()

                share(s, got)

        arrivals(k - 1)
        if k == 1:
            others(lambda d: tiny_copy(d, d).wait_recv())
            own_tiny.wait()
        yield
    arrivals(count - 1)
    yield
    for s in range(count):
        for recv, part in ((rdy, pl.ds(0, cut)), (rdx, pl.ds(cut, size - cut))):
            got = unit(X + Y, s).at[part]
            remote(got, got, recv.at[s], recv.at[s], flip(X)).wait_recv()
        cross(3, s, unit(X + Y, s)).start()
    for s in range(count):
        for kind in range(4):
            got = unit((CORE, X + CORE, Y + CORE, X + Y + CORE)[kind], s)
            remote(got, got, rc.at[kind, s], rc.at[kind, s], flip(CORE)).wait_recv()
    own.wait()
    others(lambda d: tiny_copy(d, me).wait_send())
    for s in range(count):
        for mask in (X, Y):
            side(mask, s, unit(0, s)).wait_send()
            halves(mask, s).wait_send()
        for kind in range(4):
            cross(kind, s, unit((0, X, Y, X + Y)[kind], s)).wait_send()
    for k in range(last):

        @pl.when((p < last) & (p >= k))
        def _():
            chain(k, 1, p - k, unit(0, p - k)).wait_send()

        @pl.when((p > 0) & (p + k <= last))
        def _():
            chain(k, -1, p + k, unit(0, p + k)).wait_send()


def load_weights(wpack_h, out, tiny, sems):
    big = pltpu.make_async_copy(wpack_h.at[:, pl.ds(0, SMALL)], out, sems.at[0])
    little = pltpu.make_async_copy(wpack_h.at[:, pl.ds(SMALL, ROWS), pl.ds(0, TINY)], tiny, sems.at[1])
    big.start()
    little.start()
    yield
    little.wait()
    yield
    yield
    yield
    yield
    big.wait()


class Sums:
    def __init__(self, gp, out, rc, ra, rb, rx, ry, rz, cs, cr, as_, ar, bs, br, xs, xr, ys, yr, zs, zr):
        self.__dict__.update(
            gp=gp, out=out, rc=rc, ra=ra, rb=rb, rx=rx, ry=ry, rz=rz,
            c=(cs, cr), a=(as_, ar), b=(bs, br), x=(xs, xr), y=(ys, yr), z=(zs, zr),
        )
        self.dp, self.p = lax.axis_index("dp"), lax.axis_index("sub")
        self.count = lax.axis_size("sub")
        self.order = [lax.rem(self.p + off, self.count) for off in (2, 1, 3, 0)]
        self.sent = []

    def flip(self, mask):
        return (jnp.bitwise_xor(self.dp, mask), self.p)

    def place(self, mask, s):
        return jnp.bitwise_xor(self.dp, mask) * self.count + s

    def push(self, pair, index, src, dst, device):
        copy = remote(src, dst, pair[0].at[index], pair[1].at[index], device)
        copy.start()
        self.sent.append(copy)

    def take(self, pair, index, ref):
        remote(ref, ref, pair[0].at[index], pair[1].at[index], (self.dp, self.p)).wait_recv()

    def core(self, g):
        start, n1, n2, _ = PARTS[g]
        rows = pl.ds(start, n1 + n2)
        for k in (3, 1, 2, 0):
            src = self.gp.at[pl.ds(self.place((0, X, Y, X + Y)[k] + CORE, 0), self.count), rows]
            self.push(self.c, (g, k), src, self.rc.at[k, :, rows], self.flip(CORE))

    def ready(self, g, k):
        start, n1, n2, _ = PARTS[g]
        self.take(self.c, (g, k), self.rc.at[k, :, pl.ds(start, n1 + n2)])

    def total(self, k, s, start, size):
        at = slice(start, start + size)
        own = self.gp[self.place((0, X, Y, X + Y)[k], s), at]
        return own.astype(f32) + self.rc[k, s, at].astype(f32)

    def diagonal(self, g):
        start, n1, n2, half = PARTS[g]
        self.ready(g, 3)
        for s in self.order:
            d = self.place(X + Y, s)
            self.gp[d, start : start + n1 + n2] = self.total(3, s, start, n1 + n2).astype(bf16)
            self.push(
                self.a, (g, s), self.gp.at[d, pl.ds(start, n1)], self.ra.at[s, pl.ds(half, n1)], self.flip(X)
            )
            if n2:
                self.push(
                    self.b, (g, s), self.gp.at[d, pl.ds(start + n1, n2)], self.rb.at[s, pl.ds(half, n2)], self.flip(Y)
                )

    def sides(self, g):
        start, n1, n2, half = PARTS[g]
        rows = pl.ds(start, n1 + n2)
        self.ready(g, 1)
        self.ready(g, 2)
        for s in self.order:
            d = self.place(X, s)
            self.gp[d, start : start + n1] = self.total(1, s, start, n1).astype(bf16)
            if n2:
                self.take(self.b, (g, s), self.rb.at[s, pl.ds(half, n2)])
                more = self.rb[s, half : half + n2].astype(f32)
                self.gp[d, start + n1 : start + n1 + n2] = (self.total(1, s, start + n1, n2) + more).astype(bf16)
            self.push(self.x, (g, s), self.gp.at[d, rows], self.rx.at[s, rows], self.flip(X))
            d = self.place(Y, s)
            if n2:
                self.gp[d, start + n1 : start + n1 + n2] = self.total(2, s, start + n1, n2).astype(bf16)
            self.take(self.a, (g, s), self.ra.at[s, pl.ds(half, n1)])
            more = self.ra[s, half : half + n1].astype(f32)
            self.gp[d, start : start + n1] = (self.total(2, s, start, n1) + more).astype(bf16)
            self.push(self.y, (g, s), self.gp.at[d, rows], self.ry.at[s, rows], self.flip(Y))

    def owners(self, g):
        start, n1, n2, _ = PARTS[g]
        size = n1 + n2
        rows = pl.ds(start, size)
        at = slice(start, start + size)
        self.ready(g, 0)
        for i, s in enumerate(self.order):
            self.take(self.x, (g, s), self.rx.at[s, rows])
            self.take(self.y, (g, s), self.ry.at[s, rows])
            mine = self.total(0, s, start, size) + self.rx[s, at].astype(f32) + self.ry[s, at].astype(f32)
            if i < self.count - 1:
                d = self.place(0, s)
                self.gp[d, at] = mine.astype(bf16)
                self.push(self.z, (g, i), self.gp.at[d, rows], self.rz.at[i, rows], (self.dp, s))
            else:
                self.out[at] = mine

    def final(self, g):
        start, n1, n2, _ = PARTS[g]
        size = n1 + n2
        at = slice(start, start + size)
        mine = self.out[at]
        for i in range(self.count - 1):
            self.take(self.z, (g, i), self.rz.at[i, pl.ds(start, size)])
            mine = mine + self.rz[i, at].astype(f32)
        self.out[at] = mine

    def finish(self):
        for copy in self.sent:
            copy.wait_send()


class NoSums:
    def __init__(self):
        self.core = self.diagonal = self.sides = self.owners = self.final = lambda g: None
        self.finish = lambda: None


def step(gather, sums, clips, ins, outs, scratch, wp, tiny, gp):
    frames_h, valid_ref, memory_h, ctm_h, ctr_ref = ins
    nm_h, ro_ref, gf_h, gm_h = outs
    (
        zm, zf, ctm, table, gain, bias, lw_m, lw_f, dw_m, dw_f, lr_m, lr_f, ar_m, ar_f, rm_s, rf_s, stat,
        summary, queries, keys, values, probs, context, after, normed, dgelu, activ, gafter, gsum,
        acc_w, acc_r, in_sem, out_sem,
    ) = scratch
    mem, read = memory_h.shape[1], ROWS
    toks = frames_h.shape[1]
    rows = clips * read
    groups = wp.shape[0]
    width = zm.shape[2]
    wide = mem + read
    mean_of = 1.0 / width

    def in_copies(c):
        return (
            pltpu.make_async_copy(memory_h.at[c], zm.at[c, pl.ds(read, mem)], in_sem.at[0, c]),
            pltpu.make_async_copy(frames_h.at[c], zf.at[c], in_sem.at[1, c]),
            pltpu.make_async_copy(ctm_h.at[c], ctm.at[c], in_sem.at[2, c]),
        )

    def out_copies(c):
        return (
            pltpu.make_async_copy(ctm.at[c], nm_h.at[c], out_sem.at[0, c]),
            pltpu.make_async_copy(zm.at[c, pl.ds(read, mem)], gm_h.at[c], out_sem.at[1, c]),
            pltpu.make_async_copy(zf.at[c], gf_h.at[c], out_sem.at[2, c]),
        )

    @pl.loop(0, clips)
    def _(c):
        zm[c, 0:read] = jnp.zeros((read, width), bf16)
        for copy in in_copies(c):
            copy.start()

    def clip_loop(low, high, batch, body):
        @pl.loop(low // batch, high // batch)
        def _(i):
            lockstep([functools.partial(body, i * batch + k) for k in range(batch)])

    ones = jnp.ones((8, 128), bf16)
    memory_lane = lax.broadcasted_iota(jnp.int32, (1, wide), 1) >= read

    def unit_rows(z):
        square = z * z
        folded = (square[:, 0:128] + square[:, 128:256]) + (square[:, 256:384] + square[:, 384:512])
        return lax.rsqrt(dot(ones, folded, 1, 1) * mean_of + NORM_EPS)

    def rows_of(c):
        return pl.ds(pl.multiple_of(c * read, read), read)

    def ahead(c):
        for copy in in_copies(c):
            copy.wait()
        z_m, z_f, g = zm[c], zf[c], ctm[c]
        yield
        r_m, r_f = unit_rows(z_m), unit_rows(z_f)
        yield
        d_m, d_f = dot(g, z_m, 1, 1), dot(g, z_f, 1, 1)
        yield
        rm_s[c], rf_s[c] = r_m, r_f
        dw_m[c], dw_f[c] = d_m, d_f

    def reading(c):
        z_m, z_f, r_m, r_f, d_m, d_f = zm[c], zf[c], rm_s[c], rf_s[c], dw_m[c], dw_f[c]
        live = valid_ref[pl.ds(c, 1), :] > 0
        tab = table[...]
        yield
        u_m, u_f = dot(tab, z_m, 1, 1), dot(tab, z_f, 1, 1)
        yield
        l_m = jnp.where(memory_lane, u_m * r_m[0:1], MASKED)
        l_f = jnp.where(live, u_f * r_f[0:1], MASKED)
        top = jnp.maximum(jnp.max(l_m, axis=1, keepdims=True), jnp.max(l_f, axis=1, keepdims=True))
        yield
        e_m, e_f = jnp.exp(l_m - top), jnp.exp(l_f - top)
        total = jnp.sum(e_m, axis=1, keepdims=True) + jnp.sum(e_f, axis=1, keepdims=True)
        inv = 1.0 / total[mem:]
        a_m, a_f = e_m[mem:] * inv, e_f[mem:] * inv
        yield
        made = dot(a_m.astype(bf16), z_m) + dot(a_f.astype(bf16), z_f)
        moved = jnp.sum(e_m[0:mem] * d_m, axis=1, keepdims=True) + jnp.sum(
            e_f[0:mem] * d_f, axis=1, keepdims=True
        )
        yield
        lw_m[c], lw_f[c] = l_m[0:mem], l_f[0:mem]
        lr_m[c], lr_f[c] = l_m[mem:], l_f[mem:]
        ar_m[c], ar_f[c] = a_m, a_f
        stat[c, :, 0:1], stat[c, :, 1:2], stat[c, :, 2:3] = top[0:mem], total[0:mem], moved
        summary[rows_of(c)] = made

    half = clips // 2
    third = clips // 3
    next(gather)
    clip_loop(0, half, 2, ahead)
    next(gather)
    turned = tiny[:, :, 0:128].reshape(groups * ROWS, 128).astype(f32).T
    gain[...] = turned[112:120]
    table[0:mem] = (turned[0:mem] * turned[115:116]).astype(bf16)
    table[mem:wide] = (turned[mem:wide] * turned[112:113]).astype(bf16)
    piece = bias.shape[1] // groups
    for d in range(groups):
        bias[:, piece * d : piece * (d + 1)] = tiny[d, 0:1, 128 : 128 + piece].astype(f32)
    clip_loop(half, clips, 2, ahead)
    next(gather)
    clip_loop(0, third, 2, reading)
    next(gather)
    clip_loop(third, 2 * third, 2, reading)
    next(gather)
    clip_loop(2 * third, clips, 2, reading)
    for _ in gather:
        pass

    def mat(m):
        return wp[:, ROWS * m : ROWS * (m + 1)].reshape(groups * ROWS, width)

    per = groups // 4

    def out_mat(j):
        return wp[per * j : per * (j + 1), 128:192].reshape(width, width)

    def unit(v):
        return lax.rsqrt(jnp.mean(v * v, axis=-1, keepdims=True) + NORM_EPS)

    summ = summary[...]
    hidden = (summ * unit(summ) * gain[1:2]).astype(bf16)
    normed[...] = hidden
    queries[...] = dot(hidden, mat(0)).astype(bf16)
    keys[...] = dot(hidden, mat(1)).astype(bf16)
    values[...] = dot(hidden, mat(2)).astype(bf16)
    scale = HEAD_DIM**-0.5
    block = 128
    blocks = rows // block
    pairs = HEADS // 2
    row_clip = lax.broadcasted_iota(jnp.int32, (block, block), 0) // read
    col_clip = lax.broadcasted_iota(jnp.int32, (block, block), 1) // read
    same = row_clip == col_clip
    low_lane = lax.broadcasted_iota(jnp.int32, (block, block), 1) < HEAD_DIM

    def half_of(v, side):
        zero = jnp.zeros_like(v)
        return jnp.where(low_lane, v, zero) if side == 0 else jnp.where(low_lane, zero, v)

    def attend(b, pair):
        at = pl.ds(pl.multiple_of(b * block, block), block)
        lanes = slice(pair * block, (pair + 1) * block)
        q, k, v = queries[at, lanes], keys[at, lanes], values[at, lanes]
        yield
        scores = [dot(half_of(q, side), k, 1, 1) for side in range(2)]
        yield
        masked = [jnp.where(same, s * scale, MASKED) for s in scores]
        tops = [jnp.max(s, axis=1, keepdims=True) for s in masked]
        yield
        parts = [jnp.exp(s - top) for s, top in zip(masked, tops)]
        sums_ = [jnp.sum(e, axis=1, keepdims=True) for e in parts]
        yield
        made = [e * (1.0 / s) for e, s in zip(parts, sums_)]
        got = [dot(p.astype(bf16), v) for p in made]
        yield
        probs[b, 2 * pair], probs[b, 2 * pair + 1] = made
        context[at, lanes] = jnp.where(low_lane, got[0], got[1]).astype(bf16)

    @pl.loop(0, blocks)
    def _(b):
        lockstep([functools.partial(attend, b, pair) for pair in range(pairs)])

    aft = summary[...] + dot(context[...], mat(3))
    after[...] = aft
    fed = (aft * unit(aft) * gain[2:3]).astype(bf16)
    for j in range(4):
        cols = slice(width * j, width * (j + 1))
        pre = dot(fed, mat(4 + j)) + bias[:, cols]
        square = pre * pre
        t = jnp.tanh(GELU_A * pre * (1.0 + GELU_B * square))
        most = 0.5 + 0.5 * t
        activ[:, cols] = (pre * most).astype(bf16)
        dgelu[:, cols] = most + (0.5 * GELU_A) * pre * (1.0 - t * t) * (
            1.0 + (3.0 * GELU_B) * square
        )
    out = after[...]
    for j in range(4):
        out = out + dot(activ[:, width * j : width * (j + 1)], out_mat(j))
    ro_ref[...] = out.astype(bf16)

    eye = lax.broadcasted_iota(jnp.int32, (read, read), 0) == lax.broadcasted_iota(
        jnp.int32, (read, read), 1
    )

    def joining(c):
        at = rows_of(c)
        ro, g, tab, ctr = ro_ref[at], ctm[c], table[0:mem], ctr_ref[at].astype(f32)
        top, total, moved = stat[c, :, 0:1], stat[c, :, 1:2], stat[c, :, 2:3]
        yield
        x = dot(jnp.concatenate([tab, g], axis=0), ro, 1, 1)
        r = unit_rows(ro)
        yield
        l, d = x[0:mem] * r[0:1], x[mem:]
        new_top = jnp.maximum(top, jnp.max(l, axis=1, keepdims=True))
        yield
        old = jnp.exp(top - new_top)
        e = jnp.exp(l - new_top)
        total = total * old + jnp.sum(e, axis=1, keepdims=True)
        moved = moved * old + jnp.sum(e * d, axis=1, keepdims=True)
        yield
        inv = 1.0 / total
        a, mean = e * inv, moved * inv
        b = a * (d - mean)
        k = (r[0:1] * r[0:1]) * (jnp.sum(b * l, axis=0, keepdims=True) * mean_of)
        left = jnp.concatenate([a, b * r[0:1], jnp.where(eye, -k, 0.0)], axis=0).astype(bf16)
        yield
        made = dot(left, jnp.concatenate([g, tab, ro], axis=0), 0, 0) + ctr
        yield
        zm[c, 0:read] = ro
        rm_s[c, :, 0:read] = r
        lw_m[c, :, 0:read], dw_m[c, :, 0:read] = l, d
        stat[c, :, 0:1], stat[c, :, 1:2] = new_top + jnp.log(total), mean
        gafter[at] = made

    clip_loop(0, clips, 4, joining)

    aft = after[...]
    unit_aft = unit(aft)
    flat_aft = aft * unit_aft
    fed = (flat_aft * gain[2:3]).astype(bf16)
    g_out = gafter[...].astype(bf16)
    d_fed = jnp.zeros((rows, width), f32)
    for j in range(4):
        cols = slice(width * j, width * (j + 1))
        d_low = (dot(g_out, out_mat(j), 1, 1) * dgelu[:, cols]).astype(bf16)
        bias[:, cols] = jnp.sum(d_low.astype(f32), axis=0, keepdims=True)
        gp[per * j : per * (j + 1), 128:192] = (
            dot(activ[:, cols], g_out, 0, 0).astype(bf16).reshape(per, 64, width)
        )
        gp[:, ROWS * (4 + j) : ROWS * (5 + j)] = (
            dot(fed, d_low, 0, 0).astype(bf16).reshape(groups, ROWS, width)
        )
        d_fed = d_fed + dot(d_low, mat(4 + j), 1, 1)
    sums.core(0)
    d_gain_mlp = jnp.sum(d_fed * flat_aft, axis=0, keepdims=True)
    d_flat = d_fed * gain[2:3]
    g_mid = gafter[...] + unit_aft * (
        d_flat - flat_aft * jnp.mean(d_flat * flat_aft, axis=-1, keepdims=True)
    )
    gafter[...] = g_mid
    g_low = g_mid.astype(bf16)
    gp[:, 3 * ROWS : 4 * ROWS] = (
        dot(context[...], g_low, 0, 0).astype(bf16).reshape(groups, ROWS, width)
    )
    context[...] = dot(g_low, mat(3), 1, 1).astype(bf16)
    sums.diagonal(0)

    def attend_back(b, pair):
        at = pl.ds(pl.multiple_of(b * block, block), block)
        lanes = slice(pair * block, (pair + 1) * block)
        q, k, v, dc = queries[at, lanes], keys[at, lanes], values[at, lanes], context[at, lanes]
        ps = (probs[b, 2 * pair], probs[b, 2 * pair + 1])
        yield
        dps = [dot(half_of(dc, side), v, 1, 1) for side in range(2)]
        dvs = [dot(p.astype(bf16), dc, 0, 0) for p in ps]
        yield
        means = [jnp.sum(dp * p, axis=1, keepdims=True) for dp, p in zip(dps, ps)]
        yield
        lows = [(scale * p * (dp - m)).astype(bf16) for p, dp, m in zip(ps, dps, means)]
        dqs = [dot(low, k) for low in lows]
        dks = [dot(low, q, 0, 0) for low in lows]
        yield
        queries[at, lanes] = jnp.where(low_lane, dqs[0], dqs[1]).astype(bf16)
        keys[at, lanes] = jnp.where(low_lane, dks[0], dks[1]).astype(bf16)
        values[at, lanes] = jnp.where(low_lane, dvs[0], dvs[1]).astype(bf16)

    @pl.loop(0, blocks)
    def _(b):
        lockstep([functools.partial(attend_back, b, pair) for pair in range(pairs)])

    hidden = normed[...]
    d_hid = jnp.zeros((rows, width), f32)
    for m, g in enumerate((queries, keys, values)):
        g_now = g[...]
        gp[:, ROWS * m : ROWS * (m + 1)] = (
            dot(hidden, g_now, 0, 0).astype(bf16).reshape(groups, ROWS, width)
        )
        d_hid = d_hid + dot(g_now, mat(m), 1, 1)
    sums.core(1)
    summ = summary[...]
    unit_sum = unit(summ)
    flat_sum = summ * unit_sum
    d_gain_attn = jnp.sum(d_hid * flat_sum, axis=0, keepdims=True)
    d_flat = d_hid * gain[1:2]
    gsum[...] = (
        gafter[...]
        + unit_sum * (d_flat - flat_sum * jnp.mean(d_flat * flat_sum, axis=-1, keepdims=True))
    ).astype(bf16)
    sums.sides(0)

    acc_w[...] = jnp.zeros_like(acc_w)
    acc_r[...] = jnp.zeros_like(acc_r)

    def closing(c):
        z_m, z_f, g, gr = zm[c], zf[c], ctm[c], gsum[rows_of(c)]
        r_m, r_f, l_m, l_f, d_m, d_f = rm_s[c, 0:1], rf_s[c, 0:1], lw_m[c], lw_f[c], dw_m[c], dw_f[c]
        q_m, q_f, a_m, a_f = lr_m[c], lr_f[c], ar_m[c], ar_f[c]
        lse, mean = stat[c, :, 0:1], stat[c, :, 1:2]
        tab = table[...]
        yield
        x_m, x_f = dot(gr, z_m, 1, 1), dot(gr, z_f, 1, 1)
        w_m, w_f = jnp.exp(l_m - lse), jnp.exp(l_f - lse)
        yield
        b_m, b_f = w_m * (d_m - mean), w_f * (d_f - mean)
        k_m = jnp.sum(b_m * l_m, axis=0, keepdims=True)
        k_f = jnp.sum(b_f * l_f, axis=0, keepdims=True)
        mean_r = jnp.sum(x_m * a_m, axis=1, keepdims=True) + jnp.sum(x_f * a_f, axis=1, keepdims=True)
        yield
        c_m, c_f = a_m * (x_m - mean_r), a_f * (x_f - mean_r)
        k_m = (k_m + jnp.sum(c_m * q_m, axis=0, keepdims=True)) * (r_m * r_m * mean_of)
        k_f = (k_f + jnp.sum(c_f * q_f, axis=0, keepdims=True)) * (r_f * r_f * mean_of)
        left_m = jnp.concatenate([w_m, b_m * r_m, a_m, c_m * r_m], axis=0).astype(bf16)
        left_f = jnp.concatenate([w_f, b_f * r_f, a_f, c_f * r_f], axis=0).astype(bf16)
        yield
        made = dot(left_m, z_m) + dot(left_f, z_f)
        back = jnp.concatenate([g, tab[0:mem], gr, tab[mem:]], axis=0)
        t_m = jnp.broadcast_to(k_m, (8, wide)).T
        t_f = jnp.broadcast_to(k_f, (8, toks)).T
        yield
        dz_m = dot(left_m, back, 0, 0) - z_m.astype(f32) * t_m[:, 0:1]
        dz_f = dot(left_f, back, 0, 0) - z_f.astype(f32) * t_f[:, 0:1]
        yield
        ctm[c] = made[0:mem].astype(bf16)
        acc_w[...] += made[mem : 2 * mem]
        acc_r[...] += made[2 * mem + read :]
        zm[c], zf[c] = dz_m.astype(bf16), dz_f.astype(bf16)
        for copy in out_copies(c):
            copy.start()

    quarter = clips // 4
    clip_loop(0, quarter, 2, closing)
    sums.owners(0)
    sums.diagonal(1)
    clip_loop(quarter, 2 * quarter, 2, closing)
    sums.sides(1)
    clip_loop(2 * quarter, 3 * quarter, 2, closing)
    sums.owners(1)
    clip_loop(3 * quarter, clips, 2, closing)

    zero_rows = jnp.zeros((1, width), f32)
    rest = jnp.concatenate(
        [zero_rows, d_gain_attn, d_gain_mlp, zero_rows, jnp.zeros((12, width), f32)], axis=0
    )
    stacked = jnp.concatenate([acc_w[...], acc_r[...], rest], axis=0)
    gp[:, SMALL:PACK] = jnp.zeros((groups, ROWS, width), bf16)
    gp[:, SMALL:PACK, 0:128] = stacked.T.astype(bf16).reshape(groups, ROWS, 128)
    for d in range(groups):
        gp[d, SMALL : SMALL + 1, 128 : 128 + piece] = bias[:, piece * d : piece * (d + 1)].astype(bf16)
    sums.core(2)
    sums.final(0)
    sums.diagonal(2)
    sums.final(1)
    sums.sides(2)
    sums.owners(2)
    sums.final(2)

    @pl.loop(0, clips)
    def _(c):
        for copy in out_copies(c):
            copy.wait()

    sums.finish()


def step_scratch(clips, toks, mem, read, width):
    vm, sem = pltpu.VMEM, pltpu.SemaphoreType.DMA
    rows, wide = clips * read, mem + read
    return [
        vm((clips, wide, width), bf16),
        vm((clips, toks, width), bf16),
        vm((clips, mem, width), bf16),
        vm((wide, width), bf16),
        vm((8, width), f32),
        vm((1, 4 * width), f32),
        vm((clips, mem, wide), f32),
        vm((clips, mem, toks), f32),
        vm((clips, mem, wide), f32),
        vm((clips, mem, toks), f32),
        vm((clips, read, wide), f32),
        vm((clips, read, toks), f32),
        vm((clips, read, wide), f32),
        vm((clips, read, toks), f32),
        vm((clips, 8, wide), f32),
        vm((clips, 8, toks), f32),
        vm((clips, mem, 8), f32),
        vm((rows, width), f32),
        vm((rows, width), bf16),
        vm((rows, width), bf16),
        vm((rows, width), bf16),
        vm((rows // 128, HEADS, 128, 128), f32),
        vm((rows, width), bf16),
        vm((rows, width), f32),
        vm((rows, width), bf16),
        vm((rows, 4 * width), f32),
        vm((rows, 4 * width), bf16),
        vm((rows, width), f32),
        vm((rows, width), bf16),
        vm((mem, width), f32),
        vm((read, width), f32),
        sem((3, clips)),
        sem((3, clips)),
    ]


STEP_SCRATCH = 33


def plain_kernel(clips, *refs):
    ins, wpack_h, outs, gp = refs[0:5], refs[5], refs[6:10], refs[10]
    wp, tiny, sems = refs[11:14]
    step(load_weights(wpack_h, wp, tiny, sems), NoSums(), clips, ins, outs, refs[14:], wp, tiny, gp)


def whole_kernel(clips, *refs):
    weights, ins, state = refs[0:7], refs[7:12], refs[12:18]
    outs, red, buf = refs[18:22], refs[22], refs[23]
    refs = refs[24:]
    wp, tiny, gp = refs[0:3]
    gather_refs, refs = refs[3:21], refs[21:]
    sum_refs, refs = refs[0:18], refs[18:]
    momentum_refs, refs = refs[0:4], refs[4:]
    gather = gather_weights(weights, wp, tiny, *gather_refs)
    step(gather, Sums(gp, red, *sum_refs), clips, ins, outs, refs, wp, tiny, gp)
    send_momentum(red, *state, momentum_refs[0], buf, *momentum_refs[1:])


def run_step(frames, valid, memory, ct_memory, ct_read, wpack=None, weights=(), state=()):
    clips, toks, width = frames.shape
    mem, read = memory.shape[1], ct_read.shape[1]
    groups, rows = width // ROWS, clips * read
    vm, sem, made = pltpu.VMEM, pltpu.SemaphoreType.DMA, jax.ShapeDtypeStruct
    hbm = pl.BlockSpec(memory_space=pl.ANY)
    inside = pl.BlockSpec(memory_space=pltpu.VMEM)
    out_shape = [
        made(memory.shape, bf16), made((rows, width), bf16), made(frames.shape, bf16), made(memory.shape, bf16),
    ]
    out_specs = [hbm, inside, hbm, hbm]
    in_specs = [hbm, inside, hbm, hbm, inside]
    operands = [frames, valid, memory, ct_memory, ct_read.reshape(rows, width)]
    scratch = [vm((groups, SMALL, width), bf16), vm((groups, ROWS, TINY), bf16)]
    params = dict(vmem_limit_bytes=VMEM_LIMIT)
    if weights:
        n = lax.axis_size("sub")
        kernel = whole_kernel
        operands = [*weights, *operands, *state]
        in_specs = [inside] * len(weights) + in_specs + [inside] * len(state)
        out_shape += [made((PACK, width), f32), made((groups, 64, width), bf16)]
        out_specs += [inside, hbm]
        scratch += [
            vm((groups, PACK, width), bf16),
            vm((SMALL, width), bf16), vm((ROWS, TINY), bf16), sem((groups,)), sem((groups,)), sem((2,)),
            *[sem((n,))] * 6, sem((4, n)), *[sem((n,))] * 5, sem((4, n)),
            vm((4, n, PACK, width), bf16),
            vm((n, 112, width), bf16),
            vm((n, 96, width), bf16),
            vm((n, PACK, width), bf16),
            vm((n, PACK, width), bf16),
            vm((n - 1, PACK, width), bf16),
            *[sem((3, 4))] * 2, *[sem((3, n))] * 8, *[sem((3, n - 1))] * 2,
            vm((PACK, width), bf16), sem((len(OWNERS),)), sem((groups,)), sem,
        ]
        params.update(collective_id=1, has_side_effects=True)
    else:
        kernel = plain_kernel
        operands.append(wpack)
        in_specs.append(hbm)
        out_shape.append(made((groups, PACK, width), bf16))
        out_specs.append(inside)
        scratch.append(sem((2,)))
    outs = pl.pallas_call(
        functools.partial(kernel, clips),
        out_shape=tuple(out_shape),
        in_specs=in_specs,
        out_specs=tuple(out_specs),
        scratch_shapes=scratch + step_scratch(clips, toks, mem, read, width),
        compiler_params=pltpu.CompilerParams(**params),
        name="clip_step",
    )(*operands)
    return (outs[0], outs[1].reshape(ct_read.shape), *outs[2:])


OWNERS = ((2, 0), (4, 3), (2, 3), (4, 0), (0, 1), (6, 2), (0, 3))
PIECES = ((0, 16), (16, 16), (32, 16), (48, 16), (64, 64), (128, 64), (192, 16))


def is_owner(m):
    return (lax.axis_index("dp") == OWNERS[m][0]) & (lax.axis_index("sub") == OWNERS[m][1])


def small_grads(red, gains_t):
    return (
        red[SMALL:PACK, 0:96] * gains_t[:, 3:4],
        red[SMALL:PACK, 96:112] * gains_t[:, 0:1],
    )


def send_momentum(acc, attn_mom, w_in_mom, w_out_mom, s_read_mom, s_write_mom, gains, pk, buf, gsend, grecv, gown):
    width = acc.shape[1]
    count = lax.axis_size("sub")
    me = lax.axis_index("dp") * count + lax.axis_index("sub")
    for m in range(4):
        at = slice(ROWS * m, ROWS * (m + 1))
        pk[at] = (0.5 * attn_mom[m] + acc[at]).astype(bf16)
        at = slice(64 + ROWS * m, 64 + ROWS * (m + 1))
        pk[at] = (0.5 * w_in_mom[:, width * m : width * (m + 1)] + acc[at]).astype(bf16)
    pk[128:192] = (0.5 * w_out_mom[...] + acc[128:192]).astype(bf16)
    g_write, g_read = small_grads(acc, turn_gains(gains[...]))
    pk[SMALL:PACK] = jnp.zeros((ROWS, width), bf16)
    pk[SMALL:PACK, 0:96] = (0.5 * s_write_mom[...] + g_write).astype(bf16)
    pk[SMALL:PACK, 96:112] = (0.5 * s_read_mom[...] + g_read).astype(bf16)

    def piece(m):
        start, size = PIECES[m]
        return pk.at[pl.ds(start, size)], buf.at[me, pl.ds(0, size)]

    def away(m):
        src, dst = piece(m)
        return remote(src, dst, gsend.at[m], grecv.at[me], OWNERS[m])

    def home(m):
        src, dst = piece(m)
        return pltpu.make_async_copy(src, dst, gown)

    many = range(len(OWNERS))
    for m in (4, 5, 0, 1, 2, 3, 6):

        @pl.when(jnp.logical_not(is_owner(m)))
        def _():
            away(m).start()

    for m in many:

        @pl.when(is_owner(m))
        def _():
            home(m).start()

            @pl.loop(0, buf.shape[0])
            def _(d):
                @pl.when(d != me)
                def _():
                    got = buf.at[d, pl.ds(0, PIECES[m][1])]
                    remote(got, got, grecv.at[d], grecv.at[d], OWNERS[m]).wait_recv()

            home(m).wait()

        @pl.when(jnp.logical_not(is_owner(m)))
        def _():
            away(m).wait_send()


def iterate(x, low):
    blocks = x.shape[0]
    total = jnp.zeros((1, 1), f32)
    for j in range(blocks):
        total = total + jnp.sum(x[j] * x[j], keepdims=True)
    scale = 1.0 / (jnp.sqrt(total) + 1e-07)
    for j in range(blocks):
        x[j] = x[j] * scale
        low[j] = x[j].astype(bf16)

    @pl.loop(0, 5)
    def _(_):
        q = dot(low[0], low[0], 1, 1)
        for j in range(1, blocks):
            q = q + dot(low[j], low[j], 1, 1)
        q_low = q.astype(bf16)
        mixed = (NS[1] * q + NS[2] * dot(q_low, q_low)).astype(bf16)
        for j in range(blocks):
            new = NS[0] * x[j] + dot(mixed, low[j])
            x[j] = new
            low[j] = new.astype(bf16)


def exact_dot(a, b, ca=1, cb=0):
    return lax.dot_general(a, b, (((ca,), (cb,)), ((), ())), preferred_element_type=f32, precision=highest)


def iterate_small(x, same):
    norm = jnp.sum(x * x, axis=1, keepdims=True)
    total = jnp.sum(jnp.where(same, norm.T, 0.0), axis=1, keepdims=True)
    x = x * (1.0 / (jnp.sqrt(total) + 1e-07))
    for _ in range(5):
        q = jnp.where(same, exact_dot(x, x, 1, 1), 0.0)
        mixed = NS[1] * q + NS[2] * exact_dot(q, q)
        x = NS[0] * x + exact_dot(mixed, x)
    return x


def muon_kernel(
    red, buf, attn_mom, w_in_mom, w_out_mom, s_read_mom, s_write_mom, s_read, s_write,
    gains, gains_first, gains_second, bias, bias_first, bias_second,
    xo, g_attn, g_in, g_out, g_read, g_write, g_gains, g_bias,
    n_gains, n_bias, m_attn, m_in, m_out, m_read, m_write,
    n_gains_first, n_gains_second, n_bias_first, n_bias_second,
    x, low,
):
    width = red.shape[1]
    groups = buf.shape[0]
    for m in range(4):
        lanes = slice(width * m, width * (m + 1))
        g = red[ROWS * m : ROWS * (m + 1)]
        g_attn[m] = g
        m_attn[m] = 0.5 * attn_mom[m] + g
        g = red[64 + ROWS * m : 64 + ROWS * (m + 1)]
        g_in[:, lanes] = g
        m_in[:, lanes] = 0.5 * w_in_mom[:, lanes] + g
    g = red[128:192]
    g_out[...] = g
    m_out[...] = 0.5 * w_out_mom[...] + g
    gains_t = turn_gains(gains[...])
    made_write, made_read = small_grads(red, gains_t)
    g_write[...] = made_write
    g_read[...] = made_read
    m_write[...] = 0.5 * s_write_mom[...] + made_write
    m_read[...] = 0.5 * s_read_mom[...] + made_read
    low_write = s_write[...].astype(bf16).astype(f32)
    low_read = s_read[...].astype(bf16).astype(f32)
    to_read = jnp.sum(low_read * red[SMALL:PACK, 96:112], axis=1, keepdims=True)
    to_write = jnp.sum(low_write * red[SMALL:PACK, 0:96], axis=1, keepdims=True)
    column = lax.broadcasted_iota(jnp.int32, (ROWS, 128), 1)
    wide = jnp.where(
        column == 112, to_read, jnp.where(column == 115, to_write, red[SMALL:PACK, 0:128])
    )
    grad_gains = wide.T[112:116]
    g_gains[...] = grad_gains
    n_gains[...], n_gains_first[...], n_gains_second[...] = adam_step(
        gains[...], gains_first[...], gains_second[...], grad_gains
    )
    grad_bias = red[SMALL : SMALL + 1, 128:192]
    g_bias[...] = grad_bias
    n_bias[...], n_bias_first[...], n_bias_second[...] = adam_step(
        bias[...], bias_first[...], bias_second[...], grad_bias
    )

    @pl.when(is_owner(0) | is_owner(1) | is_owner(2) | is_owner(3))
    def _():
        x[0] = buf[:, 0:ROWS].reshape(width, width).astype(f32)
        iterate(x.at[0:1], low.at[0:1])
        xo[:, 0:ROWS] = low[0].reshape(groups, ROWS, width)

    @pl.when(is_owner(4))
    def _():
        for j in range(4):
            x[j] = buf[:, ROWS * j : ROWS * (j + 1)].reshape(width, width).astype(f32)
        iterate(x, low)
        for j in range(4):
            xo[:, ROWS * j : ROWS * (j + 1)] = low[j].reshape(groups, ROWS, width)

    @pl.when(is_owner(5))
    def _():
        per = groups // 4
        for j in range(4):
            x[j] = buf[per * j : per * (j + 1)].reshape(width, width).astype(f32).T
        iterate(x, low)
        for j in range(4):
            xo[per * j : per * (j + 1)] = x[j].T.astype(bf16).reshape(per, 64, width)

    @pl.when(is_owner(6))
    def _():
        table = buf[:, 0:ROWS, 0:128].reshape(width, 128).astype(f32).T
        row = lax.broadcasted_iota(jnp.int32, (128, 128), 0)
        col = lax.broadcasted_iota(jnp.int32, (128, 128), 1)
        same = ((row < 96) & (col < 96)) | ((row >= 96) & (col >= 96))
        made = iterate_small(table, same)
        xo[:, 0:ROWS, 0:128] = made.T.astype(bf16).reshape(groups, ROWS, 128)


def spread_kernel(xo, xrec, ssem, rsem, osem):
    count = lax.axis_size("sub")
    me = lax.axis_index("dp") * count + lax.axis_index("sub")
    groups = xo.shape[0]
    many = range(len(OWNERS))
    barrier = pltpu.get_barrier_semaphore()
    for m in many:

        @pl.when(jnp.logical_not(is_owner(m)))
        def _():
            pl.semaphore_signal(barrier, inc=1, device_id=OWNERS[m], device_id_type=MESH)

    for m in many:
        start, size = PIECES[m]

        def target(m=m, start=start, size=size):
            return xrec.at[pl.ds(start, size)]

        def away(d, m=m, size=size):
            return remote(
                xo.at[d, pl.ds(0, size)], target(), ssem.at[d], rsem.at[m], (d // count, lax.rem(d, count))
            )

        @pl.when(is_owner(m))
        def _():
            pl.semaphore_wait(barrier, groups - 1)
            home = pltpu.make_async_copy(xo.at[me, pl.ds(0, size)], target(), osem)
            home.start()

            @pl.loop(0, groups)
            def _(d):
                @pl.when(d != me)
                def _():
                    away(d).start()

            home.wait()

            @pl.loop(0, groups)
            def _(d):
                @pl.when(d != me)
                def _():
                    away(d).wait_send()

    for m in many:
        start, size = PIECES[m]

        @pl.when(jnp.logical_not(is_owner(m)))
        def _():
            got = xrec.at[pl.ds(start, size)]
            remote(got, got, rsem.at[m], rsem.at[m], OWNERS[m]).wait_recv()


def finish_kernel(xrec, attn, w_in, w_out, s_read, s_write, n_attn, n_in, n_out, n_read, n_write):
    width = xrec.shape[1]
    for m in range(4):
        lanes = slice(width * m, width * (m + 1))
        n_attn[m] = attn[m] - xrec[ROWS * m : ROWS * (m + 1)].astype(f32)
        n_in[:, lanes] = w_in[:, lanes] - xrec[64 + ROWS * m : 64 + ROWS * (m + 1)].astype(f32)
    n_out[...] = w_out[...] - 2.0 * xrec[128:192].astype(f32)
    small = xrec[SMALL:PACK, 0:128].astype(f32)
    n_write[...] = s_write[...] - math.sqrt(512 / 96) * small[:, 0:96]
    n_read[...] = s_read[...] - math.sqrt(512 / 16) * small[:, 96:112]


highest = lax.Precision.HIGHEST
NS = (3.4445, -4.775, 2.0315)


def canonical(attn, w_in, w_out, s_read, s_write, gains, bias):
    width = attn.shape[2]
    groups = attn.shape[1] // ROWS
    a = attn.astype(bf16).reshape(4, groups, ROWS, width).transpose(1, 0, 2, 3)
    i = w_in.astype(bf16).reshape(groups, ROWS, 4, width).transpose(0, 2, 1, 3)
    o = w_out.astype(bf16).reshape(groups, 64, width)
    s = jnp.concatenate([s_write, s_read, gains.T], axis=1).astype(bf16)
    s = jnp.pad(s, ((0, 0), (0, 128 - s.shape[1]))).reshape(groups, ROWS, 128)
    b = bias.astype(bf16).reshape(groups, 1, 64)
    b = jnp.pad(b, ((0, 0), (0, ROWS - 1), (0, width - 128 - 64)))
    return jnp.concatenate(
        [
            a.reshape(groups, 64, width),
            i.reshape(groups, 64, width),
            o,
            jnp.concatenate([s, b], axis=2),
        ],
        axis=1,
    )


def natural(pack, mem, read):
    groups, _, width = pack.shape
    a = pack[:, 0:64].reshape(groups, 4, ROWS, width).transpose(1, 0, 2, 3)
    i = pack[:, 64:128].reshape(groups, 4, ROWS, width).transpose(0, 2, 1, 3)
    s = pack[:, SMALL:PACK, 0:128].reshape(groups * ROWS, 128)
    return (
        a.reshape(4, groups * ROWS, width),
        i.reshape(groups * ROWS, 4 * width),
        pack[:, 128:192].reshape(groups * 64, width),
        s[:, 0:mem],
        s[:, mem : mem + read],
        s[:, mem + read + 1 : mem + read + 3],
        pack[:, SMALL, 128:192].reshape(groups * 64),
    )


def adam_step(weight, first, second, grad):
    first_new = 0.5 * first + 0.5 * grad
    second_new = 0.5 * second + 0.5 * grad * grad
    part = 1.0 - 0.5**10
    moved = 0.25 * (first_new / part) / (jnp.sqrt(second_new / part) + 1e-08)
    return weight - moved, first_new, second_new


def orthogonalize(matrix):
    tall = matrix.shape[0] > matrix.shape[1]
    x = matrix.T if tall else matrix
    x = x / (jnp.sqrt(jnp.sum(x * x)) + 1e-07)
    for _ in range(5):
        q = jnp.dot(x, x.T, precision=highest)
        mixed = NS[1] * q + NS[2] * jnp.dot(q, q, precision=highest)
        x = NS[0] * x + jnp.dot(mixed, x, precision=highest)
    return x.T if tall else x


def any_slice(
    frames, valid, memory, ct_memory, ct_read,
    attn, w_in, w_out, s_read, s_write, gains, bias,
    attn_mom, w_in_mom, w_out_mom, s_read_mom, s_write_mom,
    gains_first, gains_second, bias_first, bias_second,
):
    axes = ("dp", "sub")
    mem, read = memory.shape[1], ct_read.shape[1]

    def gather(v, axis):
        return lax.all_gather(v.astype(bf16), axes, axis=axis, tiled=True)

    def scatter(v, axis):
        return lax.psum_scatter(v, axes, scatter_dimension=axis, tiled=True)

    wpack = canonical(
        gather(attn, 1), gather(w_in, 0), gather(w_out, 0), gather(s_read, 0),
        gather(s_write, 0), gather(gains, 1), gather(bias, 0),
    )
    new_memory, read_out, grad_frames, grad_memory, gpack = run_step(
        frames, valid, memory, ct_memory, ct_read, wpack
    )
    sums = natural(gpack.astype(f32), mem, read)
    g_attn, g_in, g_out, sum_w, sum_r, g_two, g_bias = (
        scatter(v, axis) for v, axis in zip(sums, (1, 0, 0, 0, 0, 0, 0))
    )
    low_gain = gains.astype(bf16).astype(f32)
    low_w, low_r = s_write.astype(bf16).astype(f32), s_read.astype(bf16).astype(f32)
    g_s_write = low_gain[3][:, None] * sum_w
    g_s_read = low_gain[0][:, None] * sum_r
    g_gains = jnp.stack(
        [jnp.sum(low_r * sum_r, axis=1), g_two[:, 0], g_two[:, 1], jnp.sum(low_w * sum_w, axis=1)]
    )
    moms = (
        0.5 * attn_mom + g_attn,
        0.5 * w_in_mom + g_in,
        0.5 * w_out_mom + g_out,
        0.5 * s_read_mom + g_s_read,
        0.5 * s_write_mom + g_s_write,
    )
    whole = [gather(v, axis).astype(f32) for v, axis in zip(moms, (1, 0, 0, 0, 0))]
    matrices = [whole[0][m] for m in range(4)] + whole[1:]
    rank, count = lax.axis_index(axes), lax.axis_size(axes)
    owned = [
        lax.cond(rank == m * count // 8, orthogonalize, jnp.zeros_like, matrix)
        for m, matrix in enumerate(matrices)
    ]
    ortho = (
        scatter(jnp.stack(owned[:4]), 1), *(scatter(v, 0) for v in owned[4:])
    )
    stepped = []
    for weight, part, full in zip((attn, w_in, w_out, s_read, s_write), ortho, whole):
        ratio = max(1.0, full.shape[-2] / full.shape[-1]) ** 0.5
        stepped.append(weight - ratio * part)
    n_gains = adam_step(gains, gains_first, gains_second, g_gains)
    n_bias = adam_step(bias, bias_first, bias_second, g_bias)
    return (
        new_memory, read_out, grad_frames, grad_memory,
        g_attn, g_in, g_out, g_s_read, g_s_write, g_gains, g_bias,
        *stepped, n_gains[0], n_bias[0], *moms, n_gains[1], n_gains[2], n_bias[1], n_bias[2],
    )


def this_slice(
    frames, valid, memory, ct_memory, ct_read,
    attn, w_in, w_out, s_read, s_write, gains, bias,
    attn_mom, w_in_mom, w_out_mom, s_read_mom, s_write_mom,
    gains_first, gains_second, bias_first, bias_second,
):
    inside, anywhere = pl.BlockSpec(memory_space=pltpu.VMEM), pl.BlockSpec(memory_space=pl.ANY)

    def like(*arrays):
        return tuple(jax.ShapeDtypeStruct(a.shape, f32) for a in arrays)

    def row(v):
        return v.reshape(1, -1)

    moms = (attn_mom, w_in_mom, w_out_mom, s_read_mom, s_write_mom)
    weights = (attn, w_in, w_out, s_read, s_write)
    new_memory, read_out, grad_frames, grad_memory, red, buf = run_step(
        frames, valid, memory, ct_memory, ct_read, None, (*weights, gains, row(bias)), (*moms, gains)
    )
    biases = (row(bias), row(bias_first), row(bias_second))
    groups, width = buf.shape[0], buf.shape[2]
    made = pl.pallas_call(
        muon_kernel,
        out_shape=(
            jax.ShapeDtypeStruct(buf.shape, bf16),
            *like(*weights, gains, biases[0]),
            *like(gains, biases[0]),
            *like(*moms, gains, gains, biases[0], biases[0]),
        ),
        in_specs=[inside] * 15,
        out_specs=(inside,) * 19 ,
        scratch_shapes=[pltpu.VMEM((4, width, width), f32), pltpu.VMEM((4, width, width), bf16)],
        compiler_params=pltpu.CompilerParams(vmem_limit_bytes=60 * 1024 * 1024),
        name="muon",
    )(red, buf, *moms, s_read, s_write, gains, gains_first, gains_second, *biases)
    xo, grads, (n_gains, n_bias), new_moms, adams = made[0], made[1:8], made[8:10], made[10:15], made[15:]
    sem = pltpu.SemaphoreType.DMA
    xrec = pl.pallas_call(
        spread_kernel,
        out_shape=jax.ShapeDtypeStruct((PACK, width), bf16),
        in_specs=[anywhere],
        out_specs=anywhere,
        scratch_shapes=[sem((groups,)), sem((len(OWNERS),)), sem],
        compiler_params=pltpu.CompilerParams(collective_id=3, has_side_effects=True),
        name="spread_ortho",
    )(xo)
    stepped = pl.pallas_call(
        finish_kernel,
        out_shape=like(*weights),
        in_specs=[inside] * 6,
        out_specs=(inside,) * 5,
        name="finish",
    )(xrec, *weights)
    flat = bias.shape
    return (
        new_memory, read_out, grad_frames, grad_memory,
        *grads[:6], grads[6].reshape(flat),
        *stepped, n_gains, n_bias.reshape(flat), *new_moms,
        adams[0], adams[1], adams[2].reshape(flat), adams[3].reshape(flat),
    )


def solution(mesh):
    both = ("dp", "sub")
    rows3, rows2, rows1 = P(both, None, None), P(both, None), P(both)
    mid, last = P(None, both, None), P(None, both)
    weights = (mid, rows2, rows2, rows2, rows2)
    here = (mesh.shape["dp"], mesh.shape["sub"]) == (8, 4)
    return jax.shard_map(
        this_slice if here else any_slice,
        mesh=mesh,
        in_specs=(
            rows3, rows2, rows3, rows3, rows3, *weights, last, rows1, *weights, last, last, rows1, rows1,
        ),
        out_specs=(
            rows3, rows3, rows3, rows3, *weights, last, rows1, *weights, last, rows1, *weights,
            last, last, rows1, rows1,
        ),
        check_vma=False,
    )
```

```python
import functools
import math

import jax
import jax.numpy as jnp
from jax import lax
from jax.experimental import pallas as pl
from jax.experimental.pallas import tpu as pltpu
from jax.sharding import PartitionSpec as P

f32 = jnp.float32
bf16 = jnp.bfloat16
MESH = pl.DeviceIdType.MESH

HEADS = 8
HEAD_DIM = 64
NORM_EPS = 1e-06
MASKED = -1000000000.0
GELU_A = math.sqrt(2.0 / math.pi)
GELU_B = 0.044715
VMEM_LIMIT = 60 * 1024 * 1024

ROWS = 16
PACK = 208
SMALL = 192
TINY = 256
X, Y, CORE = 2, 4, 1
PARTS = ((64, 64, 64, 0), (0, 32, 32, 64))


def dot(a, b, ca=1, cb=0):
    return lax.dot_general(a, b, (((ca,), (cb,)), ((), ())), preferred_element_type=f32)


def remote(src, dst, send, recv, device):
    return pltpu.make_async_remote_copy(
        src_ref=src, dst_ref=dst, send_sem=send, recv_sem=recv, device_id=device, device_id_type=MESH
    )


def lockstep(bodies):
    done = object()
    running = [body() for body in bodies]
    while running:
        running = [body for body in running if next(body, done) is not done]


def turn_gains(g):
    eye = (
        lax.broadcasted_iota(jnp.int32, (4, 4), 0) == lax.broadcasted_iota(jnp.int32, (4, 4), 1)
    ).astype(bf16)
    return dot(g.astype(bf16), eye, 0, 0)


def gather_weights(weights, out, tiny, x_ref, x_tiny, tsend, trecv, own_sem, up, down, sx, sy, fx, fy, sc, rz, rx, ry, rdx, rdy, rc):
    attn, w_in, w_out, s_read, s_write, gains, bias = weights
    dp, p = lax.axis_index("dp"), lax.axis_index("sub")
    count = lax.axis_size("sub")
    last = count - 1
    me = dp * count + p
    total = out.shape[0]
    size = x_ref.shape[0]
    cut = size // 2
    width = x_ref.shape[1]

    def device(d):
        return (d // count, lax.rem(d, count))

    def flip(mask):
        return (jnp.bitwise_xor(dp, mask), p)

    def unit(mask, s):
        return out.at[jnp.bitwise_xor(dp, mask) * count + s]

    def others(act):
        @pl.loop(0, total)
        def _(d):
            @pl.when(d != me)
            def _():
                act(d)

    barrier = pltpu.get_barrier_semaphore()
    others(lambda d: pl.semaphore_signal(barrier, inc=1, device_id=device(d), device_id_type=MESH))
    x_tiny[...] = jnp.zeros((ROWS, TINY), bf16)
    x_tiny[:, 0:96] = s_write[...].astype(bf16)
    x_tiny[:, 96:112] = s_read[...].astype(bf16)
    x_tiny[:, 112:116] = turn_gains(gains[...]).astype(bf16)
    x_tiny[0:1, 128:192] = bias[...].astype(bf16)
    for m in range(4):
        x_ref[ROWS * m : ROWS * (m + 1)] = attn[m].astype(bf16)
        x_ref[64 + ROWS * m : 64 + ROWS * (m + 1)] = w_in[:, width * m : width * (m + 1)].astype(bf16)
    x_ref[128:192] = w_out[...].astype(bf16)
    own = pltpu.make_async_copy(x_ref, unit(0, p), own_sem.at[0])
    own_tiny = pltpu.make_async_copy(x_tiny, tiny.at[me], own_sem.at[1])
    own.start()
    own_tiny.start()
    pl.semaphore_wait(barrier, total - 1)

    def tiny_copy(d, place):
        return remote(x_tiny, tiny.at[place], tsend.at[d], trecv.at[place], device(d))

    def chain(step, way, s, src):
        sems = up if way > 0 else down
        return remote(src, unit(0, s), sems.at[step], rz.at[s], (dp, p + way))

    def side(mask, s, src):
        send, recv = (sx, rx) if mask == X else (sy, ry)
        return remote(src, unit(0, s), send.at[s], recv.at[s], flip(mask))

    def halves(mask, s):
        other = Y if mask == X else X
        part = pl.ds(0, cut) if mask == X else pl.ds(cut, size - cut)
        send, recv = (fy, rdy) if mask == X else (fx, rdx)
        ref = unit(mask, s).at[part]
        return remote(ref, ref, send.at[s], recv.at[s], flip(other))

    def cross(kind, s, src):
        return remote(src, unit((0, X, Y, X + Y)[kind], s), sc.at[kind, s], rc.at[kind, s], flip(CORE))

    def share(s, src):
        side(X, s, src).start()
        side(Y, s, src).start()
        cross(0, s, src).start()

    others(lambda d: tiny_copy(d, me).start())

    @pl.when(p < last)
    def _():
        chain(0, 1, p, x_ref).start()

    @pl.when(p > 0)
    def _():
        chain(0, -1, p, x_ref).start()

    share(p, x_ref)

    def arrived(s):
        for mask, kind in ((X, 1), (Y, 2)):
            recv = rx if mask == X else ry
            got = unit(mask, s)
            remote(got, got, recv.at[s], recv.at[s], flip(mask)).wait_recv()
            halves(mask, s).start()
            cross(kind, s, got).start()

    def arrivals(k):
        if k == 0:
            arrived(p)
            return

        @pl.when(p >= k)
        def _():
            arrived(p - k)

        @pl.when(p + k <= last)
        def _():
            arrived(p + k)

    yield
    for k in range(1, count):
        for way in (1, -1):

            @pl.when(p >= k if way > 0 else p + k <= last)
            def _():
                s = p - k * way
                got = unit(0, s)
                remote(got, got, rz.at[s], rz.at[s], (dp, p)).wait_recv()
                if k < last:

                    @pl.when(p < last if way > 0 else p > 0)
                    def _():
                        chain(k, way, s, got).start()

                share(s, got)

        arrivals(k - 1)
        if k == 1:
            others(lambda d: tiny_copy(d, d).wait_recv())
            own_tiny.wait()
        yield
    arrivals(count - 1)
    yield
    for s in range(count):
        for recv, part in ((rdy, pl.ds(0, cut)), (rdx, pl.ds(cut, size - cut))):
            got = unit(X + Y, s).at[part]
            remote(got, got, recv.at[s], recv.at[s], flip(X)).wait_recv()
        cross(3, s, unit(X + Y, s)).start()
    for s in range(count):
        for kind in range(4):
            got = unit((CORE, X + CORE, Y + CORE, X + Y + CORE)[kind], s)
            remote(got, got, rc.at[kind, s], rc.at[kind, s], flip(CORE)).wait_recv()
    own.wait()
    others(lambda d: tiny_copy(d, me).wait_send())
    for s in range(count):
        for mask in (X, Y):
            side(mask, s, unit(0, s)).wait_send()
            halves(mask, s).wait_send()
        for kind in range(4):
            cross(kind, s, unit((0, X, Y, X + Y)[kind], s)).wait_send()
    for k in range(last):

        @pl.when((p < last) & (p >= k))
        def _():
            chain(k, 1, p - k, unit(0, p - k)).wait_send()

        @pl.when((p > 0) & (p + k <= last))
        def _():
            chain(k, -1, p + k, unit(0, p + k)).wait_send()


def load_weights(wpack_h, out, tiny, sems):
    big = pltpu.make_async_copy(wpack_h.at[:, pl.ds(0, SMALL)], out, sems.at[0])
    little = pltpu.make_async_copy(wpack_h.at[:, pl.ds(SMALL, ROWS), pl.ds(0, TINY)], tiny, sems.at[1])
    big.start()
    little.start()
    yield
    little.wait()
    yield
    yield
    yield
    yield
    big.wait()


class Sums:
    def __init__(self, momentum, gp, out, rc, ra, rb, rx, ry, rz, tin, cs, cr, as_, ar, bs, br, xs, xr, ys, yr, zs, zr, ts, tr):
        self.__dict__.update(
            momentum=momentum, gp=gp, out=out, rc=rc, ra=ra, rb=rb, rx=rx, ry=ry, rz=rz, tin=tin,
            c=(cs, cr), a=(as_, ar), b=(bs, br), x=(xs, xr), y=(ys, yr), z=(zs, zr), t=(ts, tr),
        )
        self.dp, self.p = lax.axis_index("dp"), lax.axis_index("sub")
        self.count = lax.axis_size("sub")
        self.order = [lax.rem(self.p + off, self.count) for off in (2, 1, 3, 0)]
        self.sent = []

    def flip(self, mask):
        return (jnp.bitwise_xor(self.dp, mask), self.p)

    def place(self, mask, s):
        return jnp.bitwise_xor(self.dp, mask) * self.count + s

    def push(self, pair, index, src, dst, device):
        copy = remote(src, dst, pair[0].at[index], pair[1].at[index], device)
        copy.start()
        self.sent.append(copy)

    def take(self, pair, index, ref):
        remote(ref, ref, pair[0].at[index], pair[1].at[index], (self.dp, self.p)).wait_recv()

    def core(self, g):
        start, n1, n2, _ = PARTS[g]
        rows = pl.ds(start, n1 + n2)
        for k in (3, 1, 2, 0):
            src = self.gp.at[pl.ds(self.place((0, X, Y, X + Y)[k] + CORE, 0), self.count), rows]
            self.push(self.c, (g, k), src, self.rc.at[k, :, rows], self.flip(CORE))

    def ready(self, g, k):
        start, n1, n2, _ = PARTS[g]
        self.take(self.c, (g, k), self.rc.at[k, :, pl.ds(start, n1 + n2)])

    def total(self, k, s, start, size):
        at = slice(start, start + size)
        own = self.gp[self.place((0, X, Y, X + Y)[k], s), at]
        return own.astype(f32) + self.rc[k, s, at].astype(f32)

    def diagonal(self, g):
        start, n1, n2, half = PARTS[g]
        self.ready(g, 3)
        for s in self.order:
            d = self.place(X + Y, s)
            self.gp[d, start : start + n1 + n2] = self.total(3, s, start, n1 + n2).astype(bf16)
            self.push(
                self.a, (g, s), self.gp.at[d, pl.ds(start, n1)], self.ra.at[s, pl.ds(half, n1)], self.flip(X)
            )
            if n2:
                self.push(
                    self.b, (g, s), self.gp.at[d, pl.ds(start + n1, n2)], self.rb.at[s, pl.ds(half, n2)], self.flip(Y)
                )

    def sides(self, g):
        start, n1, n2, half = PARTS[g]
        rows = pl.ds(start, n1 + n2)
        self.ready(g, 1)
        self.ready(g, 2)
        for s in self.order:
            d = self.place(X, s)
            self.gp[d, start : start + n1] = self.total(1, s, start, n1).astype(bf16)
            if n2:
                self.take(self.b, (g, s), self.rb.at[s, pl.ds(half, n2)])
                more = self.rb[s, half : half + n2].astype(f32)
                self.gp[d, start + n1 : start + n1 + n2] = (self.total(1, s, start + n1, n2) + more).astype(bf16)
            self.push(self.x, (g, s), self.gp.at[d, rows], self.rx.at[s, rows], self.flip(X))
            d = self.place(Y, s)
            if n2:
                self.gp[d, start + n1 : start + n1 + n2] = self.total(2, s, start + n1, n2).astype(bf16)
            self.take(self.a, (g, s), self.ra.at[s, pl.ds(half, n1)])
            more = self.ra[s, half : half + n1].astype(f32)
            self.gp[d, start : start + n1] = (self.total(2, s, start, n1) + more).astype(bf16)
            self.push(self.y, (g, s), self.gp.at[d, rows], self.ry.at[s, rows], self.flip(Y))

    def owners(self, g):
        start, n1, n2, _ = PARTS[g]
        size = n1 + n2
        rows = pl.ds(start, size)
        at = slice(start, start + size)
        self.ready(g, 0)
        for i, s in enumerate(self.order):
            self.take(self.x, (g, s), self.rx.at[s, rows])
            self.take(self.y, (g, s), self.ry.at[s, rows])
            mine = self.total(0, s, start, size) + self.rx[s, at].astype(f32) + self.ry[s, at].astype(f32)
            if i < self.count - 1:
                d = self.place(0, s)
                self.gp[d, at] = mine.astype(bf16)
                self.push(self.z, (g, i), self.gp.at[d, rows], self.rz.at[i, rows], (self.dp, s))
            else:
                self.out[at] = mine

    def final(self, g):
        start, n1, n2, _ = PARTS[g]
        size = n1 + n2
        at = slice(start, start + size)
        mine = self.out[at]
        for i in range(self.count - 1):
            self.take(self.z, (g, i), self.rz.at[i, pl.ds(start, size)])
            mine = mine + self.rz[i, at].astype(f32)
        self.out[at] = mine
        self.momentum.send(g)

    def small_core(self):
        rows, lanes = pl.ds(SMALL, ROWS), pl.ds(0, TINY)
        for k in (3, 1, 2, 0):
            src = self.gp.at[pl.ds(self.place((0, X, Y, X + Y)[k] + CORE, 0), self.count), rows, lanes]
            self.push(self.c, (2, k), src, self.rc.at[k, :, rows, lanes], self.flip(CORE))

    def small_send(self):
        for k in (3, 1, 2, 0):
            mask = (0, X, Y, X + Y)[k]
            self.take(self.c, (2, k), self.rc.at[k, :, pl.ds(SMALL, ROWS), pl.ds(0, TINY)])
            for i, s in enumerate(self.order):
                d = self.place(mask, s)
                own = self.gp[d, SMALL:PACK, 0:TINY].astype(f32)
                made = own + self.rc[k, s, SMALL:PACK, 0:TINY].astype(f32)
                if k == 0 and i == self.count - 1:
                    self.out[SMALL:PACK, 0:TINY] = made
                else:
                    self.gp[d, SMALL:PACK, 0:TINY] = made.astype(bf16)
                    src = self.gp.at[d, pl.ds(SMALL, ROWS), pl.ds(0, TINY)]
                    copy = remote(
                        src, self.tin.at[k, self.p], self.t[0].at[k, s], self.t[1].at[k, self.p],
                        (jnp.bitwise_xor(self.dp, mask), s),
                    )
                    copy.start()
                    self.sent.append(copy)

    def small_final(self):
        mine = self.out[SMALL:PACK, 0:TINY]
        for k in range(4):
            for i, s in enumerate(self.order):
                if not (k == 0 and i == self.count - 1):
                    self.take(self.t, (k, s), self.tin.at[k, s])
                    mine = mine + self.tin[k, s].astype(f32)
        self.out[SMALL:PACK, 0:TINY] = mine
        self.out[SMALL:PACK, TINY:] = jnp.zeros((ROWS, self.out.shape[1] - TINY), f32)
        self.momentum.send(2)

    def early(self):
        self.momentum.early()

    def finish(self):
        for copy in self.sent:
            copy.wait_send()


class NoSums:
    def __init__(self):
        self.core = self.diagonal = self.sides = self.owners = self.final = lambda g: None
        self.finish = self.small_core = self.small_send = self.small_final = self.early = lambda: None


def step(gather, sums, clips, ins, outs, scratch, wp, tiny, gp):
    frames_h, valid_ref, memory_h, ctm_h, ctr_ref = ins
    nm_h, ro_ref, gf_h, gm_h = outs
    (
        zm, zf, ctm, table, gain, bias, lw_m, lw_f, dw_m, dw_f, lr_m, lr_f, ar_m, ar_f, rm_s, rf_s, stat,
        summary, queries, keys, values, probs, context, after, normed, normed_mlp, spare, activ, gafter, d_fed_s, gsum,
        acc_w, acc_r, joined, raw, in_sem, out_sem, raw_sem,
    ) = scratch
    mem, read = memory_h.shape[1], ROWS
    toks = zf.shape[1]
    rows = clips * read
    groups = wp.shape[0]
    width = zm.shape[2]
    wide = mem + read
    mean_of = 1.0 / width

    def in_copies(c):
        return (
            pltpu.make_async_copy(memory_h.at[c], zm.at[c], in_sem.at[0, c]),
            pltpu.make_async_copy(ctm_h.at[c], ctm.at[c], in_sem.at[1, c]),
        )

    def out_copies(c):
        return (
            pltpu.make_async_copy(ctm.at[c], nm_h.at[c], out_sem.at[0, c]),
            pltpu.make_async_copy(zm.at[c], gm_h.at[c], out_sem.at[1, c]),
        )

    chunk = raw.shape[1] // clips
    chunks = [(t, min(chunk, toks - t)) for t in range(0, toks, chunk)]
    tiles = width // 128

    def raw_copy(i, out=False):
        t, n = chunks[i]
        here, there = raw.at[i % 2, pl.ds(0, n * clips)], pl.ds(t * clips, n * clips)
        if out:
            return pltpu.make_async_copy(here, gf_h.at[there], raw_sem.at[i])
        return pltpu.make_async_copy(frames_h.at[there], here, raw_sem.at[i])

    for i in range(min(2, len(chunks))):
        raw_copy(i).start()

    @pl.loop(0, clips)
    def _(c):
        for copy in in_copies(c):
            copy.start()

    def frames_in():
        for i, (t, n) in enumerate(chunks):
            raw_copy(i).wait()
            for q in range(tiles):
                spare[q, 0 : n * clips] = raw[i % 2, 0 : n * clips, 128 * q : 128 * (q + 1)].astype(f32)
            if i + 2 < len(chunks):
                raw_copy(i + 2).start()

            @pl.loop(0, clips)
            def _(c):
                for q in range(tiles):
                    zf[c, t : t + n, 128 * q : 128 * (q + 1)] = spare[
                        q, pl.ds(c, n, stride=clips)
                    ].astype(bf16)

    def frames_out():
        for i, (t, n) in enumerate(chunks):
            @pl.loop(0, clips)
            def _(c):
                for q in range(tiles):
                    spare[q, pl.ds(c, n, stride=clips)] = zf[
                        c, t : t + n, 128 * q : 128 * (q + 1)
                    ].astype(f32)

            if i >= 2:
                raw_copy(i - 2, True).wait()
            for q in range(tiles):
                raw[i % 2, 0 : n * clips, 128 * q : 128 * (q + 1)] = spare[q, 0 : n * clips].astype(bf16)
            raw_copy(i, True).start()

    def clip_loop(low, high, batch, body):
        @pl.loop(low // batch, high // batch)
        def _(i):
            lockstep([functools.partial(body, i * batch + k) for k in range(batch)])

    ones = jnp.ones((8, 128), bf16)
    place = lax.broadcasted_iota(jnp.int32, (mem, 8), 1)

    def unit_rows(z):
        square = z * z
        folded = (square[:, 0:128] + square[:, 128:256]) + (square[:, 256:384] + square[:, 384:512])
        return lax.rsqrt(dot(ones, folded, 1, 1) * mean_of + NORM_EPS)

    def rows_of(c):
        return pl.ds(pl.multiple_of(c * read, read), read)

    def ahead(c):
        for copy in in_copies(c):
            copy.wait()
        z_m, z_f, g = zm[c], zf[c], ctm[c]
        yield
        r_m, r_f = unit_rows(z_m), unit_rows(z_f)
        yield
        d_m, d_f = dot(g, z_m, 1, 1), dot(g, z_f, 1, 1)
        yield
        rm_s[c], rf_s[c] = r_m, r_f
        dw_m[c], dw_f[c] = d_m.astype(bf16), d_f.astype(bf16)

    def reading(c):
        z_m, z_f, r_m, r_f = zm[c], zf[c], rm_s[c], rf_s[c]
        d_m, d_f = dw_m[c].astype(f32), dw_f[c].astype(f32)
        live = valid_ref[pl.ds(c, 1), :] > 0
        tab = table[...]
        yield
        u_m, u_f = dot(tab, z_m, 1, 1), dot(tab, z_f, 1, 1)
        yield
        l_m = u_m * r_m[0:1]
        l_f = jnp.where(live, u_f * r_f[0:1], MASKED)
        top = jnp.maximum(jnp.max(l_m, axis=1, keepdims=True), jnp.max(l_f, axis=1, keepdims=True))
        yield
        e_m, e_f = jnp.exp(l_m - top), jnp.exp(l_f - top)
        total = jnp.sum(e_m, axis=1, keepdims=True) + jnp.sum(e_f, axis=1, keepdims=True)
        inv = 1.0 / total[mem:]
        a_m, a_f = e_m[mem:] * inv, e_f[mem:] * inv
        yield
        a_m, a_f = a_m.astype(bf16), a_f.astype(bf16)
        made = dot(a_m, z_m) + dot(a_f, z_f)
        moved = jnp.sum(e_m[0:mem] * d_m, axis=1, keepdims=True) + jnp.sum(
            e_f[0:mem] * d_f, axis=1, keepdims=True
        )
        yield
        lw_m[c], lw_f[c] = l_m[0:mem], l_f[0:mem]
        lr_m[c], lr_f[c] = l_m[mem:].astype(bf16), l_f[mem:].astype(bf16)
        ar_m[c], ar_f[c] = a_m, a_f
        stat[c] = jnp.where(
            place == 0, top[0:mem], jnp.where(place == 1, total[0:mem], moved)
        ).T
        summary[rows_of(c)] = made

    half = clips // 2
    third = clips // 3
    next(gather)
    frames_in()
    clip_loop(0, half, 2, ahead)
    next(gather)
    turned = tiny[:, :, 0:128].reshape(groups * ROWS, 128).astype(f32).T
    gain[...] = turned[112:120]
    table[0:mem] = (turned[0:mem] * turned[115:116]).astype(bf16)
    table[mem:wide] = (turned[mem:wide] * turned[112:113]).astype(bf16)
    piece = bias.shape[1] // groups
    for d in range(groups):
        bias[:, piece * d : piece * (d + 1)] = tiny[d, 0:1, 128 : 128 + piece].astype(f32)
    clip_loop(half, clips, 2, ahead)
    next(gather)
    clip_loop(0, third, 2, reading)
    next(gather)
    clip_loop(third, 2 * third, 2, reading)
    next(gather)
    clip_loop(2 * third, clips, 2, reading)
    for _ in gather:
        pass

    def mat(m):
        return wp[:, ROWS * m : ROWS * (m + 1)].reshape(groups * ROWS, width)

    per = groups // 4

    def out_mat(j):
        return wp[pl.ds(per * j, per), 128:192].reshape(width, width)

    def unit(v):
        return lax.rsqrt(jnp.mean(v * v, axis=-1, keepdims=True) + NORM_EPS)

    summ = summary[...]
    hidden = (summ * unit(summ) * gain[1:2]).astype(bf16)
    normed[...] = hidden
    queries[...] = dot(hidden, mat(0)).astype(bf16)
    keys[...] = dot(hidden, mat(1)).astype(bf16)
    values[...] = dot(hidden, mat(2)).astype(bf16)
    scale = HEAD_DIM**-0.5
    block = 128
    blocks = rows // block
    pairs = HEADS // 2
    row_clip = lax.broadcasted_iota(jnp.int32, (block, block), 0) // read
    col_clip = lax.broadcasted_iota(jnp.int32, (block, block), 1) // read
    same = row_clip == col_clip
    low_lane = lax.broadcasted_iota(jnp.int32, (block, block), 1) < HEAD_DIM

    def half_of(v, side):
        zero = jnp.zeros_like(v)
        return jnp.where(low_lane, v, zero) if side == 0 else jnp.where(low_lane, zero, v)

    def attend(b, pair):
        at = pl.ds(pl.multiple_of(b * block, block), block)
        lanes = slice(pair * block, (pair + 1) * block)
        q, k, v = queries[at, lanes], keys[at, lanes], values[at, lanes]
        yield
        scores = [dot(half_of(q, side), k, 1, 1) for side in range(2)]
        yield
        masked = [jnp.where(same, s * scale, MASKED) for s in scores]
        tops = [jnp.max(s, axis=1, keepdims=True) for s in masked]
        yield
        parts = [jnp.exp(s - top) for s, top in zip(masked, tops)]
        sums_ = [jnp.sum(e, axis=1, keepdims=True) for e in parts]
        yield
        made = [(e * (1.0 / s)).astype(bf16) for e, s in zip(parts, sums_)]
        got = [dot(p, v) for p in made]
        yield
        probs[b, 2 * pair], probs[b, 2 * pair + 1] = made
        context[at, lanes] = jnp.where(low_lane, got[0], got[1]).astype(bf16)

    @pl.loop(0, blocks)
    def _(b):
        lockstep([functools.partial(attend, b, pair) for pair in range(pairs)])

    aft = summary[...] + dot(context[...], mat(3))
    after[...] = aft
    fed = (aft * unit(aft) * gain[2:3]).astype(bf16)
    def columns(j):
        return pl.ds(pl.multiple_of(width * j, width), width)

    def rows_at(j):
        return pl.ds(pl.multiple_of(rows * j, rows), rows)

    def in_mat(j):
        return wp[:, pl.ds(pl.multiple_of(64 + ROWS * j, ROWS), ROWS)].reshape(groups * ROWS, width)

    normed_mlp[...] = fed
    gafter[...] = jnp.zeros_like(gafter)

    @pl.loop(0, 4)
    def _(j):
        pre = dot(normed_mlp[...], in_mat(j)) + bias[:, columns(j)]
        square = pre * pre
        t = jnp.tanh(GELU_A * pre * (1.0 + GELU_B * square))
        most = 0.5 + 0.5 * t
        act = (pre * most).astype(bf16)
        activ[0:rows, columns(j)] = act
        slope = most + (0.5 * GELU_A) * pre * (1.0 - t * t) * (1.0 + (3.0 * GELU_B) * square)
        for q in range(tiles):
            spare[q, rows_at(j)] = slope[:, 128 * q : 128 * (q + 1)]
        gafter[...] = gafter[...] + dot(act, out_mat(j))

    out = after[...] + gafter[...]
    ro_ref[...] = out.astype(bf16)

    many = block // read

    def joining(b):
        at = slice(block * b, block * (b + 1))
        ro, ctr = ro_ref[at], ctr_ref[at].astype(f32)
        gs = [ctm[many * b + i] for i in range(many)]
        now = stat[many * b : many * (b + 1)]
        tab = table[0:mem]
        yield
        ro_f = ro.astype(f32)
        r = unit(ro_f)
        l = dot(ro, tab, 1, 1) * r
        d = jnp.concatenate(
            [dot(ro[read * i : read * (i + 1)], g, 1, 1) for i, g in enumerate(gs)], axis=0
        )
        yield
        l_c, d_c = l.reshape(many, read, mem), d.reshape(many, read, mem)
        top, total, moved = now[:, 0:1], now[:, 1:2], now[:, 2:3]
        new_top = jnp.maximum(top, jnp.max(l_c, axis=1, keepdims=True))
        old, e = jnp.exp(top - new_top), jnp.exp(l_c - new_top)
        total = total * old + jnp.sum(e, axis=1, keepdims=True)
        moved = moved * old + jnp.sum(e * d_c, axis=1, keepdims=True)
        inv = 1.0 / total
        a, mean = e * inv, moved * inv
        b_all = (a * (d_c - mean)).reshape(block, mem)
        k = jnp.sum(b_all * l, axis=1, keepdims=True) * (r * r * mean_of)
        a_low = a.reshape(block, mem).astype(bf16)
        h_low = (b_all * r).astype(bf16)
        yield
        made = dot(h_low, tab) + jnp.concatenate(
            [dot(a_low[read * i : read * (i + 1)], g) for i, g in enumerate(gs)], axis=0
        )
        yield
        gafter[at] = made - ro_f * k + ctr
        joined[at, 0:mem], joined[at, 128 : 128 + mem] = a_low, h_low
        stat[many * b : many * (b + 1), 0:1] = new_top + jnp.log(total)
        stat[many * b : many * (b + 1), 1:2] = mean

    lockstep([functools.partial(joining, b) for b in range(blocks)])

    gsum[...] = gafter[...].astype(bf16)
    d_fed_s[...] = jnp.zeros_like(d_fed_s)

    @pl.loop(0, 4)
    def _(j):
        g_out, fed = gsum[...], normed_mlp[...]
        slope = jnp.concatenate([spare[q, rows_at(j)] for q in range(tiles)], axis=1)
        d_low = (dot(g_out, out_mat(j), 1, 1) * slope).astype(bf16)
        bias[:, columns(j)] = jnp.sum(d_low.astype(f32), axis=0, keepdims=True)
        gp[pl.ds(per * j, per), 128:192] = (
            dot(activ[0:rows, columns(j)], g_out, 0, 0).astype(bf16).reshape(per, 64, width)
        )
        gp[:, pl.ds(pl.multiple_of(64 + ROWS * j, ROWS), ROWS)] = (
            dot(fed, d_low, 0, 0).astype(bf16).reshape(groups, ROWS, width)
        )
        d_fed_s[...] += dot(d_low, in_mat(j), 1, 1)

    sums.core(0)
    aft = after[...]
    unit_aft = unit(aft)
    flat_aft = aft * unit_aft
    d_fed = d_fed_s[...]
    d_gain_mlp = jnp.sum(d_fed * flat_aft, axis=0, keepdims=True)
    d_flat = d_fed * gain[2:3]
    g_mid = gafter[...] + unit_aft * (
        d_flat - flat_aft * jnp.mean(d_flat * flat_aft, axis=-1, keepdims=True)
    )
    gafter[...] = g_mid
    g_low = g_mid.astype(bf16)
    gp[:, 3 * ROWS : 4 * ROWS] = (
        dot(context[...], g_low, 0, 0).astype(bf16).reshape(groups, ROWS, width)
    )
    context[...] = dot(g_low, mat(3), 1, 1).astype(bf16)
    sums.diagonal(0)

    def attend_back(b, pair):
        at = pl.ds(pl.multiple_of(b * block, block), block)
        lanes = slice(pair * block, (pair + 1) * block)
        q, k, v, dc = queries[at, lanes], keys[at, lanes], values[at, lanes], context[at, lanes]
        lows = (probs[b, 2 * pair], probs[b, 2 * pair + 1])
        ps = [p.astype(f32) for p in lows]
        yield
        dps = [dot(half_of(dc, side), v, 1, 1) for side in range(2)]
        dvs = [dot(p, dc, 0, 0) for p in lows]
        yield
        means = [jnp.sum(dp * p, axis=1, keepdims=True) for dp, p in zip(dps, ps)]
        yield
        lows = [(scale * p * (dp - m)).astype(bf16) for p, dp, m in zip(ps, dps, means)]
        dqs = [dot(low, k) for low in lows]
        dks = [dot(low, q, 0, 0) for low in lows]
        yield
        queries[at, lanes] = jnp.where(low_lane, dqs[0], dqs[1]).astype(bf16)
        keys[at, lanes] = jnp.where(low_lane, dks[0], dks[1]).astype(bf16)
        values[at, lanes] = jnp.where(low_lane, dvs[0], dvs[1]).astype(bf16)

    @pl.loop(0, blocks)
    def _(b):
        lockstep([functools.partial(attend_back, b, pair) for pair in range(pairs)])

    hidden = normed[...]
    d_hid = jnp.zeros((rows, width), f32)
    for m, g in enumerate((queries, keys, values)):
        g_now = g[...]
        gp[:, ROWS * m : ROWS * (m + 1)] = (
            dot(hidden, g_now, 0, 0).astype(bf16).reshape(groups, ROWS, width)
        )
        d_hid = d_hid + dot(g_now, mat(m), 1, 1)
    sums.core(1)
    summ = summary[...]
    unit_sum = unit(summ)
    flat_sum = summ * unit_sum
    d_gain_attn = jnp.sum(d_hid * flat_sum, axis=0, keepdims=True)
    d_flat = d_hid * gain[1:2]
    gsum[...] = (
        gafter[...]
        + unit_sum * (d_flat - flat_sum * jnp.mean(d_flat * flat_sum, axis=-1, keepdims=True))
    ).astype(bf16)
    sums.sides(0)
    sums.diagonal(1)

    acc_w[...] = jnp.zeros_like(acc_w)
    acc_r[...] = jnp.zeros_like(acc_r)

    def closing(c):
        z_m, z_f, g, gr = zm[c], zf[c], ctm[c], gsum[rows_of(c)]
        ro, pair = ro_ref[rows_of(c)], joined[rows_of(c)]
        r_m, r_f, l_m, l_f = rm_s[c, 0:1], rf_s[c, 0:1], lw_m[c], lw_f[c]
        d_m, d_f = dw_m[c].astype(f32), dw_f[c].astype(f32)
        q_m, q_f, a_m, a_f = (v[c].astype(f32) for v in (lr_m, lr_f, ar_m, ar_f))
        now = stat[c].T
        lse, mean = now[:, 0:1], now[:, 1:2]
        tab = table[...]
        yield
        x_m, x_f = dot(gr, z_m, 1, 1), dot(gr, z_f, 1, 1)
        w_m, w_f = jnp.exp(l_m - lse), jnp.exp(l_f - lse)
        yield
        b_m, b_f = w_m * (d_m - mean), w_f * (d_f - mean)
        k_m = jnp.sum(b_m * l_m, axis=0, keepdims=True)
        k_f = jnp.sum(b_f * l_f, axis=0, keepdims=True)
        mean_r = jnp.sum(x_m * a_m, axis=1, keepdims=True) + jnp.sum(x_f * a_f, axis=1, keepdims=True)
        yield
        c_m, c_f = a_m * (x_m - mean_r), a_f * (x_f - mean_r)
        k_m = (k_m + jnp.sum(c_m * q_m, axis=0, keepdims=True)) * (r_m * r_m * mean_of)
        k_f = (k_f + jnp.sum(c_f * q_f, axis=0, keepdims=True)) * (r_f * r_f * mean_of)
        left_m = jnp.concatenate([w_m, b_m * r_m, a_m, c_m * r_m], axis=0).astype(bf16)
        left_f = jnp.concatenate([w_f, b_f * r_f, a_f, c_f * r_f], axis=0).astype(bf16)
        yield
        made = dot(left_m, z_m) + dot(left_f, z_f)
        joins = (dot(pair[:, 0:mem], ro, 0, 0), dot(pair[:, 128 : 128 + mem], ro, 0, 0))
        back = jnp.concatenate([g, tab[0:mem], gr, tab[mem:]], axis=0)
        t_m = jnp.broadcast_to(k_m, (8, mem)).T
        t_f = jnp.broadcast_to(k_f, (8, toks)).T
        yield
        dz_m = dot(left_m, back, 0, 0) - z_m.astype(f32) * t_m[:, 0:1]
        dz_f = dot(left_f, back, 0, 0) - z_f.astype(f32) * t_f[:, 0:1]
        yield
        ctm[c] = (made[0:mem] + joins[0]).astype(bf16)
        acc_w[...] += made[mem : 2 * mem] + joins[1]
        acc_r[...] += made[2 * mem + read :]
        zm[c], zf[c] = dz_m.astype(bf16), dz_f.astype(bf16)
        for copy in out_copies(c):
            copy.start()

    late = clips - clips // 4
    clip_loop(0, late, 2, closing)
    sums.owners(0)
    sums.sides(1)
    clip_loop(late, clips, 2, closing)

    zero_rows = jnp.zeros((1, width), f32)
    rest = jnp.concatenate(
        [zero_rows, d_gain_attn, d_gain_mlp, zero_rows, jnp.zeros((12, width), f32)], axis=0
    )
    stacked = jnp.concatenate([acc_w[...], acc_r[...], rest], axis=0)
    gp[:, SMALL:PACK] = jnp.zeros((groups, ROWS, width), bf16)
    gp[:, SMALL:PACK, 0:128] = stacked.T.astype(bf16).reshape(groups, ROWS, 128)
    for d in range(groups):
        gp[d, SMALL : SMALL + 1, 128 : 128 + piece] = bias[:, piece * d : piece * (d + 1)].astype(bf16)
    sums.small_core()
    sums.final(0)
    sums.small_send()
    frames_out()
    sums.owners(1)
    sums.final(1)
    sums.early()
    sums.small_final()

    @pl.loop(0, clips)
    def _(c):
        for copy in out_copies(c):
            copy.wait()

    for i in range(max(0, len(chunks) - 2), len(chunks)):
        raw_copy(i, True).wait()
    sums.finish()


def step_scratch(clips, toks, mem, read, width):
    vm, sem = pltpu.VMEM, pltpu.SemaphoreType.DMA
    rows, wide = clips * read, mem + read
    return [
        vm((clips, mem, width), bf16),
        vm((clips, toks, width), bf16),
        vm((clips, mem, width), bf16),
        vm((wide, width), bf16),
        vm((8, width), f32),
        vm((1, 4 * width), f32),
        vm((clips, mem, mem), f32),
        vm((clips, mem, toks), f32),
        vm((clips, mem, mem), bf16),
        vm((clips, mem, toks), bf16),
        vm((clips, read, mem), bf16),
        vm((clips, read, toks), bf16),
        vm((clips, read, mem), bf16),
        vm((clips, read, toks), bf16),
        vm((clips, 8, mem), f32),
        vm((clips, 8, toks), f32),
        vm((clips, 8, mem), f32),
        vm((rows, width), f32),
        vm((rows, width), bf16),
        vm((rows, width), bf16),
        vm((rows, width), bf16),
        vm((rows // 128, HEADS, 128, 128), bf16),
        vm((rows, width), bf16),
        vm((rows, width), f32),
        vm((rows, width), bf16),
        vm((rows, width), bf16),
        vm((width // 128, 4 * max(rows, width), 128), f32),
        vm((max(rows, width), 4 * width), bf16),
        vm((rows, width), f32),
        vm((rows, width), f32),
        vm((rows, width), bf16),
        vm((mem, width), f32),
        vm((read, width), f32),
        vm((rows, 256), bf16),
        vm((2, 16 * clips, width), bf16),
        sem((2, clips)),
        sem((2, clips)),
        sem((-(-toks // 16),)),
    ]


def plain_kernel(clips, *refs):
    ins, wpack_h, outs, gp = refs[0:5], refs[5], refs[6:10], refs[10]
    wp, tiny, sems = refs[11:14]
    step(load_weights(wpack_h, wp, tiny, sems), NoSums(), clips, ins, outs, refs[14:], wp, tiny, gp)


def whole_kernel(clips, *refs):
    weights, ins, state = refs[0:7], refs[7:12], refs[12:18]
    outs, red, xrec = refs[18:22], refs[22], refs[23]
    refs = refs[24:]
    wp, tiny, gp = refs[0:3]
    gather_refs, refs = refs[3:21], refs[21:]
    sum_refs, refs = refs[0:21], refs[21:]
    muon_refs, refs = refs[0:8], refs[8:]
    gather = gather_weights(weights, wp, tiny, *gather_refs)
    muon = Muon(red, state, xrec, *muon_refs, refs[26], refs[27])
    step(gather, Sums(muon, gp, red, *sum_refs), clips, ins, outs, refs, wp, tiny, gp)
    muon.finish()


def run_step(frames, valid, memory, ct_memory, ct_read, wpack=None, weights=(), state=()):
    clips, toks, width = frames.shape
    mem, read = memory.shape[1], ct_read.shape[1]
    groups, rows = width // ROWS, clips * read
    vm, sem, made = pltpu.VMEM, pltpu.SemaphoreType.DMA, jax.ShapeDtypeStruct
    hbm = pl.BlockSpec(memory_space=pl.ANY)
    inside = pl.BlockSpec(memory_space=pltpu.VMEM)
    out_shape = [
        made(memory.shape, bf16), made((rows, width), bf16), made((toks * clips, width), bf16), made(memory.shape, bf16),
    ]
    out_specs = [hbm, inside, hbm, hbm]
    in_specs = [hbm, inside, hbm, hbm, inside]
    frames = frames.transpose(1, 0, 2).reshape(toks * clips, width)
    operands = [frames, valid, memory, ct_memory, ct_read.reshape(rows, width)]
    scratch = [vm((groups, SMALL, width), bf16), vm((groups, ROWS, TINY), bf16)]
    params = dict(vmem_limit_bytes=VMEM_LIMIT)
    if weights:
        n = lax.axis_size("sub")
        kernel = whole_kernel
        operands = [*weights, *operands, *state]
        in_specs = [inside] * len(weights) + in_specs + [inside] * len(state)
        out_shape += [made((PACK, width), f32), made((PACK, width), bf16)]
        out_specs += [inside, inside]
        scratch += [
            vm((groups, PACK, width), bf16),
            vm((SMALL, width), bf16), vm((ROWS, TINY), bf16), sem((groups,)), sem((groups,)), sem((2,)),
            *[sem((n,))] * 6, sem((4, n)), *[sem((n,))] * 5, sem((4, n)),
            vm((4, n, PACK, width), bf16),
            vm((n, 112, width), bf16),
            vm((n, 96, width), bf16),
            vm((n, PACK, width), bf16),
            vm((n, PACK, width), bf16),
            vm((n - 1, PACK, width), bf16),
            vm((4, n, ROWS, TINY), bf16),
            *[sem((3, 4))] * 2, *[sem((2, n))] * 8, *[sem((2, n - 1))] * 2, *[sem((4, n))] * 2,
            vm((PACK, width), bf16), vm((groups, 64, width), bf16), sem((len(OWNERS),)), sem((groups,)), sem,
            sem((groups,)), sem((len(OWNERS),)), sem,
        ]
        params.update(collective_id=1, has_side_effects=True)
    else:
        kernel = plain_kernel
        operands.append(wpack)
        in_specs.append(hbm)
        out_shape.append(made((groups, PACK, width), bf16))
        out_specs.append(inside)
        scratch.append(sem((2,)))
    outs = pl.pallas_call(
        functools.partial(kernel, clips),
        out_shape=tuple(out_shape),
        in_specs=in_specs,
        out_specs=tuple(out_specs),
        scratch_shapes=scratch + step_scratch(clips, toks, mem, read, width),
        compiler_params=pltpu.CompilerParams(**params),
        name="clip_step",
    )(*operands)
    return outs


def clip_outputs(outs, clips):
    new_memory, read_out, by_token, grad_memory = outs
    width = by_token.shape[1]
    frames = by_token.reshape(-1, clips, width).transpose(1, 0, 2)
    return new_memory, read_out.reshape(clips, ROWS, width), frames, grad_memory


OWNERS = ((2, 0), (4, 3), (2, 3), (4, 0), (0, 1), (6, 2), (0, 3))
PIECES = ((0, 16), (16, 16), (32, 16), (48, 16), (64, 64), (128, 64), (192, 16))


def is_owner(m):
    return (lax.axis_index("dp") == OWNERS[m][0]) & (lax.axis_index("sub") == OWNERS[m][1])


def small_grads(red, gains_t):
    return (
        red[SMALL:PACK, 0:96] * gains_t[:, 3:4],
        red[SMALL:PACK, 96:112] * gains_t[:, 0:1],
    )


def exact_dot(a, b, ca=1, cb=0):
    return lax.dot_general(a, b, (((ca,), (cb,)), ((), ())), preferred_element_type=f32, precision=highest)


def iterate_small(x, same):
    norm = jnp.sum(x * x, axis=1, keepdims=True)
    total = jnp.sum(jnp.where(same, norm.T, 0.0), axis=1, keepdims=True)
    x = x * (1.0 / (jnp.sqrt(total) + 1e-07))
    for _ in range(5):
        q = jnp.where(same, exact_dot(x, x, 1, 1), 0.0)
        mixed = NS[1] * q + NS[2] * exact_dot(q, q)
        x = NS[0] * x + exact_dot(mixed, x)
    return x


class Muon:
    def __init__(self, acc, state, xrec, pk, buf, gsend, grecv, gown, ssend, srecv, sown, x, low):
        self.__dict__.update(
            acc=acc, state=state, xrec=xrec, pk=pk, buf=buf, gsend=gsend, grecv=grecv, gown=gown,
            ssend=ssend, srecv=srecv, sown=sown, x=x, low=low,
        )
        self.count = lax.axis_size("sub")
        self.me = lax.axis_index("dp") * self.count + lax.axis_index("sub")
        self.groups = buf.shape[0]

    def piece(self, m):
        start, size = PIECES[m]
        return self.pk.at[pl.ds(start, size)], self.buf.at[self.me, pl.ds(0, size)]

    def away(self, m):
        return remote(*self.piece(m), self.gsend.at[m], self.grecv.at[self.me], OWNERS[m])

    def home(self, m):
        return pltpu.make_async_copy(*self.piece(m), self.gown)

    def send(self, part):
        attn_mom, w_in_mom, w_out_mom, s_read_mom, s_write_mom, gains = self.state
        acc, pk = self.acc, self.pk
        width = acc.shape[1]
        if part == 0:
            for m in range(4):
                at = slice(64 + ROWS * m, 64 + ROWS * (m + 1))
                pk[at] = (0.5 * w_in_mom[:, width * m : width * (m + 1)] + acc[at]).astype(bf16)
            pk[128:192] = (0.5 * w_out_mom[...] + acc[128:192]).astype(bf16)
        elif part == 1:
            for m in range(4):
                at = slice(ROWS * m, ROWS * (m + 1))
                pk[at] = (0.5 * attn_mom[m] + acc[at]).astype(bf16)
        else:
            g_write, g_read = small_grads(acc, turn_gains(gains[...]))
            pk[SMALL:PACK] = jnp.zeros((ROWS, width), bf16)
            pk[SMALL:PACK, 0:96] = (0.5 * s_write_mom[...] + g_write).astype(bf16)
            pk[SMALL:PACK, 96:112] = (0.5 * s_read_mom[...] + g_read).astype(bf16)
        for m in ((4, 5), (0, 1, 2, 3), (6,))[part]:

            @pl.when(jnp.logical_not(is_owner(m)))
            def _():
                self.away(m).start()

            @pl.when(is_owner(m))
            def _():
                self.home(m).start()

    def each_other(self, act):
        @pl.loop(0, self.groups)
        def _(d):
            @pl.when(d != self.me)
            def _():
                act(d)

    def whole(self, m):
        def take(d):
            got = self.buf.at[d, pl.ds(0, PIECES[m][1])]
            remote(got, got, self.grecv.at[d], self.grecv.at[d], OWNERS[m]).wait_recv()

        self.each_other(take)
        self.home(m).wait()

    def row_copy(self, m, d):
        start, size = PIECES[m]
        return remote(
            self.buf.at[d, pl.ds(0, size)], self.xrec.at[pl.ds(start, size)], self.ssend.at[d], self.srecv.at[m],
            (d // self.count, lax.rem(d, self.count)),
        )

    def row_home(self, m):
        start, size = PIECES[m]
        return pltpu.make_async_copy(
            self.buf.at[self.me, pl.ds(0, size)], self.xrec.at[pl.ds(start, size)], self.sown
        )

    def spread(self, m):
        self.each_other(lambda d: self.row_copy(m, d).start())
        self.row_home(m).start()

    def spread_wait(self, m):
        self.each_other(lambda d: self.row_copy(m, d).wait_send())
        self.row_home(m).wait()

    def put(self, j, value):
        n = value.shape[0]
        for q in range(value.shape[1] // 128):
            self.x[q, n * j : n * (j + 1)] = value[:, 128 * q : 128 * (q + 1)]

    def get(self, j, n):
        return jnp.concatenate([self.x[q, n * j : n * (j + 1)] for q in range(self.x.shape[0])], axis=1)

    def iterate(self, blocks, n):
        low = self.low
        total = jnp.zeros((1, 1), f32)
        for j in range(blocks):
            now = self.get(j, n)
            total = total + jnp.sum(now * now, keepdims=True)
        scale = 1.0 / (jnp.sqrt(total) + 1e-07)
        for j in range(blocks):
            now = self.get(j, n) * scale
            self.put(j, now)
            low[0:n, n * j : n * (j + 1)] = now.astype(bf16)

        self.sweep(blocks, n, 3)

    def sweep(self, blocks, n, times):
        low = self.low

        def block(j):
            return low[0:n, n * j : n * (j + 1)]

        @pl.loop(0, times)
        def _(_):
            q = dot(block(0), block(0), 1, 1)
            for j in range(1, blocks):
                q = q + dot(block(j), block(j), 1, 1)
            q_low = q.astype(bf16)
            mixed = (NS[1] * q + NS[2] * dot(q_low, q_low)).astype(bf16)
            for j in range(blocks):
                new = NS[0] * self.get(j, n) + dot(mixed, block(j))
                self.put(j, new)
                low[0:n, n * j : n * (j + 1)] = new.astype(bf16)

    def early(self):
        buf, groups = self.buf, self.groups
        width = buf.shape[2]
        per = groups // 4

        @pl.when(is_owner(4))
        def _():
            self.whole(4)
            for j in range(4):
                self.put(j, buf[:, ROWS * j : ROWS * (j + 1)].reshape(width, width).astype(f32))

        @pl.when(is_owner(5))
        def _():
            self.whole(5)
            for j in range(4):
                self.put(j, buf[per * j : per * (j + 1)].reshape(width, width).astype(f32).T)

        @pl.when(is_owner(4) | is_owner(5))
        def _():
            self.iterate(4, width)

    def work(self):
        buf, groups = self.buf, self.groups
        width = buf.shape[2]
        per = groups // 4

        @pl.when(is_owner(4) | is_owner(5))
        def _():
            self.sweep(4, width, 2)

        @pl.when(is_owner(4))
        def _():
            for j in range(4):
                buf[:, ROWS * j : ROWS * (j + 1)] = self.low[0:width, width * j : width * (j + 1)].reshape(
                    groups, ROWS, width
                )

        @pl.when(is_owner(5))
        def _():
            for j in range(4):
                buf[per * j : per * (j + 1)] = self.get(j, width).T.astype(bf16).reshape(per, 64, width)

        for m in range(4):

            @pl.when(is_owner(m))
            def _():
                self.whole(m)

        @pl.when(is_owner(0) | is_owner(1) | is_owner(2) | is_owner(3))
        def _():
            self.put(0, buf[:, 0:ROWS].reshape(width, width).astype(f32))
            self.iterate(1, width)
            self.sweep(1, width, 2)
            buf[:, 0:ROWS] = self.low[0:width, 0:width].reshape(groups, ROWS, width)

        @pl.when(is_owner(6))
        def _():
            self.whole(6)
            table = buf[:, 0:ROWS, 0:128].reshape(width, 128).astype(f32).T
            row = lax.broadcasted_iota(jnp.int32, (128, 128), 0)
            col = lax.broadcasted_iota(jnp.int32, (128, 128), 1)
            same = ((row < 96) & (col < 96)) | ((row >= 96) & (col >= 96))
            made = iterate_small(table, same)
            buf[:, 0:ROWS, 0:128] = made.T.astype(bf16).reshape(groups, ROWS, 128)

    def finish(self):
        many = range(len(OWNERS))
        self.work()
        for m in many:

            @pl.when(is_owner(m))
            def _():
                self.spread(m)

        for m in many:

            @pl.when(jnp.logical_not(is_owner(m)))
            def _():
                self.away(m).wait_send()
                start, size = PIECES[m]
                got = self.xrec.at[pl.ds(start, size)]
                remote(got, got, self.srecv.at[m], self.srecv.at[m], OWNERS[m]).wait_recv()

            @pl.when(is_owner(m))
            def _():
                self.spread_wait(m)


def finish_kernel(
    red, xrec, attn, w_in, w_out, s_read, s_write, attn_mom, w_in_mom, w_out_mom, s_read_mom, s_write_mom,
    gains, gains_first, gains_second, bias, bias_first, bias_second, nm_in, ro_in, gf_in, gm_in,
    nm, ro, gf, gm, g_attn, g_in, g_out, g_read, g_write, g_gains, g_bias,
    n_attn, n_in, n_out, n_read, n_write, n_gains, n_bias, m_attn, m_in, m_out, m_read, m_write,
    n_gains_first, n_gains_second, n_bias_first, n_bias_second, sems, *stages,
):
    width = red.shape[1]
    ins, outs = [], []
    for src, stage, dst, cuts in zip((gf_in, nm_in, gm_in, ro_in), stages, (gf, nm, gm, ro), (3, 2, 2, 1)):
        size = src.shape[0] // cuts
        for i in range(cuts):
            at, k = pl.ds(size * i, size), len(ins)
            ins.append(pltpu.make_async_copy(src.at[at], stage.at[at], sems.at[0, k]))
            outs.append(pltpu.make_async_copy(stage.at[at], dst.at[at], sems.at[1, k]))
            ins[k].start()
    for copy_in, copy_out in zip(ins, outs):
        copy_in.wait()
        copy_out.start()
    for m in range(4):
        lanes = slice(width * m, width * (m + 1))
        at = slice(ROWS * m, ROWS * (m + 1))
        g = red[at]
        g_attn[m] = g
        m_attn[m] = 0.5 * attn_mom[m] + g
        n_attn[m] = attn[m] - xrec[at].astype(f32)
        at = slice(64 + ROWS * m, 64 + ROWS * (m + 1))
        g = red[at]
        g_in[:, lanes] = g
        m_in[:, lanes] = 0.5 * w_in_mom[:, lanes] + g
        n_in[:, lanes] = w_in[:, lanes] - xrec[at].astype(f32)
    g = red[128:192]
    g_out[...] = g
    m_out[...] = 0.5 * w_out_mom[...] + g
    n_out[...] = w_out[...] - 2.0 * xrec[128:192].astype(f32)
    small = xrec[SMALL:PACK, 0:128].astype(f32)
    n_write[...] = s_write[...] - math.sqrt(512 / 96) * small[:, 0:96]
    n_read[...] = s_read[...] - math.sqrt(512 / 16) * small[:, 96:112]
    made_write, made_read = small_grads(red, turn_gains(gains[...]))
    g_write[...] = made_write
    g_read[...] = made_read
    m_write[...] = 0.5 * s_write_mom[...] + made_write
    m_read[...] = 0.5 * s_read_mom[...] + made_read
    low_write = s_write[...].astype(bf16).astype(f32)
    low_read = s_read[...].astype(bf16).astype(f32)
    to_read = jnp.sum(low_read * red[SMALL:PACK, 96:112], axis=1, keepdims=True)
    to_write = jnp.sum(low_write * red[SMALL:PACK, 0:96], axis=1, keepdims=True)
    column = lax.broadcasted_iota(jnp.int32, (ROWS, 128), 1)
    wide = jnp.where(
        column == 112, to_read, jnp.where(column == 115, to_write, red[SMALL:PACK, 0:128])
    )
    grad_gains = wide.T[112:116]
    g_gains[...] = grad_gains
    n_gains[...], n_gains_first[...], n_gains_second[...] = adam_step(
        gains[...], gains_first[...], gains_second[...], grad_gains
    )
    grad_bias = red[SMALL : SMALL + 1, 128:192]
    g_bias[...] = grad_bias
    n_bias[...], n_bias_first[...], n_bias_second[...] = adam_step(
        bias[...], bias_first[...], bias_second[...], grad_bias
    )
    for copy in outs:
        copy.wait()


highest = lax.Precision.HIGHEST
NS = (3.4445, -4.775, 2.0315)


def canonical(attn, w_in, w_out, s_read, s_write, gains, bias):
    width = attn.shape[2]
    groups = attn.shape[1] // ROWS
    a = attn.astype(bf16).reshape(4, groups, ROWS, width).transpose(1, 0, 2, 3)
    i = w_in.astype(bf16).reshape(groups, ROWS, 4, width).transpose(0, 2, 1, 3)
    o = w_out.astype(bf16).reshape(groups, 64, width)
    s = jnp.concatenate([s_write, s_read, gains.T], axis=1).astype(bf16)
    s = jnp.pad(s, ((0, 0), (0, 128 - s.shape[1]))).reshape(groups, ROWS, 128)
    b = bias.astype(bf16).reshape(groups, 1, 64)
    b = jnp.pad(b, ((0, 0), (0, ROWS - 1), (0, width - 128 - 64)))
    return jnp.concatenate(
        [
            a.reshape(groups, 64, width),
            i.reshape(groups, 64, width),
            o,
            jnp.concatenate([s, b], axis=2),
        ],
        axis=1,
    )


def natural(pack, mem, read):
    groups, _, width = pack.shape
    a = pack[:, 0:64].reshape(groups, 4, ROWS, width).transpose(1, 0, 2, 3)
    i = pack[:, 64:128].reshape(groups, 4, ROWS, width).transpose(0, 2, 1, 3)
    s = pack[:, SMALL:PACK, 0:128].reshape(groups * ROWS, 128)
    return (
        a.reshape(4, groups * ROWS, width),
        i.reshape(groups * ROWS, 4 * width),
        pack[:, 128:192].reshape(groups * 64, width),
        s[:, 0:mem],
        s[:, mem : mem + read],
        s[:, mem + read + 1 : mem + read + 3],
        pack[:, SMALL, 128:192].reshape(groups * 64),
    )


def adam_step(weight, first, second, grad):
    first_new = 0.5 * first + 0.5 * grad
    second_new = 0.5 * second + 0.5 * grad * grad
    part = 1.0 - 0.5**10
    moved = 0.25 * (first_new / part) / (jnp.sqrt(second_new / part) + 1e-08)
    return weight - moved, first_new, second_new


def orthogonalize(matrix):
    tall = matrix.shape[0] > matrix.shape[1]
    x = matrix.T if tall else matrix
    x = x / (jnp.sqrt(jnp.sum(x * x)) + 1e-07)
    for _ in range(5):
        q = jnp.dot(x, x.T, precision=highest)
        mixed = NS[1] * q + NS[2] * jnp.dot(q, q, precision=highest)
        x = NS[0] * x + jnp.dot(mixed, x, precision=highest)
    return x.T if tall else x


def any_slice(
    frames, valid, memory, ct_memory, ct_read,
    attn, w_in, w_out, s_read, s_write, gains, bias,
    attn_mom, w_in_mom, w_out_mom, s_read_mom, s_write_mom,
    gains_first, gains_second, bias_first, bias_second,
):
    axes = ("dp", "sub")
    mem, read = memory.shape[1], ct_read.shape[1]

    def gather(v, axis):
        return lax.all_gather(v.astype(bf16), axes, axis=axis, tiled=True)

    def scatter(v, axis):
        return lax.psum_scatter(v, axes, scatter_dimension=axis, tiled=True)

    wpack = canonical(
        gather(attn, 1), gather(w_in, 0), gather(w_out, 0), gather(s_read, 0),
        gather(s_write, 0), gather(gains, 1), gather(bias, 0),
    )
    *step_outs, gpack = run_step(frames, valid, memory, ct_memory, ct_read, wpack)
    new_memory, read_out, grad_frames, grad_memory = clip_outputs(step_outs, frames.shape[0])
    sums = natural(gpack.astype(f32), mem, read)
    g_attn, g_in, g_out, sum_w, sum_r, g_two, g_bias = (
        scatter(v, axis) for v, axis in zip(sums, (1, 0, 0, 0, 0, 0, 0))
    )
    low_gain = gains.astype(bf16).astype(f32)
    low_w, low_r = s_write.astype(bf16).astype(f32), s_read.astype(bf16).astype(f32)
    g_s_write = low_gain[3][:, None] * sum_w
    g_s_read = low_gain[0][:, None] * sum_r
    g_gains = jnp.stack(
        [jnp.sum(low_r * sum_r, axis=1), g_two[:, 0], g_two[:, 1], jnp.sum(low_w * sum_w, axis=1)]
    )
    moms = (
        0.5 * attn_mom + g_attn,
        0.5 * w_in_mom + g_in,
        0.5 * w_out_mom + g_out,
        0.5 * s_read_mom + g_s_read,
        0.5 * s_write_mom + g_s_write,
    )
    whole = [gather(v, axis).astype(f32) for v, axis in zip(moms, (1, 0, 0, 0, 0))]
    matrices = [whole[0][m] for m in range(4)] + whole[1:]
    rank, count = lax.axis_index(axes), lax.axis_size(axes)
    owned = [
        lax.cond(rank == m * count // 8, orthogonalize, jnp.zeros_like, matrix)
        for m, matrix in enumerate(matrices)
    ]
    ortho = (
        scatter(jnp.stack(owned[:4]), 1), *(scatter(v, 0) for v in owned[4:])
    )
    stepped = []
    for weight, part, full in zip((attn, w_in, w_out, s_read, s_write), ortho, whole):
        ratio = max(1.0, full.shape[-2] / full.shape[-1]) ** 0.5
        stepped.append(weight - ratio * part)
    n_gains = adam_step(gains, gains_first, gains_second, g_gains)
    n_bias = adam_step(bias, bias_first, bias_second, g_bias)
    return (
        new_memory, read_out, grad_frames, grad_memory,
        g_attn, g_in, g_out, g_s_read, g_s_write, g_gains, g_bias,
        *stepped, n_gains[0], n_bias[0], *moms, n_gains[1], n_gains[2], n_bias[1], n_bias[2],
    )


def this_slice(
    frames, valid, memory, ct_memory, ct_read,
    attn, w_in, w_out, s_read, s_write, gains, bias,
    attn_mom, w_in_mom, w_out_mom, s_read_mom, s_write_mom,
    gains_first, gains_second, bias_first, bias_second,
):
    inside, anywhere = pl.BlockSpec(memory_space=pltpu.VMEM), pl.BlockSpec(memory_space=pl.ANY)

    def like(*arrays):
        return tuple(jax.ShapeDtypeStruct(a.shape, f32) for a in arrays)

    def row(v):
        return v.reshape(1, -1)

    moms = (attn_mom, w_in_mom, w_out_mom, s_read_mom, s_write_mom)
    weights = (attn, w_in, w_out, s_read, s_write)
    *step_outs, red, xrec = run_step(
        frames, valid, memory, ct_memory, ct_read, None, (*weights, gains, row(bias)), (*moms, gains)
    )
    biases = (row(bias), row(bias_first), row(bias_second))
    made = pl.pallas_call(
        finish_kernel,
        out_shape=(
            *(jax.ShapeDtypeStruct(v.shape, bf16) for v in step_outs),
            *like(*weights, gains, biases[0]),
            *like(*weights, gains, biases[0]),
            *like(*moms, gains, gains, biases[0], biases[0]),
        ),
        in_specs=[inside] * 18 + [anywhere] * 4,
        out_specs=(anywhere,) * 4 + (inside,) * 23,
        scratch_shapes=[
            pltpu.SemaphoreType.DMA((2, 9)), *(pltpu.VMEM(step_outs[i].shape, bf16) for i in (2, 0, 3, 1)),
        ],
        compiler_params=pltpu.CompilerParams(vmem_limit_bytes=VMEM_LIMIT),
        name="finish",
    )(red, xrec, *weights, *moms, gains, gains_first, gains_second, *biases, *step_outs)
    flat = bias.shape
    return tuple(
        v.reshape(flat) if v.shape == biases[0].shape else v
        for v in (*clip_outputs(made[:4], frames.shape[0]), *made[4:])
    )


def solution(mesh):
    both = ("dp", "sub")
    rows3, rows2, rows1 = P(both, None, None), P(both, None), P(both)
    mid, last = P(None, both, None), P(None, both)
    weights = (mid, rows2, rows2, rows2, rows2)
    here = (mesh.shape["dp"], mesh.shape["sub"]) == (8, 4)
    return jax.shard_map(
        this_slice if here else any_slice,
        mesh=mesh,
        in_specs=(
            rows3, rows2, rows3, rows3, rows3, *weights, last, rows1, *weights, last, last, rows1, rows1,
        ),
        out_specs=(
            rows3, rows3, rows3, rows3, *weights, last, rows1, *weights, last, rows1, *weights,
            last, last, rows1, rows1,
        ),
        check_vma=False,
    )
```

```python
import functools
import math

import jax
import jax.numpy as jnp
from jax import lax
from jax.experimental import pallas as pl
from jax.experimental.pallas import tpu as pltpu
from jax.sharding import PartitionSpec as P

f32 = jnp.float32
bf16 = jnp.bfloat16
MESH = pl.DeviceIdType.MESH

HEADS = 8
HEAD_DIM = 64
NORM_EPS = 1e-06
MASKED = -1000000000.0
GELU_A = math.sqrt(2.0 / math.pi)
GELU_B = 0.044715
VMEM_LIMIT = 60 * 1024 * 1024

ROWS = 16
PACK = 208
SMALL = 192
TINY = 256
X, Y, CORE = 2, 4, 1
TOGETHER = (False, True)
PARTS = ((64, 64, 64, 0), (0, 32, 32, 64))


def dot(a, b, ca=1, cb=0):
    return lax.dot_general(a, b, (((ca,), (cb,)), ((), ())), preferred_element_type=f32)


def remote(src, dst, send, recv, device):
    return pltpu.make_async_remote_copy(
        src_ref=src, dst_ref=dst, send_sem=send, recv_sem=recv, device_id=device, device_id_type=MESH
    )


def lockstep(bodies):
    done = object()
    running = [body() for body in bodies]
    while running:
        running = [body for body in running if next(body, done) is not done]


def turn_gains(g):
    eye = (
        lax.broadcasted_iota(jnp.int32, (4, 4), 0) == lax.broadcasted_iota(jnp.int32, (4, 4), 1)
    ).astype(bf16)
    return dot(g.astype(bf16), eye, 0, 0)


GATHERED = ((0, 192),)


class Gather:
    def __init__(self, weights, out, tiny, x_ref, x_tiny, tsend, trecv, own_sem, up, down, sx, sy, fx, fy, sc, rz, rx, ry, rdx, rdy, rc):
        self.__dict__.update(
            weights=weights, out=out, tiny=tiny, x_ref=x_ref, x_tiny=x_tiny, tsend=tsend, trecv=trecv, own_sem=own_sem,
            up=up, down=down, sx=sx, sy=sy, fx=fx, fy=fy, sc=sc, rz=rz, rx=rx, ry=ry, rdx=rdx, rdy=rdy, rc=rc,
        )
        self.dp, self.p = lax.axis_index("dp"), lax.axis_index("sub")
        self.count = lax.axis_size("sub")
        self.last = self.count - 1
        self.me = self.dp * self.count + self.p
        self.groups = out.shape[0]

    def device(self, d):
        return (d // self.count, lax.rem(d, self.count))

    def flip(self, mask):
        return (jnp.bitwise_xor(self.dp, mask), self.p)

    def unit(self, g, mask, s):
        return self.out.at[jnp.bitwise_xor(self.dp, mask) * self.count + s, pl.ds(*GATHERED[g])]

    def half(self, g, mask, s, second):
        start, size = GATHERED[g]
        d = jnp.bitwise_xor(self.dp, mask) * self.count + s
        return self.out.at[d, pl.ds(start + (size // 2 if second else 0), size // 2)]

    def column(self, g, mask, second=None):
        start, size = GATHERED[g]
        if second is not None:
            start, size = start + (size // 2 if second else 0), size // 2
        return self.out.at[pl.ds(jnp.bitwise_xor(self.dp, mask) * self.count, self.count), pl.ds(start, size)]

    def own(self, g):
        return self.x_ref.at[pl.ds(*GATHERED[g])]

    def others(self, act):
        @pl.loop(0, self.groups)
        def _(d):
            @pl.when(d != self.me)
            def _():
                act(d)

    def tiny_copy(self, d):
        return remote(self.x_tiny, self.tiny.at[self.me], self.tsend, self.trecv, self.device(d))

    def chain(self, g, step, way, s, src):
        sems = self.up if way > 0 else self.down
        return remote(src, self.unit(g, 0, s), sems.at[g, step], self.rz.at[g, s], (self.dp, self.p + way))

    def side(self, g, mask, s, src):
        send, recv = (self.sx, self.rx) if mask == X else (self.sy, self.ry)
        return remote(src, self.unit(g, 0, s), send.at[g], recv.at[g, s], self.flip(mask))

    def halves(self, g, mask, s):
        other = Y if mask == X else X
        send, recv = (self.fy, self.rdy) if mask == X else (self.fx, self.rdx)
        ref = self.half(g, mask, s, mask == Y)
        return remote(ref, ref, send.at[g], recv.at[g], self.flip(other))

    def cross(self, g, kind):
        ref = self.column(g, (0, X, Y, X + Y)[kind])
        return remote(ref, ref, self.sc.at[g, kind], self.rc.at[g, kind], self.flip(CORE))

    def share(self, g, s, src):
        self.side(g, X, s, src).start()
        self.side(g, Y, s, src).start()

    def take(self, ref, sem):
        remote(ref, ref, sem, sem, (self.dp, self.p)).wait_recv()

    def sent(self, ref, sem):
        remote(ref, ref, sem, sem, (self.dp, self.p)).wait_send()

    def local(self, g):
        return pltpu.make_async_copy(self.own(g), self.unit(g, 0, self.p), self.own_sem.at[g])

    def local_tiny(self):
        return pltpu.make_async_copy(self.x_tiny, self.tiny.at[self.me], self.own_sem.at[len(GATHERED)])

    def start(self):
        attn, w_in, w_out, s_read, s_write, gains, bias = self.weights
        x_ref, x_tiny, p = self.x_ref, self.x_tiny, self.p
        width = x_ref.shape[1]
        barrier = pltpu.get_barrier_semaphore()
        self.others(
            lambda d: pl.semaphore_signal(barrier, inc=1, device_id=self.device(d), device_id_type=MESH)
        )
        x_tiny[...] = jnp.zeros((ROWS, TINY), bf16)
        x_tiny[:, 0:96] = s_write[...].astype(bf16)
        x_tiny[:, 96:112] = s_read[...].astype(bf16)
        x_tiny[:, 112:116] = turn_gains(gains[...]).astype(bf16)
        x_tiny[0:1, 128:192] = bias[...].astype(bf16)
        for m in range(4):
            x_ref[ROWS * m : ROWS * (m + 1)] = attn[m].astype(bf16)
            x_ref[64 + ROWS * m : 64 + ROWS * (m + 1)] = w_in[:, width * m : width * (m + 1)].astype(bf16)
        x_ref[128:192] = w_out[...].astype(bf16)
        self.local_tiny().start()
        for g in range(len(GATHERED)):
            self.local(g).start()
        pl.semaphore_wait(barrier, self.groups - 1)
        for g in range(len(GATHERED)):

            @pl.when(p < self.last)
            def _():
                self.chain(g, 0, 1, p, self.own(g)).start()

            @pl.when(p > 0)
            def _():
                self.chain(g, 0, -1, p, self.own(g)).start()

            self.share(g, p, self.own(g))
            if g == 0:
                self.others(lambda d: self.tiny_copy(d).start())

    def tables(self):
        self.take(self.tiny.at[pl.ds(0, self.groups - 1)], self.trecv)
        self.local_tiny().wait()

    def arrived(self, g, s):
        for mask, recv in ((X, self.rx), (Y, self.ry)):
            got = self.unit(g, mask, s)
            self.take(got, recv.at[g, s])
            self.halves(g, mask, s).start()

    def arrivals(self, g, k):
        p = self.p
        if k == 0:
            self.arrived(g, p)
            return

        @pl.when(p >= k)
        def _():
            self.arrived(g, p - k)

        @pl.when(p + k <= self.last)
        def _():
            self.arrived(g, p + k)

    def stage(self, g, k):
        p, last = self.p, self.last
        if k <= last:
            for way in (1, -1):

                @pl.when(p >= k if way > 0 else p + k <= last)
                def _():
                    s = p - k * way
                    got = self.unit(g, 0, s)
                    self.take(got, self.rz.at[g, s])
                    if k < last:

                        @pl.when(p < last if way > 0 else p > 0)
                        def _():
                            self.chain(g, k, way, s, got).start()

                    self.share(g, s, got)

        if k == last:
            self.local(g).wait()
            self.cross(g, 0).start()
        self.arrivals(g, k - 1)
        if k > last:
            self.cross(g, 1).start()
            self.cross(g, 2).start()

    def end(self, g):
        self.take(self.column(g, X + Y, False), self.rdy.at[g])
        self.take(self.column(g, X + Y, True), self.rdx.at[g])
        self.cross(g, 3).start()
        for kind, mask in enumerate((CORE, X + CORE, Y + CORE, X + Y + CORE)):
            self.take(self.column(g, mask), self.rc.at[g, kind])

    def finish(self):
        p, last = self.p, self.last
        self.sent(self.tiny.at[pl.ds(0, self.groups - 1)], self.tsend)
        for g in range(len(GATHERED)):
            self.sent(self.column(g, 0), self.sx.at[g])
            self.sent(self.column(g, 0), self.sy.at[g])
            self.sent(self.column(g, X, False), self.fy.at[g])
            self.sent(self.column(g, Y, True), self.fx.at[g])
            for kind in range(4):
                self.cross(g, kind).wait_send()
            for k in range(last):

                @pl.when((p < last) & (p >= k))
                def _():
                    self.chain(g, k, 1, p - k, self.unit(g, 0, p - k)).wait_send()

                @pl.when((p > 0) & (p + k <= last))
                def _():
                    self.chain(g, k, -1, p + k, self.unit(g, 0, p + k)).wait_send()


class Load:
    def __init__(self, wpack_h, out, tiny, sems):
        self.big = pltpu.make_async_copy(wpack_h.at[:, pl.ds(0, SMALL)], out, sems.at[0])
        self.little = pltpu.make_async_copy(wpack_h.at[:, pl.ds(SMALL, ROWS), pl.ds(0, TINY)], tiny, sems.at[1])

    def start(self):
        self.big.start()
        self.little.start()

    def tables(self):
        self.little.wait()

    def stage(self, g, k):
        pass

    def end(self, g):
        if g == 0:
            self.big.wait()

    def finish(self):
        pass


class Sums:
    def __init__(self, momentum, gp, out, rc, ra, rb, rx, ry, rz, tin, cs, cr, as_, ar, bs, br, xs, xr, ys, yr, zs, zr, ts, tr):
        self.__dict__.update(
            momentum=momentum, gp=gp, out=out, rc=rc, ra=ra, rb=rb, rx=rx, ry=ry, rz=rz, tin=tin,
            c=(cs, cr), a=(as_, ar), b=(bs, br), x=(xs, xr), y=(ys, yr), z=(zs, zr), t=(ts, tr),
        )
        self.dp, self.p = lax.axis_index("dp"), lax.axis_index("sub")
        self.count = lax.axis_size("sub")
        self.order = [lax.rem(self.p + off, self.count) for off in (2, 1, 3, 0)]
        self.sent = []

    def flip(self, mask):
        return (jnp.bitwise_xor(self.dp, mask), self.p)

    def place(self, mask, s):
        return jnp.bitwise_xor(self.dp, mask) * self.count + s

    def push(self, pair, index, src, dst, device):
        copy = remote(src, dst, pair[0].at[index], pair[1].at[index], device)
        copy.start()
        self.sent.append(copy)

    def take(self, pair, index, ref):
        remote(ref, ref, pair[0].at[index], pair[1].at[index], (self.dp, self.p)).wait_recv()

    def core(self, g):
        start, n1, n2, _ = PARTS[g]
        rows = pl.ds(start, n1 + n2)
        for k in (3, 1, 2, 0):
            src = self.gp.at[pl.ds(self.place((0, X, Y, X + Y)[k] + CORE, 0), self.count), rows]
            self.push(self.c, (g, k), src, self.rc.at[k, :, rows], self.flip(CORE))

    def ready(self, g, k):
        start, n1, n2, _ = PARTS[g]
        self.take(self.c, (g, k), self.rc.at[k, :, pl.ds(start, n1 + n2)])

    def total(self, k, s, start, size):
        at = slice(start, start + size)
        own = self.gp[self.place((0, X, Y, X + Y)[k], s), at]
        return own.astype(f32) + self.rc[k, s, at].astype(f32)

    def batches(self, g):
        if TOGETHER[g]:
            return [(0, pl.ds(0, self.count), self.order)]
        return [(s, pl.ds(s, 1), [s]) for s in self.order]

    def some(self, mask, at, start, size):
        first = self.place(mask, 0) + at.start
        return self.gp.at[pl.ds(first, at.size), pl.ds(start, size)]

    def diagonal(self, g):
        start, n1, n2, half = PARTS[g]
        self.ready(g, 3)
        for index, at, units in self.batches(g):
            for s in units:
                d = self.place(X + Y, s)
                self.gp[d, start : start + n1 + n2] = self.total(3, s, start, n1 + n2).astype(bf16)
            self.push(
                self.a, (g, index), self.some(X + Y, at, start, n1), self.ra.at[at, pl.ds(half, n1)], self.flip(X)
            )
            self.push(
                self.b, (g, index), self.some(X + Y, at, start + n1, n2), self.rb.at[at, pl.ds(half, n2)], self.flip(Y)
            )

    def sides(self, g):
        start, n1, n2, half = PARTS[g]
        rows = pl.ds(start, n1 + n2)
        self.ready(g, 1)
        self.ready(g, 2)
        for index, at, units in self.batches(g):
            self.take(self.b, (g, index), self.rb.at[at, pl.ds(half, n2)])
            for s in units:
                d = self.place(X, s)
                self.gp[d, start : start + n1] = self.total(1, s, start, n1).astype(bf16)
                more = self.rb[s, half : half + n2].astype(f32)
                self.gp[d, start + n1 : start + n1 + n2] = (self.total(1, s, start + n1, n2) + more).astype(bf16)
            self.push(self.x, (g, index), self.some(X, at, start, n1 + n2), self.rx.at[at, rows], self.flip(X))
            self.take(self.a, (g, index), self.ra.at[at, pl.ds(half, n1)])
            for s in units:
                d = self.place(Y, s)
                self.gp[d, start + n1 : start + n1 + n2] = self.total(2, s, start + n1, n2).astype(bf16)
                more = self.ra[s, half : half + n1].astype(f32)
                self.gp[d, start : start + n1] = (self.total(2, s, start, n1) + more).astype(bf16)
            self.push(self.y, (g, index), self.some(Y, at, start, n1 + n2), self.ry.at[at, rows], self.flip(Y))

    def owners(self, g, turns=None):
        start, n1, n2, _ = PARTS[g]
        size = n1 + n2
        rows = pl.ds(start, size)
        at = slice(start, start + size)
        turns = range(self.count) if turns is None else turns
        if 0 in turns:
            self.ready(g, 0)
            if TOGETHER[g]:
                self.take(self.x, (g, 0), self.rx.at[:, rows])
                self.take(self.y, (g, 0), self.ry.at[:, rows])
        for i in turns:
            s = self.order[i]
            if not TOGETHER[g]:
                self.take(self.x, (g, s), self.rx.at[pl.ds(s, 1), rows])
                self.take(self.y, (g, s), self.ry.at[pl.ds(s, 1), rows])
            mine = self.total(0, s, start, size) + self.rx[s, at].astype(f32) + self.ry[s, at].astype(f32)
            if i < self.count - 1:
                d = self.place(0, s)
                self.gp[d, at] = mine.astype(bf16)
                self.push(self.z, (g, i), self.gp.at[d, rows], self.rz.at[i, rows], (self.dp, s))
            else:
                self.out[at] = mine

    def final(self, g):
        start, n1, n2, _ = PARTS[g]
        size = n1 + n2
        at = slice(start, start + size)
        mine = self.out[at]
        for i in range(self.count - 1):
            self.take(self.z, (g, i), self.rz.at[i, pl.ds(start, size)])
            mine = mine + self.rz[i, at].astype(f32)
        self.out[at] = mine
        self.momentum.send(g)

    def small_core(self):
        rows, lanes = pl.ds(SMALL, ROWS), pl.ds(0, TINY)
        for k in (3, 1, 2, 0):
            src = self.gp.at[pl.ds(self.place((0, X, Y, X + Y)[k] + CORE, 0), self.count), rows, lanes]
            self.push(self.c, (2, k), src, self.rc.at[k, :, rows, lanes], self.flip(CORE))

    def small_send(self):
        for k in (3, 1, 2, 0):
            mask = (0, X, Y, X + Y)[k]
            self.take(self.c, (2, k), self.rc.at[k, :, pl.ds(SMALL, ROWS), pl.ds(0, TINY)])
            for i, s in enumerate(self.order):
                d = self.place(mask, s)
                own = self.gp[d, SMALL:PACK, 0:TINY].astype(f32)
                made = own + self.rc[k, s, SMALL:PACK, 0:TINY].astype(f32)
                if k == 0 and i == self.count - 1:
                    self.out[SMALL:PACK, 0:TINY] = made
                else:
                    self.gp[d, SMALL:PACK, 0:TINY] = made.astype(bf16)
                    src = self.gp.at[d, pl.ds(SMALL, ROWS), pl.ds(0, TINY)]
                    copy = remote(
                        src, self.tin.at[k, self.p], self.t[0].at[k, s], self.t[1].at[k, self.p],
                        (jnp.bitwise_xor(self.dp, mask), s),
                    )
                    copy.start()
                    self.sent.append(copy)

    def small_final(self):
        mine = self.out[SMALL:PACK, 0:TINY]
        for k in range(4):
            for i, s in enumerate(self.order):
                if not (k == 0 and i == self.count - 1):
                    self.take(self.t, (k, s), self.tin.at[k, s])
                    mine = mine + self.tin[k, s].astype(f32)
        self.out[SMALL:PACK, 0:TINY] = mine
        self.out[SMALL:PACK, TINY:] = jnp.zeros((ROWS, self.out.shape[1] - TINY), f32)
        self.momentum.send(2)

    def early(self):
        self.momentum.early()

    def late(self):
        self.momentum.late()
        self.momentum.work()

    def finish(self):
        for copy in self.sent:
            copy.wait_send()


class NoSums:
    def __init__(self):
        self.core = self.diagonal = self.sides = self.final = lambda g: None
        self.owners = lambda g, turns=None: None
        self.finish = self.small_core = self.small_send = self.small_final = self.early = self.late = lambda: None


def step(gather, sums, clips, ins, outs, scratch, wp, tiny, gp):
    frames_h, valid_ref, memory_h, ctm_h, ctr_ref = ins
    nm_h, ro_ref, gf_h, gm_h = outs
    (
        zm, zf, ctm, table, gain, bias, lw_m, lw_f, dw_m, dw_f, lr_m, lr_f, ar_m, ar_f, rm_s, rf_s, stat,
        summary, queries, keys, values, probs, context, after, normed, normed_mlp, spare, activ, gafter, d_fed_s, gsum,
        acc_w, acc_r, joined, raw, in_sem, out_sem, raw_sem,
    ) = scratch
    mem, read = memory_h.shape[1], ROWS
    toks = zf.shape[1]
    rows = clips * read
    groups = wp.shape[0]
    width = zm.shape[2]
    wide = mem + read
    mean_of = 1.0 / width

    def in_copies(c):
        return (
            pltpu.make_async_copy(memory_h.at[c], zm.at[c], in_sem.at[0, c]),
            pltpu.make_async_copy(ctm_h.at[c], ctm.at[c], in_sem.at[1, c]),
        )

    def out_copies(c):
        return (
            pltpu.make_async_copy(ctm.at[c], nm_h.at[c], out_sem.at[0, c]),
            pltpu.make_async_copy(zm.at[c], gm_h.at[c], out_sem.at[1, c]),
        )

    chunk = raw.shape[1] // clips
    chunks = [(t, min(chunk, toks - t)) for t in range(0, toks, chunk)]
    tiles = width // 128

    def raw_copy(i, out=False):
        t, n = chunks[i]
        here, there = raw.at[i % 2, pl.ds(0, n * clips)], pl.ds(t * clips, n * clips)
        if out:
            return pltpu.make_async_copy(here, gf_h.at[there], raw_sem.at[i])
        return pltpu.make_async_copy(frames_h.at[there], here, raw_sem.at[i])

    for i in range(min(2, len(chunks))):
        raw_copy(i).start()

    @pl.loop(0, clips)
    def _(c):
        for copy in in_copies(c):
            copy.start()

    def frames_in():
        for i, (t, n) in enumerate(chunks):
            raw_copy(i).wait()
            for q in range(tiles):
                spare[q, 0 : n * clips] = raw[i % 2, 0 : n * clips, 128 * q : 128 * (q + 1)].astype(f32)
            if i + 2 < len(chunks):
                raw_copy(i + 2).start()

            @pl.loop(0, clips)
            def _(c):
                for q in range(tiles):
                    zf[c, t : t + n, 128 * q : 128 * (q + 1)] = spare[
                        q, pl.ds(c, n, stride=clips)
                    ].astype(bf16)

    def frames_out():
        for i, (t, n) in enumerate(chunks):
            @pl.loop(0, clips)
            def _(c):
                for q in range(tiles):
                    spare[q, pl.ds(c, n, stride=clips)] = zf[
                        c, t : t + n, 128 * q : 128 * (q + 1)
                    ].astype(f32)

            if i >= 2:
                raw_copy(i - 2, True).wait()
            for q in range(tiles):
                raw[i % 2, 0 : n * clips, 128 * q : 128 * (q + 1)] = spare[q, 0 : n * clips].astype(bf16)
            raw_copy(i, True).start()

    def clip_loop(low, high, batch, body):
        @pl.loop(low // batch, high // batch)
        def _(i):
            lockstep([functools.partial(body, i * batch + k) for k in range(batch)])

    ones = jnp.ones((8, 128), bf16)
    place = lax.broadcasted_iota(jnp.int32, (mem, 8), 1)

    def unit_rows(z):
        square = z * z
        folded = (square[:, 0:128] + square[:, 128:256]) + (square[:, 256:384] + square[:, 384:512])
        return lax.rsqrt(dot(ones, folded, 1, 1) * mean_of + NORM_EPS)

    def rows_of(c):
        return pl.ds(pl.multiple_of(c * read, read), read)

    def ahead(c):
        for copy in in_copies(c):
            copy.wait()
        z_m, z_f, g = zm[c], zf[c], ctm[c]
        yield
        r_m, r_f = unit_rows(z_m), unit_rows(z_f)
        yield
        d_m, d_f = dot(g, z_m, 1, 1), dot(g, z_f, 1, 1)
        yield
        rm_s[c], rf_s[c] = r_m, r_f
        dw_m[c], dw_f[c] = d_m.astype(bf16), d_f.astype(bf16)

    def reading(c):
        z_m, z_f, r_m, r_f = zm[c], zf[c], rm_s[c], rf_s[c]
        d_m, d_f = dw_m[c].astype(f32), dw_f[c].astype(f32)
        live = valid_ref[pl.ds(c, 1), :] > 0
        tab = table[...]
        yield
        u_m, u_f = dot(tab, z_m, 1, 1), dot(tab, z_f, 1, 1)
        yield
        l_m = u_m * r_m[0:1]
        l_f = jnp.where(live, u_f * r_f[0:1], MASKED)
        top = jnp.maximum(jnp.max(l_m, axis=1, keepdims=True), jnp.max(l_f, axis=1, keepdims=True))
        yield
        e_m, e_f = jnp.exp(l_m - top), jnp.exp(l_f - top)
        total = jnp.sum(e_m, axis=1, keepdims=True) + jnp.sum(e_f, axis=1, keepdims=True)
        inv = 1.0 / total[mem:]
        a_m, a_f = e_m[mem:] * inv, e_f[mem:] * inv
        yield
        a_m, a_f = a_m.astype(bf16), a_f.astype(bf16)
        made = dot(a_m, z_m) + dot(a_f, z_f)
        moved = jnp.sum(e_m[0:mem] * d_m, axis=1, keepdims=True) + jnp.sum(
            e_f[0:mem] * d_f, axis=1, keepdims=True
        )
        yield
        lw_m[c], lw_f[c] = l_m[0:mem], l_f[0:mem]
        lr_m[c], lr_f[c] = l_m[mem:].astype(bf16), l_f[mem:].astype(bf16)
        ar_m[c], ar_f[c] = a_m, a_f
        stat[c] = jnp.where(
            place == 0, top[0:mem], jnp.where(place == 1, total[0:mem], moved)
        ).T
        summary[rows_of(c)] = made

    half = clips // 2
    third = clips // 3
    gather.start()
    frames_in()
    clip_loop(0, half, 2, ahead)
    gather.stage(0, 1)
    clip_loop(half, clips, 2, ahead)
    gather.tables()
    turned = tiny[:, :, 0:128].reshape(groups * ROWS, 128).astype(f32).T
    gain[...] = turned[112:120]
    table[0:mem] = (turned[0:mem] * turned[115:116]).astype(bf16)
    table[mem:wide] = (turned[mem:wide] * turned[112:113]).astype(bf16)
    piece = bias.shape[1] // groups
    for d in range(groups):
        bias[:, piece * d : piece * (d + 1)] = tiny[d, 0:1, 128 : 128 + piece].astype(f32)
    gather.stage(0, 2)
    clip_loop(0, third, 2, reading)
    gather.stage(0, 3)
    clip_loop(third, 2 * third, 2, reading)
    gather.stage(0, 4)
    clip_loop(2 * third, clips, 2, reading)
    gather.end(0)

    def mat(m):
        return wp[:, ROWS * m : ROWS * (m + 1)].reshape(groups * ROWS, width)

    per = groups // 4

    def out_mat(j):
        return wp[pl.ds(per * j, per), 128:192].reshape(width, width)

    def unit(v):
        return lax.rsqrt(jnp.mean(v * v, axis=-1, keepdims=True) + NORM_EPS)

    summ = summary[...]
    hidden = (summ * unit(summ) * gain[1:2]).astype(bf16)
    normed[...] = hidden
    queries[...] = dot(hidden, mat(0)).astype(bf16)
    keys[...] = dot(hidden, mat(1)).astype(bf16)
    values[...] = dot(hidden, mat(2)).astype(bf16)
    scale = HEAD_DIM**-0.5
    block = 128
    blocks = rows // block
    pairs = HEADS // 2
    row_clip = lax.broadcasted_iota(jnp.int32, (block, block), 0) // read
    col_clip = lax.broadcasted_iota(jnp.int32, (block, block), 1) // read
    same = row_clip == col_clip
    low_lane = lax.broadcasted_iota(jnp.int32, (block, block), 1) < HEAD_DIM

    def half_of(v, side):
        zero = jnp.zeros_like(v)
        return jnp.where(low_lane, v, zero) if side == 0 else jnp.where(low_lane, zero, v)

    def attend(b, pair):
        at = pl.ds(pl.multiple_of(b * block, block), block)
        lanes = slice(pair * block, (pair + 1) * block)
        q, k, v = queries[at, lanes], keys[at, lanes], values[at, lanes]
        yield
        scores = [dot(half_of(q, side), k, 1, 1) for side in range(2)]
        yield
        masked = [jnp.where(same, s * scale, MASKED) for s in scores]
        tops = [jnp.max(s, axis=1, keepdims=True) for s in masked]
        yield
        parts = [jnp.exp(s - top) for s, top in zip(masked, tops)]
        sums_ = [jnp.sum(e, axis=1, keepdims=True) for e in parts]
        yield
        made = [(e * (1.0 / s)).astype(bf16) for e, s in zip(parts, sums_)]
        got = [dot(p, v) for p in made]
        yield
        probs[b, 2 * pair], probs[b, 2 * pair + 1] = made
        context[at, lanes] = jnp.where(low_lane, got[0], got[1]).astype(bf16)

    @pl.loop(0, blocks)
    def _(b):
        lockstep([functools.partial(attend, b, pair) for pair in range(pairs)])

    aft = summary[...] + dot(context[...], mat(3))
    after[...] = aft
    fed = (aft * unit(aft) * gain[2:3]).astype(bf16)
    def columns(j):
        return pl.ds(pl.multiple_of(width * j, width), width)

    def rows_at(j):
        return pl.ds(pl.multiple_of(rows * j, rows), rows)

    def in_mat(j):
        return wp[:, pl.ds(pl.multiple_of(64 + ROWS * j, ROWS), ROWS)].reshape(groups * ROWS, width)

    normed_mlp[...] = fed

    @pl.loop(0, 4)
    def _(j):
        pre = dot(normed_mlp[...], in_mat(j)) + bias[:, columns(j)]
        square = pre * pre
        t = jnp.tanh(GELU_A * pre * (1.0 + GELU_B * square))
        most = 0.5 + 0.5 * t
        activ[0:rows, columns(j)] = (pre * most).astype(bf16)
        slope = most + (0.5 * GELU_A) * pre * (1.0 - t * t) * (1.0 + (3.0 * GELU_B) * square)
        for q in range(tiles):
            spare[q, rows_at(j)] = slope[:, 128 * q : 128 * (q + 1)]

    gather.finish()
    gafter[...] = after[...]

    @pl.loop(0, 4)
    def _(j):
        gafter[...] += dot(activ[0:rows, columns(j)], out_mat(j))

    out = gafter[...]
    ro_ref[...] = out.astype(bf16)

    many = block // read

    def joining(b):
        at = slice(block * b, block * (b + 1))
        ro, ctr = ro_ref[at], ctr_ref[at].astype(f32)
        gs = [ctm[many * b + i] for i in range(many)]
        now = stat[many * b : many * (b + 1)]
        tab = table[0:mem]
        yield
        ro_f = ro.astype(f32)
        r = unit(ro_f)
        l = dot(ro, tab, 1, 1) * r
        d = jnp.concatenate(
            [dot(ro[read * i : read * (i + 1)], g, 1, 1) for i, g in enumerate(gs)], axis=0
        )
        yield
        l_c, d_c = l.reshape(many, read, mem), d.reshape(many, read, mem)
        top, total, moved = now[:, 0:1], now[:, 1:2], now[:, 2:3]
        new_top = jnp.maximum(top, jnp.max(l_c, axis=1, keepdims=True))
        old, e = jnp.exp(top - new_top), jnp.exp(l_c - new_top)
        total = total * old + jnp.sum(e, axis=1, keepdims=True)
        moved = moved * old + jnp.sum(e * d_c, axis=1, keepdims=True)
        inv = 1.0 / total
        a, mean = e * inv, moved * inv
        b_all = (a * (d_c - mean)).reshape(block, mem)
        k = jnp.sum(b_all * l, axis=1, keepdims=True) * (r * r * mean_of)
        a_low = a.reshape(block, mem).astype(bf16)
        h_low = (b_all * r).astype(bf16)
        yield
        made = dot(h_low, tab) + jnp.concatenate(
            [dot(a_low[read * i : read * (i + 1)], g) for i, g in enumerate(gs)], axis=0
        )
        yield
        gafter[at] = made - ro_f * k + ctr
        joined[at, 0:mem], joined[at, 128 : 128 + mem] = a_low, h_low
        stat[many * b : many * (b + 1), 0:1] = new_top + jnp.log(total)
        stat[many * b : many * (b + 1), 1:2] = mean

    lockstep([functools.partial(joining, b) for b in range(blocks)])

    gsum[...] = gafter[...].astype(bf16)
    d_fed_s[...] = jnp.zeros_like(d_fed_s)

    @pl.loop(0, 4)
    def _(j):
        g_out, fed = gsum[...], normed_mlp[...]
        slope = jnp.concatenate([spare[q, rows_at(j)] for q in range(tiles)], axis=1)
        d_low = (dot(g_out, out_mat(j), 1, 1) * slope).astype(bf16)
        bias[:, columns(j)] = jnp.sum(d_low.astype(f32), axis=0, keepdims=True)
        gp[pl.ds(per * j, per), 128:192] = (
            dot(activ[0:rows, columns(j)], g_out, 0, 0).astype(bf16).reshape(per, 64, width)
        )
        gp[:, pl.ds(pl.multiple_of(64 + ROWS * j, ROWS), ROWS)] = (
            dot(fed, d_low, 0, 0).astype(bf16).reshape(groups, ROWS, width)
        )
        d_fed_s[...] += dot(d_low, in_mat(j), 1, 1)

    sums.core(0)
    aft = after[...]
    unit_aft = unit(aft)
    flat_aft = aft * unit_aft
    d_fed = d_fed_s[...]
    d_gain_mlp = jnp.sum(d_fed * flat_aft, axis=0, keepdims=True)
    d_flat = d_fed * gain[2:3]
    g_mid = gafter[...] + unit_aft * (
        d_flat - flat_aft * jnp.mean(d_flat * flat_aft, axis=-1, keepdims=True)
    )
    gafter[...] = g_mid
    g_low = g_mid.astype(bf16)
    gp[:, 3 * ROWS : 4 * ROWS] = (
        dot(context[...], g_low, 0, 0).astype(bf16).reshape(groups, ROWS, width)
    )
    context[...] = dot(g_low, mat(3), 1, 1).astype(bf16)
    sums.diagonal(0)

    def attend_back(b, pair):
        at = pl.ds(pl.multiple_of(b * block, block), block)
        lanes = slice(pair * block, (pair + 1) * block)
        q, k, v, dc = queries[at, lanes], keys[at, lanes], values[at, lanes], context[at, lanes]
        lows = (probs[b, 2 * pair], probs[b, 2 * pair + 1])
        ps = [p.astype(f32) for p in lows]
        yield
        dps = [dot(half_of(dc, side), v, 1, 1) for side in range(2)]
        dvs = [dot(p, dc, 0, 0) for p in lows]
        yield
        means = [jnp.sum(dp * p, axis=1, keepdims=True) for dp, p in zip(dps, ps)]
        yield
        lows = [(scale * p * (dp - m)).astype(bf16) for p, dp, m in zip(ps, dps, means)]
        dqs = [dot(low, k) for low in lows]
        dks = [dot(low, q, 0, 0) for low in lows]
        yield
        queries[at, lanes] = jnp.where(low_lane, dqs[0], dqs[1]).astype(bf16)
        keys[at, lanes] = jnp.where(low_lane, dks[0], dks[1]).astype(bf16)
        values[at, lanes] = jnp.where(low_lane, dvs[0], dvs[1]).astype(bf16)

    @pl.loop(0, blocks)
    def _(b):
        lockstep([functools.partial(attend_back, b, pair) for pair in range(pairs)])

    hidden = normed[...]
    d_hid = jnp.zeros((rows, width), f32)
    for m, g in enumerate((queries, keys, values)):
        g_now = g[...]
        gp[:, ROWS * m : ROWS * (m + 1)] = (
            dot(hidden, g_now, 0, 0).astype(bf16).reshape(groups, ROWS, width)
        )
        d_hid = d_hid + dot(g_now, mat(m), 1, 1)
    sums.core(1)
    summ = summary[...]
    unit_sum = unit(summ)
    flat_sum = summ * unit_sum
    d_gain_attn = jnp.sum(d_hid * flat_sum, axis=0, keepdims=True)
    d_flat = d_hid * gain[1:2]
    gsum[...] = (
        gafter[...]
        + unit_sum * (d_flat - flat_sum * jnp.mean(d_flat * flat_sum, axis=-1, keepdims=True))
    ).astype(bf16)
    sums.sides(0)
    sums.diagonal(1)

    acc_w[...] = jnp.zeros_like(acc_w)
    acc_r[...] = jnp.zeros_like(acc_r)

    def closing(c):
        z_m, z_f, g, gr = zm[c], zf[c], ctm[c], gsum[rows_of(c)]
        ro, pair = ro_ref[rows_of(c)], joined[rows_of(c)]
        r_m, r_f, l_m, l_f = rm_s[c, 0:1], rf_s[c, 0:1], lw_m[c], lw_f[c]
        d_m, d_f = dw_m[c].astype(f32), dw_f[c].astype(f32)
        q_m, q_f, a_m, a_f = (v[c].astype(f32) for v in (lr_m, lr_f, ar_m, ar_f))
        now = stat[c].T
        lse, mean = now[:, 0:1], now[:, 1:2]
        tab = table[...]
        yield
        x_m, x_f = dot(gr, z_m, 1, 1), dot(gr, z_f, 1, 1)
        w_m, w_f = jnp.exp(l_m - lse), jnp.exp(l_f - lse)
        yield
        b_m, b_f = w_m * (d_m - mean), w_f * (d_f - mean)
        k_m = jnp.sum(b_m * l_m, axis=0, keepdims=True)
        k_f = jnp.sum(b_f * l_f, axis=0, keepdims=True)
        mean_r = jnp.sum(x_m * a_m, axis=1, keepdims=True) + jnp.sum(x_f * a_f, axis=1, keepdims=True)
        yield
        c_m, c_f = a_m * (x_m - mean_r), a_f * (x_f - mean_r)
        k_m = (k_m + jnp.sum(c_m * q_m, axis=0, keepdims=True)) * (r_m * r_m * mean_of)
        k_f = (k_f + jnp.sum(c_f * q_f, axis=0, keepdims=True)) * (r_f * r_f * mean_of)
        left_m = jnp.concatenate([w_m, b_m * r_m, a_m, c_m * r_m], axis=0).astype(bf16)
        left_f = jnp.concatenate([w_f, b_f * r_f, a_f, c_f * r_f], axis=0).astype(bf16)
        yield
        made = dot(left_m, z_m) + dot(left_f, z_f)
        joins = (dot(pair[:, 0:mem], ro, 0, 0), dot(pair[:, 128 : 128 + mem], ro, 0, 0))
        back = jnp.concatenate([g, tab[0:mem], gr, tab[mem:]], axis=0)
        t_m = jnp.broadcast_to(k_m, (8, mem)).T
        t_f = jnp.broadcast_to(k_f, (8, toks)).T
        yield
        dz_m = dot(left_m, back, 0, 0) - z_m.astype(f32) * t_m[:, 0:1]
        dz_f = dot(left_f, back, 0, 0) - z_f.astype(f32) * t_f[:, 0:1]
        yield
        ctm[c] = (made[0:mem] + joins[0]).astype(bf16)
        acc_w[...] += made[mem : 2 * mem] + joins[1]
        acc_r[...] += made[2 * mem + read :]
        zm[c], zf[c] = dz_m.astype(bf16), dz_f.astype(bf16)
        for copy in out_copies(c):
            copy.start()

    at_clips = [0, *(clips * part // 12 for part in (4, 7, 10, 12))]
    for turn in range(4):
        clip_loop(at_clips[turn], at_clips[turn + 1], 2, closing)
        sums.owners(0, [turn])
    sums.sides(1)

    zero_rows = jnp.zeros((1, width), f32)
    rest = jnp.concatenate(
        [zero_rows, d_gain_attn, d_gain_mlp, zero_rows, jnp.zeros((12, width), f32)], axis=0
    )
    stacked = jnp.concatenate([acc_w[...], acc_r[...], rest], axis=0)
    gp[:, SMALL:PACK] = jnp.zeros((groups, ROWS, width), bf16)
    gp[:, SMALL:PACK, 0:128] = stacked.T.astype(bf16).reshape(groups, ROWS, 128)
    for d in range(groups):
        gp[d, SMALL : SMALL + 1, 128 : 128 + piece] = bias[:, piece * d : piece * (d + 1)].astype(bf16)
    sums.small_core()
    sums.final(0)
    sums.small_send()
    frames_out()
    sums.owners(1)
    sums.final(1)
    sums.small_final()
    sums.early()
    sums.late()

    @pl.loop(0, clips)
    def _(c):
        for copy in out_copies(c):
            copy.wait()

    for i in range(max(0, len(chunks) - 2), len(chunks)):
        raw_copy(i, True).wait()
    sums.finish()


def step_scratch(clips, toks, mem, read, width):
    vm, sem = pltpu.VMEM, pltpu.SemaphoreType.DMA
    rows, wide = clips * read, mem + read
    return [
        vm((clips, mem, width), bf16),
        vm((clips, toks, width), bf16),
        vm((clips, mem, width), bf16),
        vm((wide, width), bf16),
        vm((8, width), f32),
        vm((1, 4 * width), f32),
        vm((clips, mem, mem), f32),
        vm((clips, mem, toks), f32),
        vm((clips, mem, mem), bf16),
        vm((clips, mem, toks), bf16),
        vm((clips, read, mem), bf16),
        vm((clips, read, toks), bf16),
        vm((clips, read, mem), bf16),
        vm((clips, read, toks), bf16),
        vm((clips, 8, mem), f32),
        vm((clips, 8, toks), f32),
        vm((clips, 8, mem), f32),
        vm((rows, width), f32),
        vm((rows, width), bf16),
        vm((rows, width), bf16),
        vm((rows, width), bf16),
        vm((rows // 128, HEADS, 128, 128), bf16),
        vm((rows, width), bf16),
        vm((rows, width), f32),
        vm((rows, width), bf16),
        vm((rows, width), bf16),
        vm((width // 128, 4 * max(rows, width), 128), f32),
        vm((max(rows, width), 4 * width), bf16),
        vm((rows, width), f32),
        vm((rows, width), f32),
        vm((rows, width), bf16),
        vm((mem, width), f32),
        vm((read, width), f32),
        vm((rows, 256), bf16),
        vm((2, 16 * clips, width), bf16),
        sem((2, clips)),
        sem((2, clips)),
        sem((-(-toks // 16),)),
    ]


def plain_kernel(clips, *refs):
    ins, wpack_h, outs, gp = refs[0:5], refs[5], refs[6:10], refs[10]
    wp, tiny, sems = refs[11:14]
    step(Load(wpack_h, wp, tiny, sems), NoSums(), clips, ins, outs, refs[14:], wp, tiny, gp)


def whole_kernel(clips, *refs):
    weights, ins, state = refs[0:7], refs[7:12], refs[12:18]
    outs, red, xrec = refs[18:22], refs[22], refs[23]
    refs = refs[24:]
    wp, tiny, gp = refs[0:3]
    gather_refs, refs = refs[3:21], refs[21:]
    sum_refs, refs = refs[0:21], refs[21:]
    muon_refs, refs = refs[0:8], refs[8:]
    gather = Gather(weights, wp, tiny, *gather_refs)
    muon = Muon(red, state, xrec, *muon_refs, refs[26], refs[27])
    step(gather, Sums(muon, gp, red, *sum_refs), clips, ins, outs, refs, wp, tiny, gp)
    muon.finish()


def run_step(frames, valid, memory, ct_memory, ct_read, wpack=None, weights=(), state=()):
    clips, toks, width = frames.shape
    mem, read = memory.shape[1], ct_read.shape[1]
    groups, rows = width // ROWS, clips * read
    vm, sem, made = pltpu.VMEM, pltpu.SemaphoreType.DMA, jax.ShapeDtypeStruct
    hbm = pl.BlockSpec(memory_space=pl.ANY)
    inside = pl.BlockSpec(memory_space=pltpu.VMEM)
    out_shape = [
        made(memory.shape, bf16), made((rows, width), bf16), made((toks * clips, width), bf16), made(memory.shape, bf16),
    ]
    out_specs = [hbm, inside, hbm, hbm]
    in_specs = [hbm, inside, hbm, hbm, inside]
    frames = frames.transpose(1, 0, 2).reshape(toks * clips, width)
    operands = [frames, valid, memory, ct_memory, ct_read.reshape(rows, width)]
    scratch = [vm((groups, SMALL, width), bf16), vm((groups, ROWS, TINY), bf16)]
    params = dict(vmem_limit_bytes=VMEM_LIMIT)
    if weights:
        n = lax.axis_size("sub")
        kernel = whole_kernel
        operands = [*weights, *operands, *state]
        in_specs = [inside] * len(weights) + in_specs + [inside] * len(state)
        out_shape += [made((PACK, width), f32), made((PACK, width), bf16)]
        out_specs += [inside, inside]
        scratch += [
            vm((groups, PACK, width), bf16),
            vm((SMALL, width), bf16), vm((ROWS, TINY), bf16), sem, sem, sem((len(GATHERED) + 1,)),
            *[sem((len(GATHERED), n))] * 2, *[sem((len(GATHERED),))] * 4, sem((len(GATHERED), 4)),
            *[sem((len(GATHERED), n))] * 3, *[sem((len(GATHERED),))] * 2, sem((len(GATHERED), 4)),
            vm((4, n, PACK, width), bf16),
            vm((n, 112, width), bf16),
            vm((n, 96, width), bf16),
            vm((n, PACK, width), bf16),
            vm((n, PACK, width), bf16),
            vm((n - 1, PACK, width), bf16),
            vm((4, n, ROWS, TINY), bf16),
            *[sem((3, 4))] * 2, *[sem((2, n))] * 8, *[sem((2, n - 1))] * 2, *[sem((4, n))] * 2,
            vm((PACK, width), bf16), vm((groups, 64, width), bf16), sem((len(OWNERS),)), sem((groups,)), sem,
            sem((groups,)), sem((len(OWNERS),)), sem,
        ]
        params.update(collective_id=1, has_side_effects=True)
    else:
        kernel = plain_kernel
        operands.append(wpack)
        in_specs.append(hbm)
        out_shape.append(made((groups, PACK, width), bf16))
        out_specs.append(inside)
        scratch.append(sem((2,)))
    outs = pl.pallas_call(
        functools.partial(kernel, clips),
        out_shape=tuple(out_shape),
        in_specs=in_specs,
        out_specs=tuple(out_specs),
        scratch_shapes=scratch + step_scratch(clips, toks, mem, read, width),
        compiler_params=pltpu.CompilerParams(**params),
        name="clip_step",
    )(*operands)
    return outs


def clip_outputs(outs, clips):
    new_memory, read_out, by_token, grad_memory = outs
    width = by_token.shape[1]
    frames = by_token.reshape(-1, clips, width).transpose(1, 0, 2)
    return new_memory, read_out.reshape(clips, ROWS, width), frames, grad_memory


OWNERS = ((2, 0), (4, 3), (2, 3), (4, 0), (0, 1), (6, 2), (0, 3))
PIECES = ((0, 16), (16, 16), (32, 16), (48, 16), (64, 64), (128, 64), (192, 16))


def is_owner(m):
    return (lax.axis_index("dp") == OWNERS[m][0]) & (lax.axis_index("sub") == OWNERS[m][1])


def small_grads(red, gains_t):
    return (
        red[SMALL:PACK, 0:96] * gains_t[:, 3:4],
        red[SMALL:PACK, 96:112] * gains_t[:, 0:1],
    )


def exact_dot(a, b, ca=1, cb=0):
    return lax.dot_general(a, b, (((ca,), (cb,)), ((), ())), preferred_element_type=f32, precision=highest)


def iterate_small(x, same):
    norm = jnp.sum(x * x, axis=1, keepdims=True)
    total = jnp.sum(jnp.where(same, norm.T, 0.0), axis=1, keepdims=True)
    x = x * (1.0 / (jnp.sqrt(total) + 1e-07))
    for _ in range(5):
        q = jnp.where(same, exact_dot(x, x, 1, 1), 0.0)
        mixed = NS[1] * q + NS[2] * exact_dot(q, q)
        x = NS[0] * x + exact_dot(mixed, x)
    return x


class Muon:
    def __init__(self, acc, state, xrec, pk, buf, gsend, grecv, gown, ssend, srecv, sown, x, low):
        self.__dict__.update(
            acc=acc, state=state, xrec=xrec, pk=pk, buf=buf, gsend=gsend, grecv=grecv, gown=gown,
            ssend=ssend, srecv=srecv, sown=sown, x=x, low=low,
        )
        self.count = lax.axis_size("sub")
        self.me = lax.axis_index("dp") * self.count + lax.axis_index("sub")
        self.groups = buf.shape[0]

    def piece(self, m):
        start, size = PIECES[m]
        return self.pk.at[pl.ds(start, size)], self.buf.at[self.me, pl.ds(0, size)]

    def away(self, m):
        return remote(*self.piece(m), self.gsend.at[m], self.grecv.at[self.me], OWNERS[m])

    def home(self, m):
        return pltpu.make_async_copy(*self.piece(m), self.gown)

    def send(self, part):
        attn_mom, w_in_mom, w_out_mom, s_read_mom, s_write_mom, gains = self.state
        acc, pk = self.acc, self.pk
        width = acc.shape[1]
        if part == 0:
            for m in range(4):
                at = slice(64 + ROWS * m, 64 + ROWS * (m + 1))
                pk[at] = (0.5 * w_in_mom[:, width * m : width * (m + 1)] + acc[at]).astype(bf16)
            pk[128:192] = (0.5 * w_out_mom[...] + acc[128:192]).astype(bf16)
        elif part == 1:
            for m in range(4):
                at = slice(ROWS * m, ROWS * (m + 1))
                pk[at] = (0.5 * attn_mom[m] + acc[at]).astype(bf16)
        else:
            g_write, g_read = small_grads(acc, turn_gains(gains[...]))
            pk[SMALL:PACK] = jnp.zeros((ROWS, width), bf16)
            pk[SMALL:PACK, 0:96] = (0.5 * s_write_mom[...] + g_write).astype(bf16)
            pk[SMALL:PACK, 96:112] = (0.5 * s_read_mom[...] + g_read).astype(bf16)
        for m in ((4, 5), (0, 1, 2, 3), (6,))[part]:

            @pl.when(jnp.logical_not(is_owner(m)))
            def _():
                self.away(m).start()

            @pl.when(is_owner(m))
            def _():
                self.home(m).start()

    def each_other(self, act):
        @pl.loop(0, self.groups)
        def _(d):
            @pl.when(d != self.me)
            def _():
                act(d)

    def whole(self, m):
        def take(d):
            got = self.buf.at[d, pl.ds(0, PIECES[m][1])]
            remote(got, got, self.grecv.at[d], self.grecv.at[d], OWNERS[m]).wait_recv()

        self.each_other(take)
        self.home(m).wait()

    def row_copy(self, m, d):
        start, size = PIECES[m]
        return remote(
            self.buf.at[d, pl.ds(0, size)], self.xrec.at[pl.ds(start, size)], self.ssend.at[d], self.srecv.at[m],
            (d // self.count, lax.rem(d, self.count)),
        )

    def row_home(self, m):
        start, size = PIECES[m]
        return pltpu.make_async_copy(
            self.buf.at[self.me, pl.ds(0, size)], self.xrec.at[pl.ds(start, size)], self.sown
        )

    def spread(self, m):
        self.each_other(lambda d: self.row_copy(m, d).start())
        self.row_home(m).start()

    def spread_wait(self, m):
        self.each_other(lambda d: self.row_copy(m, d).wait_send())
        self.row_home(m).wait()

    def put(self, j, value):
        n = value.shape[0]
        for q in range(value.shape[1] // 128):
            self.x[q, n * j : n * (j + 1)] = value[:, 128 * q : 128 * (q + 1)]

    def get(self, j, n):
        return jnp.concatenate([self.x[q, n * j : n * (j + 1)] for q in range(self.x.shape[0])], axis=1)

    def iterate(self, blocks, n):
        low = self.low
        total = jnp.zeros((1, 1), f32)
        for j in range(blocks):
            now = self.get(j, n)
            total = total + jnp.sum(now * now, keepdims=True)
        scale = 1.0 / (jnp.sqrt(total) + 1e-07)
        for j in range(blocks):
            now = self.get(j, n) * scale
            self.put(j, now)
            low[0:n, n * j : n * (j + 1)] = now.astype(bf16)

        self.sweep(blocks, n, 3)

    def sweep(self, blocks, n, times):
        low = self.low

        def block(j):
            return low[0:n, n * j : n * (j + 1)]

        @pl.loop(0, times)
        def _(_):
            q = dot(block(0), block(0), 1, 1)
            for j in range(1, blocks):
                q = q + dot(block(j), block(j), 1, 1)
            q_low = q.astype(bf16)
            mixed = (NS[1] * q + NS[2] * dot(q_low, q_low)).astype(bf16)
            for j in range(blocks):
                new = NS[0] * self.get(j, n) + dot(mixed, block(j))
                self.put(j, new)
                low[0:n, n * j : n * (j + 1)] = new.astype(bf16)

    def early(self):
        buf, groups = self.buf, self.groups
        width = buf.shape[2]
        per = groups // 4

        @pl.when(is_owner(4))
        def _():
            self.whole(4)
            for j in range(4):
                self.put(j, buf[:, ROWS * j : ROWS * (j + 1)].reshape(width, width).astype(f32))

        @pl.when(is_owner(5))
        def _():
            self.whole(5)
            for j in range(4):
                self.put(j, buf[per * j : per * (j + 1)].reshape(width, width).astype(f32).T)

        @pl.when(is_owner(4) | is_owner(5))
        def _():
            self.iterate(4, width)

    def late(self):
        buf, groups = self.buf, self.groups
        width = buf.shape[2]
        per = groups // 4

        @pl.when(is_owner(4) | is_owner(5))
        def _():
            self.sweep(4, width, 2)

        @pl.when(is_owner(4))
        def _():
            for j in range(4):
                buf[:, ROWS * j : ROWS * (j + 1)] = self.low[0:width, width * j : width * (j + 1)].reshape(
                    groups, ROWS, width
                )
            self.spread(4)

        @pl.when(is_owner(5))
        def _():
            for j in range(4):
                buf[per * j : per * (j + 1)] = self.get(j, width).T.astype(bf16).reshape(per, 64, width)
            self.spread(5)

    def work(self):
        buf, groups = self.buf, self.groups
        width = buf.shape[2]
        for m in range(4):

            @pl.when(is_owner(m))
            def _():
                self.whole(m)

        @pl.when(is_owner(0) | is_owner(1) | is_owner(2) | is_owner(3))
        def _():
            self.put(0, buf[:, 0:ROWS].reshape(width, width).astype(f32))
            self.iterate(1, width)
            self.sweep(1, width, 2)
            buf[:, 0:ROWS] = self.low[0:width, 0:width].reshape(groups, ROWS, width)

        for m in range(4):

            @pl.when(is_owner(m))
            def _():
                self.spread(m)

        @pl.when(is_owner(6))
        def _():
            self.whole(6)
            table = buf[:, 0:ROWS, 0:128].reshape(width, 128).astype(f32).T
            row = lax.broadcasted_iota(jnp.int32, (128, 128), 0)
            col = lax.broadcasted_iota(jnp.int32, (128, 128), 1)
            same = ((row < 96) & (col < 96)) | ((row >= 96) & (col >= 96))
            made = iterate_small(table, same)
            buf[:, 0:ROWS, 0:128] = made.T.astype(bf16).reshape(groups, ROWS, 128)
            self.spread(6)

    def finish(self):
        many = range(len(OWNERS))
        for m in many:

            @pl.when(jnp.logical_not(is_owner(m)))
            def _():
                self.away(m).wait_send()
                start, size = PIECES[m]
                got = self.xrec.at[pl.ds(start, size)]
                remote(got, got, self.srecv.at[m], self.srecv.at[m], OWNERS[m]).wait_recv()

            @pl.when(is_owner(m))
            def _():
                self.spread_wait(m)


def finish_kernel(
    red, xrec, attn, w_in, w_out, s_read, s_write, attn_mom, w_in_mom, w_out_mom, s_read_mom, s_write_mom,
    gains, gains_first, gains_second, bias, bias_first, bias_second, nm_in, ro_in, gf_in, gm_in,
    nm, ro, gf, gm, g_attn, g_in, g_out, g_read, g_write, g_gains, g_bias,
    n_attn, n_in, n_out, n_read, n_write, n_gains, n_bias, m_attn, m_in, m_out, m_read, m_write,
    n_gains_first, n_gains_second, n_bias_first, n_bias_second, sems, *stages,
):
    width = red.shape[1]
    ins, outs = [], []
    for src, stage, dst, cuts in zip((gf_in, nm_in, gm_in, ro_in), stages, (gf, nm, gm, ro), (3, 2, 2, 1)):
        size = src.shape[0] // cuts
        for i in range(cuts):
            at, k = pl.ds(size * i, size), len(ins)
            ins.append(pltpu.make_async_copy(src.at[at], stage.at[at], sems.at[0, k]))
            outs.append(pltpu.make_async_copy(stage.at[at], dst.at[at], sems.at[1, k]))
            ins[k].start()

    def pass_on(first, last):
        for k in range(first, last):
            ins[k].wait()
            outs[k].start()

    for m in range(4):
        lanes = slice(width * m, width * (m + 1))
        at = slice(ROWS * m, ROWS * (m + 1))
        g = red[at]
        g_attn[m] = g
        m_attn[m] = 0.5 * attn_mom[m] + g
        n_attn[m] = attn[m] - xrec[at].astype(f32)
        at = slice(64 + ROWS * m, 64 + ROWS * (m + 1))
        g = red[at]
        g_in[:, lanes] = g
        m_in[:, lanes] = 0.5 * w_in_mom[:, lanes] + g
        n_in[:, lanes] = w_in[:, lanes] - xrec[at].astype(f32)
        pass_on(m, m + 1)
    g = red[128:192]
    g_out[...] = g
    m_out[...] = 0.5 * w_out_mom[...] + g
    n_out[...] = w_out[...] - 2.0 * xrec[128:192].astype(f32)
    pass_on(4, len(ins))
    small = xrec[SMALL:PACK, 0:128].astype(f32)
    n_write[...] = s_write[...] - math.sqrt(512 / 96) * small[:, 0:96]
    n_read[...] = s_read[...] - math.sqrt(512 / 16) * small[:, 96:112]
    made_write, made_read = small_grads(red, turn_gains(gains[...]))
    g_write[...] = made_write
    g_read[...] = made_read
    m_write[...] = 0.5 * s_write_mom[...] + made_write
    m_read[...] = 0.5 * s_read_mom[...] + made_read
    low_write = s_write[...].astype(bf16).astype(f32)
    low_read = s_read[...].astype(bf16).astype(f32)
    to_read = jnp.sum(low_read * red[SMALL:PACK, 96:112], axis=1, keepdims=True)
    to_write = jnp.sum(low_write * red[SMALL:PACK, 0:96], axis=1, keepdims=True)
    column = lax.broadcasted_iota(jnp.int32, (ROWS, 128), 1)
    wide = jnp.where(
        column == 112, to_read, jnp.where(column == 115, to_write, red[SMALL:PACK, 0:128])
    )
    grad_gains = wide.T[112:116]
    g_gains[...] = grad_gains
    n_gains[...], n_gains_first[...], n_gains_second[...] = adam_step(
        gains[...], gains_first[...], gains_second[...], grad_gains
    )
    grad_bias = red[SMALL : SMALL + 1, 128:192]
    g_bias[...] = grad_bias
    n_bias[...], n_bias_first[...], n_bias_second[...] = adam_step(
        bias[...], bias_first[...], bias_second[...], grad_bias
    )
    for copy in outs:
        copy.wait()


highest = lax.Precision.HIGHEST
NS = (3.4445, -4.775, 2.0315)


def canonical(attn, w_in, w_out, s_read, s_write, gains, bias):
    width = attn.shape[2]
    groups = attn.shape[1] // ROWS
    a = attn.astype(bf16).reshape(4, groups, ROWS, width).transpose(1, 0, 2, 3)
    i = w_in.astype(bf16).reshape(groups, ROWS, 4, width).transpose(0, 2, 1, 3)
    o = w_out.astype(bf16).reshape(groups, 64, width)
    s = jnp.concatenate([s_write, s_read, gains.T], axis=1).astype(bf16)
    s = jnp.pad(s, ((0, 0), (0, 128 - s.shape[1]))).reshape(groups, ROWS, 128)
    b = bias.astype(bf16).reshape(groups, 1, 64)
    b = jnp.pad(b, ((0, 0), (0, ROWS - 1), (0, width - 128 - 64)))
    return jnp.concatenate(
        [
            a.reshape(groups, 64, width),
            i.reshape(groups, 64, width),
            o,
            jnp.concatenate([s, b], axis=2),
        ],
        axis=1,
    )


def natural(pack, mem, read):
    groups, _, width = pack.shape
    a = pack[:, 0:64].reshape(groups, 4, ROWS, width).transpose(1, 0, 2, 3)
    i = pack[:, 64:128].reshape(groups, 4, ROWS, width).transpose(0, 2, 1, 3)
    s = pack[:, SMALL:PACK, 0:128].reshape(groups * ROWS, 128)
    return (
        a.reshape(4, groups * ROWS, width),
        i.reshape(groups * ROWS, 4 * width),
        pack[:, 128:192].reshape(groups * 64, width),
        s[:, 0:mem],
        s[:, mem : mem + read],
        s[:, mem + read + 1 : mem + read + 3],
        pack[:, SMALL, 128:192].reshape(groups * 64),
    )


def adam_step(weight, first, second, grad):
    first_new = 0.5 * first + 0.5 * grad
    second_new = 0.5 * second + 0.5 * grad * grad
    part = 1.0 - 0.5**10
    moved = 0.25 * (first_new / part) / (jnp.sqrt(second_new / part) + 1e-08)
    return weight - moved, first_new, second_new


def orthogonalize(matrix):
    tall = matrix.shape[0] > matrix.shape[1]
    x = matrix.T if tall else matrix
    x = x / (jnp.sqrt(jnp.sum(x * x)) + 1e-07)
    for _ in range(5):
        q = jnp.dot(x, x.T, precision=highest)
        mixed = NS[1] * q + NS[2] * jnp.dot(q, q, precision=highest)
        x = NS[0] * x + jnp.dot(mixed, x, precision=highest)
    return x.T if tall else x


def any_slice(
    frames, valid, memory, ct_memory, ct_read,
    attn, w_in, w_out, s_read, s_write, gains, bias,
    attn_mom, w_in_mom, w_out_mom, s_read_mom, s_write_mom,
    gains_first, gains_second, bias_first, bias_second,
):
    axes = ("dp", "sub")
    mem, read = memory.shape[1], ct_read.shape[1]

    def gather(v, axis):
        return lax.all_gather(v.astype(bf16), axes, axis=axis, tiled=True)

    def scatter(v, axis):
        return lax.psum_scatter(v, axes, scatter_dimension=axis, tiled=True)

    wpack = canonical(
        gather(attn, 1), gather(w_in, 0), gather(w_out, 0), gather(s_read, 0),
        gather(s_write, 0), gather(gains, 1), gather(bias, 0),
    )
    *step_outs, gpack = run_step(frames, valid, memory, ct_memory, ct_read, wpack)
    new_memory, read_out, grad_frames, grad_memory = clip_outputs(step_outs, frames.shape[0])
    sums = natural(gpack.astype(f32), mem, read)
    g_attn, g_in, g_out, sum_w, sum_r, g_two, g_bias = (
        scatter(v, axis) for v, axis in zip(sums, (1, 0, 0, 0, 0, 0, 0))
    )
    low_gain = gains.astype(bf16).astype(f32)
    low_w, low_r = s_write.astype(bf16).astype(f32), s_read.astype(bf16).astype(f32)
    g_s_write = low_gain[3][:, None] * sum_w
    g_s_read = low_gain[0][:, None] * sum_r
    g_gains = jnp.stack(
        [jnp.sum(low_r * sum_r, axis=1), g_two[:, 0], g_two[:, 1], jnp.sum(low_w * sum_w, axis=1)]
    )
    moms = (
        0.5 * attn_mom + g_attn,
        0.5 * w_in_mom + g_in,
        0.5 * w_out_mom + g_out,
        0.5 * s_read_mom + g_s_read,
        0.5 * s_write_mom + g_s_write,
    )
    whole = [gather(v, axis).astype(f32) for v, axis in zip(moms, (1, 0, 0, 0, 0))]
    matrices = [whole[0][m] for m in range(4)] + whole[1:]
    rank, count = lax.axis_index(axes), lax.axis_size(axes)
    owned = [
        lax.cond(rank == m * count // 8, orthogonalize, jnp.zeros_like, matrix)
        for m, matrix in enumerate(matrices)
    ]
    ortho = (
        scatter(jnp.stack(owned[:4]), 1), *(scatter(v, 0) for v in owned[4:])
    )
    stepped = []
    for weight, part, full in zip((attn, w_in, w_out, s_read, s_write), ortho, whole):
        ratio = max(1.0, full.shape[-2] / full.shape[-1]) ** 0.5
        stepped.append(weight - ratio * part)
    n_gains = adam_step(gains, gains_first, gains_second, g_gains)
    n_bias = adam_step(bias, bias_first, bias_second, g_bias)
    return (
        new_memory, read_out, grad_frames, grad_memory,
        g_attn, g_in, g_out, g_s_read, g_s_write, g_gains, g_bias,
        *stepped, n_gains[0], n_bias[0], *moms, n_gains[1], n_gains[2], n_bias[1], n_bias[2],
    )


def this_slice(
    frames, valid, memory, ct_memory, ct_read,
    attn, w_in, w_out, s_read, s_write, gains, bias,
    attn_mom, w_in_mom, w_out_mom, s_read_mom, s_write_mom,
    gains_first, gains_second, bias_first, bias_second,
):
    inside, anywhere = pl.BlockSpec(memory_space=pltpu.VMEM), pl.BlockSpec(memory_space=pl.ANY)

    def like(*arrays):
        return tuple(jax.ShapeDtypeStruct(a.shape, f32) for a in arrays)

    def row(v):
        return v.reshape(1, -1)

    moms = (attn_mom, w_in_mom, w_out_mom, s_read_mom, s_write_mom)
    weights = (attn, w_in, w_out, s_read, s_write)
    *step_outs, red, xrec = run_step(
        frames, valid, memory, ct_memory, ct_read, None, (*weights, gains, row(bias)), (*moms, gains)
    )
    biases = (row(bias), row(bias_first), row(bias_second))
    made = pl.pallas_call(
        finish_kernel,
        out_shape=(
            *(jax.ShapeDtypeStruct(v.shape, bf16) for v in step_outs),
            *like(*weights, gains, biases[0]),
            *like(*weights, gains, biases[0]),
            *like(*moms, gains, gains, biases[0], biases[0]),
        ),
        in_specs=[inside] * 18 + [anywhere] * 4,
        out_specs=(anywhere,) * 4 + (inside,) * 23,
        scratch_shapes=[
            pltpu.SemaphoreType.DMA((2, 9)), *(pltpu.VMEM(step_outs[i].shape, bf16) for i in (2, 0, 3, 1)),
        ],
        compiler_params=pltpu.CompilerParams(vmem_limit_bytes=VMEM_LIMIT),
        name="finish",
    )(red, xrec, *weights, *moms, gains, gains_first, gains_second, *biases, *step_outs)
    flat = bias.shape
    return tuple(
        v.reshape(flat) if v.shape == biases[0].shape else v
        for v in (*clip_outputs(made[:4], frames.shape[0]), *made[4:])
    )


def solution(mesh):
    both = ("dp", "sub")
    rows3, rows2, rows1 = P(both, None, None), P(both, None), P(both)
    mid, last = P(None, both, None), P(None, both)
    weights = (mid, rows2, rows2, rows2, rows2)
    here = (mesh.shape["dp"], mesh.shape["sub"]) == (8, 4)
    return jax.shard_map(
        this_slice if here else any_slice,
        mesh=mesh,
        in_specs=(
            rows3, rows2, rows3, rows3, rows3, *weights, last, rows1, *weights, last, last, rows1, rows1,
        ),
        out_specs=(
            rows3, rows3, rows3, rows3, *weights, last, rows1, *weights, last, rows1, *weights,
            last, last, rows1, rows1,
        ),
        check_vma=False,
    )
```

```python
import functools
import math

import jax
import jax.numpy as jnp
from jax import lax
from jax.experimental import pallas as pl
from jax.experimental.pallas import tpu as pltpu
from jax.sharding import PartitionSpec as P

f32 = jnp.float32
bf16 = jnp.bfloat16
MESH = pl.DeviceIdType.MESH

HEADS = 8
HEAD_DIM = 64
NORM_EPS = 1e-06
MASKED = -1000000000.0
GELU_A = math.sqrt(2.0 / math.pi)
GELU_B = 0.044715
VMEM_LIMIT = 60 * 1024 * 1024

ROWS = 16
PACK = 208
SMALL = 192
TINY = 256
X, Y, CORE = 2, 4, 1
CROSSING = ((64, 64), (0, 64), (192, 16), (128, 64))
TOGETHER = (False, True)
PARTS = ((64, 64, 64, 0), (0, 32, 32, 64))


def dot(a, b, ca=1, cb=0):
    return lax.dot_general(a, b, (((ca,), (cb,)), ((), ())), preferred_element_type=f32)


def remote(src, dst, send, recv, device):
    return pltpu.make_async_remote_copy(
        src_ref=src, dst_ref=dst, send_sem=send, recv_sem=recv, device_id=device, device_id_type=MESH
    )


def lockstep(bodies):
    done = object()
    running = [body() for body in bodies]
    while running:
        running = [body for body in running if next(body, done) is not done]


def turn_gains(g):
    eye = (
        lax.broadcasted_iota(jnp.int32, (4, 4), 0) == lax.broadcasted_iota(jnp.int32, (4, 4), 1)
    ).astype(bf16)
    return dot(g.astype(bf16), eye, 0, 0)


GATHERED = ((0, 192),)


class Gather:
    def __init__(self, weights, out, tiny, x_ref, x_tiny, tsend, trecv, own_sem, up, down, sx, sy, fx, fy, sc, rz, rx, ry, rdx, rdy, rc):
        self.__dict__.update(
            weights=weights, out=out, tiny=tiny, x_ref=x_ref, x_tiny=x_tiny, tsend=tsend, trecv=trecv, own_sem=own_sem,
            up=up, down=down, sx=sx, sy=sy, fx=fx, fy=fy, sc=sc, rz=rz, rx=rx, ry=ry, rdx=rdx, rdy=rdy, rc=rc,
        )
        self.dp, self.p = lax.axis_index("dp"), lax.axis_index("sub")
        self.count = lax.axis_size("sub")
        self.last = self.count - 1
        self.me = self.dp * self.count + self.p
        self.groups = out.shape[0]

    def device(self, d):
        return (d // self.count, lax.rem(d, self.count))

    def flip(self, mask):
        return (jnp.bitwise_xor(self.dp, mask), self.p)

    def unit(self, g, mask, s):
        return self.out.at[jnp.bitwise_xor(self.dp, mask) * self.count + s, pl.ds(*GATHERED[g])]

    def half(self, g, mask, s, second):
        start, size = GATHERED[g]
        d = jnp.bitwise_xor(self.dp, mask) * self.count + s
        return self.out.at[d, pl.ds(start + (size // 2 if second else 0), size // 2)]

    def column(self, g, mask, second=None):
        start, size = GATHERED[g]
        if second is not None:
            start, size = start + (size // 2 if second else 0), size // 2
        return self.out.at[pl.ds(jnp.bitwise_xor(self.dp, mask) * self.count, self.count), pl.ds(start, size)]

    def own(self, g):
        return self.x_ref.at[pl.ds(*GATHERED[g])]

    def others(self, act):
        @pl.loop(0, self.groups)
        def _(d):
            @pl.when(d != self.me)
            def _():
                act(d)

    def tiny_copy(self, d):
        return remote(self.x_tiny, self.tiny.at[self.me], self.tsend, self.trecv, self.device(d))

    def chain(self, g, step, way, s, src):
        sems = self.up if way > 0 else self.down
        return remote(src, self.unit(g, 0, s), sems.at[g, step], self.rz.at[g, s], (self.dp, self.p + way))

    def side(self, g, mask, s, src):
        send, recv = (self.sx, self.rx) if mask == X else (self.sy, self.ry)
        return remote(src, self.unit(g, 0, s), send.at[g], recv.at[g, s], self.flip(mask))

    def halves(self, g, mask, s):
        other = Y if mask == X else X
        send, recv = (self.fy, self.rdy) if mask == X else (self.fx, self.rdx)
        ref = self.half(g, mask, s, mask == Y)
        return remote(ref, ref, send.at[g], recv.at[g], self.flip(other))

    def cross(self, g, kind):
        ref = self.column(g, (0, X, Y, X + Y)[kind])
        return remote(ref, ref, self.sc.at[g, kind], self.rc.at[g, kind], self.flip(CORE))

    def share(self, g, s, src):
        self.side(g, X, s, src).start()
        self.side(g, Y, s, src).start()

    def take(self, ref, sem):
        remote(ref, ref, sem, sem, (self.dp, self.p)).wait_recv()

    def sent(self, ref, sem):
        remote(ref, ref, sem, sem, (self.dp, self.p)).wait_send()

    def local(self, g):
        return pltpu.make_async_copy(self.own(g), self.unit(g, 0, self.p), self.own_sem.at[g])

    def local_tiny(self):
        return pltpu.make_async_copy(self.x_tiny, self.tiny.at[self.me], self.own_sem.at[len(GATHERED)])

    def start(self):
        attn, w_in, w_out, s_read, s_write, gains, bias = self.weights
        x_ref, x_tiny, p = self.x_ref, self.x_tiny, self.p
        width = x_ref.shape[1]
        barrier = pltpu.get_barrier_semaphore()
        self.others(
            lambda d: pl.semaphore_signal(barrier, inc=1, device_id=self.device(d), device_id_type=MESH)
        )
        x_tiny[...] = jnp.zeros((ROWS, TINY), bf16)
        x_tiny[:, 0:96] = s_write[...].astype(bf16)
        x_tiny[:, 96:112] = s_read[...].astype(bf16)
        x_tiny[:, 112:116] = turn_gains(gains[...]).astype(bf16)
        x_tiny[0:1, 128:192] = bias[...].astype(bf16)
        for m in range(4):
            x_ref[ROWS * m : ROWS * (m + 1)] = attn[m].astype(bf16)
            x_ref[64 + ROWS * m : 64 + ROWS * (m + 1)] = w_in[:, width * m : width * (m + 1)].astype(bf16)
        x_ref[128:192] = w_out[...].astype(bf16)
        self.local_tiny().start()
        for g in range(len(GATHERED)):
            self.local(g).start()
        pl.semaphore_wait(barrier, self.groups - 1)
        for g in range(len(GATHERED)):

            @pl.when(p < self.last)
            def _():
                self.chain(g, 0, 1, p, self.own(g)).start()

            @pl.when(p > 0)
            def _():
                self.chain(g, 0, -1, p, self.own(g)).start()

            self.share(g, p, self.own(g))
            if g == 0:
                self.others(lambda d: self.tiny_copy(d).start())

    def tables(self):
        self.take(self.tiny.at[pl.ds(0, self.groups - 1)], self.trecv)
        self.local_tiny().wait()

    def arrived(self, g, s):
        for mask, recv in ((X, self.rx), (Y, self.ry)):
            got = self.unit(g, mask, s)
            self.take(got, recv.at[g, s])
            self.halves(g, mask, s).start()

    def arrivals(self, g, k):
        p = self.p
        if k == 0:
            self.arrived(g, p)
            return

        @pl.when(p >= k)
        def _():
            self.arrived(g, p - k)

        @pl.when(p + k <= self.last)
        def _():
            self.arrived(g, p + k)

    def stage(self, g, k):
        p, last = self.p, self.last
        if k <= last:
            for way in (1, -1):

                @pl.when(p >= k if way > 0 else p + k <= last)
                def _():
                    s = p - k * way
                    got = self.unit(g, 0, s)
                    self.take(got, self.rz.at[g, s])
                    if k < last:

                        @pl.when(p < last if way > 0 else p > 0)
                        def _():
                            self.chain(g, k, way, s, got).start()

                    self.share(g, s, got)

        if k == last:
            self.local(g).wait()
            self.cross(g, 0).start()
        self.arrivals(g, k - 1)
        if k > last:
            self.cross(g, 1).start()
            self.cross(g, 2).start()

    def end(self, g):
        self.take(self.column(g, X + Y, False), self.rdy.at[g])
        self.take(self.column(g, X + Y, True), self.rdx.at[g])
        self.cross(g, 3).start()
        for kind, mask in enumerate((CORE, X + CORE, Y + CORE, X + Y + CORE)):
            self.take(self.column(g, mask), self.rc.at[g, kind])

    def finish(self):
        p, last = self.p, self.last
        self.sent(self.tiny.at[pl.ds(0, self.groups - 1)], self.tsend)
        for g in range(len(GATHERED)):
            self.sent(self.column(g, 0), self.sx.at[g])
            self.sent(self.column(g, 0), self.sy.at[g])
            self.sent(self.column(g, X, False), self.fy.at[g])
            self.sent(self.column(g, Y, True), self.fx.at[g])
            for kind in range(4):
                self.cross(g, kind).wait_send()
            for k in range(last):

                @pl.when((p < last) & (p >= k))
                def _():
                    self.chain(g, k, 1, p - k, self.unit(g, 0, p - k)).wait_send()

                @pl.when((p > 0) & (p + k <= last))
                def _():
                    self.chain(g, k, -1, p + k, self.unit(g, 0, p + k)).wait_send()


class Load:
    def __init__(self, wpack_h, out, tiny, sems):
        self.big = pltpu.make_async_copy(wpack_h.at[:, pl.ds(0, SMALL)], out, sems.at[0])
        self.little = pltpu.make_async_copy(wpack_h.at[:, pl.ds(SMALL, ROWS), pl.ds(0, TINY)], tiny, sems.at[1])

    def start(self):
        self.big.start()
        self.little.start()

    def tables(self):
        self.little.wait()

    def stage(self, g, k):
        pass

    def end(self, g):
        if g == 0:
            self.big.wait()

    def finish(self):
        pass


class Sums:
    def __init__(self, momentum, gp, out, rc, ra, rb, rx, ry, rz, tin, cs, cr, as_, ar, bs, br, xs, xr, ys, yr, zs, zr, ts, tr):
        self.__dict__.update(
            momentum=momentum, gp=gp, out=out, rc=rc, ra=ra, rb=rb, rx=rx, ry=ry, rz=rz, tin=tin,
            c=(cs, cr), a=(as_, ar), b=(bs, br), x=(xs, xr), y=(ys, yr), z=(zs, zr), t=(ts, tr),
        )
        self.dp, self.p = lax.axis_index("dp"), lax.axis_index("sub")
        self.count = lax.axis_size("sub")
        self.order = [lax.rem(self.p + off, self.count) for off in (2, 1, 3, 0)]
        self.sent = []

    def flip(self, mask):
        return (jnp.bitwise_xor(self.dp, mask), self.p)

    def place(self, mask, s):
        return jnp.bitwise_xor(self.dp, mask) * self.count + s

    def push(self, pair, index, src, dst, device):
        copy = remote(src, dst, pair[0].at[index], pair[1].at[index], device)
        copy.start()
        self.sent.append(copy)

    def take(self, pair, index, ref):
        remote(ref, ref, pair[0].at[index], pair[1].at[index], (self.dp, self.p)).wait_recv()

    def core(self, g):
        rows = pl.ds(*CROSSING[g])
        for k in (3, 1, 2, 0):
            src = self.gp.at[pl.ds(self.place((0, X, Y, X + Y)[k] + CORE, 0), self.count), rows]
            self.push(self.c, (g, k), src, self.rc.at[k, :, rows], self.flip(CORE))

    def ready(self, g, k):
        for index in ((3, 0), (1,))[g]:
            self.take(self.c, (index, k), self.rc.at[k, :, pl.ds(*CROSSING[index])])

    def total(self, k, s, start, size):
        at = slice(start, start + size)
        own = self.gp[self.place((0, X, Y, X + Y)[k], s), at]
        return own.astype(f32) + self.rc[k, s, at].astype(f32)

    def batches(self, g):
        if TOGETHER[g]:
            return [(0, pl.ds(0, self.count), self.order)]
        return [(s, pl.ds(s, 1), [s]) for s in self.order]

    def some(self, mask, at, start, size):
        first = self.place(mask, 0) + at.start
        return self.gp.at[pl.ds(first, at.size), pl.ds(start, size)]

    def diagonal(self, g):
        start, n1, n2, half = PARTS[g]
        self.ready(g, 3)
        for index, at, units in self.batches(g):
            for s in units:
                d = self.place(X + Y, s)
                self.gp[d, start : start + n1 + n2] = self.total(3, s, start, n1 + n2).astype(bf16)
            self.push(
                self.a, (g, index), self.some(X + Y, at, start, n1), self.ra.at[at, pl.ds(half, n1)], self.flip(X)
            )
            self.push(
                self.b, (g, index), self.some(X + Y, at, start + n1, n2), self.rb.at[at, pl.ds(half, n2)], self.flip(Y)
            )

    def sides(self, g):
        start, n1, n2, half = PARTS[g]
        rows = pl.ds(start, n1 + n2)
        self.ready(g, 1)
        self.ready(g, 2)
        for index, at, units in self.batches(g):
            self.take(self.b, (g, index), self.rb.at[at, pl.ds(half, n2)])
            for s in units:
                d = self.place(X, s)
                self.gp[d, start : start + n1] = self.total(1, s, start, n1).astype(bf16)
                more = self.rb[s, half : half + n2].astype(f32)
                self.gp[d, start + n1 : start + n1 + n2] = (self.total(1, s, start + n1, n2) + more).astype(bf16)
            self.push(self.x, (g, index), self.some(X, at, start, n1 + n2), self.rx.at[at, rows], self.flip(X))
            self.take(self.a, (g, index), self.ra.at[at, pl.ds(half, n1)])
            for s in units:
                d = self.place(Y, s)
                self.gp[d, start + n1 : start + n1 + n2] = self.total(2, s, start + n1, n2).astype(bf16)
                more = self.ra[s, half : half + n1].astype(f32)
                self.gp[d, start : start + n1] = (self.total(2, s, start, n1) + more).astype(bf16)
            self.push(self.y, (g, index), self.some(Y, at, start, n1 + n2), self.ry.at[at, rows], self.flip(Y))

    def owners(self, g, turns=None):
        start, n1, n2, _ = PARTS[g]
        size = n1 + n2
        rows = pl.ds(start, size)
        at = slice(start, start + size)
        turns = range(self.count) if turns is None else turns
        if 0 in turns:
            self.ready(g, 0)
            if TOGETHER[g]:
                self.take(self.x, (g, 0), self.rx.at[:, rows])
                self.take(self.y, (g, 0), self.ry.at[:, rows])
        for i in turns:
            s = self.order[i]
            if not TOGETHER[g]:
                self.take(self.x, (g, s), self.rx.at[pl.ds(s, 1), rows])
                self.take(self.y, (g, s), self.ry.at[pl.ds(s, 1), rows])
            mine = self.total(0, s, start, size) + self.rx[s, at].astype(f32) + self.ry[s, at].astype(f32)
            if i < self.count - 1:
                d = self.place(0, s)
                self.gp[d, at] = mine.astype(bf16)
                self.push(self.z, (g, i), self.gp.at[d, rows], self.rz.at[i, rows], (self.dp, s))
            else:
                self.out[at] = mine

    def final(self, g):
        start, n1, n2, _ = PARTS[g]
        size = n1 + n2
        at = slice(start, start + size)
        mine = self.out[at]
        for i in range(self.count - 1):
            self.take(self.z, (g, i), self.rz.at[i, pl.ds(start, size)])
            mine = mine + self.rz[i, at].astype(f32)
        self.out[at] = mine
        self.momentum.send(g)

    def small_core(self):
        rows, lanes = pl.ds(SMALL, ROWS), pl.ds(0, TINY)
        for k in (3, 1, 2, 0):
            src = self.gp.at[pl.ds(self.place((0, X, Y, X + Y)[k] + CORE, 0), self.count), rows, lanes]
            self.push(self.c, (2, k), src, self.rc.at[k, :, rows, lanes], self.flip(CORE))

    def small_send(self):
        for k in (3, 1, 2, 0):
            mask = (0, X, Y, X + Y)[k]
            self.take(self.c, (2, k), self.rc.at[k, :, pl.ds(SMALL, ROWS), pl.ds(0, TINY)])
            for i, s in enumerate(self.order):
                d = self.place(mask, s)
                own = self.gp[d, SMALL:PACK, 0:TINY].astype(f32)
                made = own + self.rc[k, s, SMALL:PACK, 0:TINY].astype(f32)
                if k == 0 and i == self.count - 1:
                    self.out[SMALL:PACK, 0:TINY] = made
                else:
                    self.gp[d, SMALL:PACK, 0:TINY] = made.astype(bf16)
                    src = self.gp.at[d, pl.ds(SMALL, ROWS), pl.ds(0, TINY)]
                    copy = remote(
                        src, self.tin.at[k, self.p], self.t[0].at[k, s], self.t[1].at[k, self.p],
                        (jnp.bitwise_xor(self.dp, mask), s),
                    )
                    copy.start()
                    self.sent.append(copy)

    def small_final(self):
        mine = self.out[SMALL:PACK, 0:TINY]
        for k in range(4):
            for i, s in enumerate(self.order):
                if not (k == 0 and i == self.count - 1):
                    self.take(self.t, (k, s), self.tin.at[k, s])
                    mine = mine + self.tin[k, s].astype(f32)
        self.out[SMALL:PACK, 0:TINY] = mine
        self.out[SMALL:PACK, TINY:] = jnp.zeros((ROWS, self.out.shape[1] - TINY), f32)
        self.momentum.send(2)

    def early(self):
        self.momentum.early()

    def late(self):
        self.momentum.late()
        self.momentum.work()

    def finish(self):
        for copy in self.sent:
            copy.wait_send()


class NoSums:
    def __init__(self):
        self.core = self.diagonal = self.sides = self.final = lambda g: None
        self.owners = lambda g, turns=None: None
        self.finish = self.small_core = self.small_send = self.small_final = self.early = self.late = lambda: None


def step(gather, sums, clips, ins, outs, scratch, wp, tiny, gp):
    frames_h, valid_ref, memory_h, ctm_h, ctr_ref = ins
    nm_h, ro_ref, gf_h, gm_h = outs
    (
        zm, zf, ctm, table, gain, bias, lw_m, lw_f, dw_m, dw_f, lr_m, lr_f, ar_m, ar_f, rm_s, rf_s, stat,
        summary, queries, keys, values, probs, context, after, normed, normed_mlp, spare, activ, gafter, d_fed_s, gsum,
        acc_w, acc_r, joined, raw, in_sem, out_sem, raw_sem,
    ) = scratch
    mem, read = memory_h.shape[1], ROWS
    toks = zf.shape[1]
    rows = clips * read
    groups = wp.shape[0]
    width = zm.shape[2]
    wide = mem + read
    mean_of = 1.0 / width

    def in_copies(c):
        return (
            pltpu.make_async_copy(memory_h.at[c], zm.at[c], in_sem.at[0, c]),
            pltpu.make_async_copy(ctm_h.at[c], ctm.at[c], in_sem.at[1, c]),
        )

    def out_copies(c):
        return (
            pltpu.make_async_copy(ctm.at[c], nm_h.at[c], out_sem.at[0, c]),
            pltpu.make_async_copy(zm.at[c], gm_h.at[c], out_sem.at[1, c]),
        )

    chunk = raw.shape[1] // clips
    chunks = [(t, min(chunk, toks - t)) for t in range(0, toks, chunk)]
    tiles = width // 128

    def raw_copy(i, out=False):
        t, n = chunks[i]
        here, there = raw.at[i % 2, pl.ds(0, n * clips)], pl.ds(t * clips, n * clips)
        if out:
            return pltpu.make_async_copy(here, gf_h.at[there], raw_sem.at[i])
        return pltpu.make_async_copy(frames_h.at[there], here, raw_sem.at[i])

    for i in range(min(2, len(chunks))):
        raw_copy(i).start()

    @pl.loop(0, clips)
    def _(c):
        for copy in in_copies(c):
            copy.start()

    def frames_in():
        for i, (t, n) in enumerate(chunks):
            raw_copy(i).wait()
            for q in range(tiles):
                spare[q, 0 : n * clips] = raw[i % 2, 0 : n * clips, 128 * q : 128 * (q + 1)].astype(f32)
            if i + 2 < len(chunks):
                raw_copy(i + 2).start()

            @pl.loop(0, clips)
            def _(c):
                for q in range(tiles):
                    zf[c, t : t + n, 128 * q : 128 * (q + 1)] = spare[
                        q, pl.ds(c, n, stride=clips)
                    ].astype(bf16)

    def frames_out():
        for i, (t, n) in enumerate(chunks):
            @pl.loop(0, clips)
            def _(c):
                for q in range(tiles):
                    spare[q, pl.ds(c, n, stride=clips)] = zf[
                        c, t : t + n, 128 * q : 128 * (q + 1)
                    ].astype(f32)

            if i >= 2:
                raw_copy(i - 2, True).wait()
            for q in range(tiles):
                raw[i % 2, 0 : n * clips, 128 * q : 128 * (q + 1)] = spare[q, 0 : n * clips].astype(bf16)
            raw_copy(i, True).start()

    def clip_loop(low, high, batch, body):
        @pl.loop(low // batch, high // batch)
        def _(i):
            lockstep([functools.partial(body, i * batch + k) for k in range(batch)])

    ones = jnp.ones((8, 128), bf16)
    place = lax.broadcasted_iota(jnp.int32, (mem, 8), 1)

    def unit_rows(z):
        square = z * z
        folded = (square[:, 0:128] + square[:, 128:256]) + (square[:, 256:384] + square[:, 384:512])
        return lax.rsqrt(dot(ones, folded, 1, 1) * mean_of + NORM_EPS)

    def rows_of(c):
        return pl.ds(pl.multiple_of(c * read, read), read)

    def ahead(c):
        for copy in in_copies(c):
            copy.wait()
        z_m, z_f, g = zm[c], zf[c], ctm[c]
        yield
        r_m, r_f = unit_rows(z_m), unit_rows(z_f)
        yield
        d_m, d_f = dot(g, z_m, 1, 1), dot(g, z_f, 1, 1)
        yield
        rm_s[c], rf_s[c] = r_m, r_f
        dw_m[c], dw_f[c] = d_m.astype(bf16), d_f.astype(bf16)

    def reading(c):
        z_m, z_f, r_m, r_f = zm[c], zf[c], rm_s[c], rf_s[c]
        d_m, d_f = dw_m[c].astype(f32), dw_f[c].astype(f32)
        live = valid_ref[pl.ds(c, 1), :] > 0
        tab = table[...]
        yield
        u_m, u_f = dot(tab, z_m, 1, 1), dot(tab, z_f, 1, 1)
        yield
        l_m = u_m * r_m[0:1]
        l_f = jnp.where(live, u_f * r_f[0:1], MASKED)
        top = jnp.maximum(jnp.max(l_m, axis=1, keepdims=True), jnp.max(l_f, axis=1, keepdims=True))
        yield
        e_m, e_f = jnp.exp(l_m - top), jnp.exp(l_f - top)
        total = jnp.sum(e_m, axis=1, keepdims=True) + jnp.sum(e_f, axis=1, keepdims=True)
        inv = 1.0 / total[mem:]
        a_m, a_f = e_m[mem:] * inv, e_f[mem:] * inv
        yield
        a_m, a_f = a_m.astype(bf16), a_f.astype(bf16)
        made = dot(a_m, z_m) + dot(a_f, z_f)
        moved = jnp.sum(e_m[0:mem] * d_m, axis=1, keepdims=True) + jnp.sum(
            e_f[0:mem] * d_f, axis=1, keepdims=True
        )
        yield
        lw_m[c], lw_f[c] = l_m[0:mem], l_f[0:mem]
        lr_m[c], lr_f[c] = l_m[mem:].astype(bf16), l_f[mem:].astype(bf16)
        ar_m[c], ar_f[c] = a_m, a_f
        stat[c] = jnp.where(
            place == 0, top[0:mem], jnp.where(place == 1, total[0:mem], moved)
        ).T
        summary[rows_of(c)] = made

    half = clips // 2
    third = clips // 3
    gather.start()
    frames_in()
    clip_loop(0, half, 2, ahead)
    gather.stage(0, 1)
    clip_loop(half, clips, 2, ahead)
    gather.tables()
    turned = tiny[:, :, 0:128].reshape(groups * ROWS, 128).astype(f32).T
    gain[...] = turned[112:120]
    table[0:mem] = (turned[0:mem] * turned[115:116]).astype(bf16)
    table[mem:wide] = (turned[mem:wide] * turned[112:113]).astype(bf16)
    piece = bias.shape[1] // groups
    for d in range(groups):
        bias[:, piece * d : piece * (d + 1)] = tiny[d, 0:1, 128 : 128 + piece].astype(f32)
    gather.stage(0, 2)
    clip_loop(0, third, 2, reading)
    gather.stage(0, 3)
    clip_loop(third, 2 * third, 2, reading)
    gather.stage(0, 4)
    clip_loop(2 * third, clips, 2, reading)
    gather.end(0)

    def mat(m):
        return wp[:, ROWS * m : ROWS * (m + 1)].reshape(groups * ROWS, width)

    per = groups // 4

    def out_mat(j):
        return wp[pl.ds(per * j, per), 128:192].reshape(width, width)

    def unit(v):
        return lax.rsqrt(jnp.mean(v * v, axis=-1, keepdims=True) + NORM_EPS)

    summ = summary[...]
    hidden = (summ * unit(summ) * gain[1:2]).astype(bf16)
    normed[...] = hidden
    queries[...] = dot(hidden, mat(0)).astype(bf16)
    keys[...] = dot(hidden, mat(1)).astype(bf16)
    values[...] = dot(hidden, mat(2)).astype(bf16)
    scale = HEAD_DIM**-0.5
    block = 128
    blocks = rows // block
    pairs = HEADS // 2
    row_clip = lax.broadcasted_iota(jnp.int32, (block, block), 0) // read
    col_clip = lax.broadcasted_iota(jnp.int32, (block, block), 1) // read
    same = row_clip == col_clip
    low_lane = lax.broadcasted_iota(jnp.int32, (block, block), 1) < HEAD_DIM

    def half_of(v, side):
        zero = jnp.zeros_like(v)
        return jnp.where(low_lane, v, zero) if side == 0 else jnp.where(low_lane, zero, v)

    def attend(b, pair):
        at = pl.ds(pl.multiple_of(b * block, block), block)
        lanes = slice(pair * block, (pair + 1) * block)
        q, k, v = queries[at, lanes], keys[at, lanes], values[at, lanes]
        yield
        scores = [dot(half_of(q, side), k, 1, 1) for side in range(2)]
        yield
        masked = [jnp.where(same, s * scale, MASKED) for s in scores]
        tops = [jnp.max(s, axis=1, keepdims=True) for s in masked]
        yield
        parts = [jnp.exp(s - top) for s, top in zip(masked, tops)]
        sums_ = [jnp.sum(e, axis=1, keepdims=True) for e in parts]
        yield
        made = [(e * (1.0 / s)).astype(bf16) for e, s in zip(parts, sums_)]
        got = [dot(p, v) for p in made]
        yield
        probs[b, 2 * pair], probs[b, 2 * pair + 1] = made
        context[at, lanes] = jnp.where(low_lane, got[0], got[1]).astype(bf16)

    @pl.loop(0, blocks)
    def _(b):
        lockstep([functools.partial(attend, b, pair) for pair in range(pairs)])

    aft = summary[...] + dot(context[...], mat(3))
    after[...] = aft
    fed = (aft * unit(aft) * gain[2:3]).astype(bf16)
    def columns(j):
        return pl.ds(pl.multiple_of(width * j, width), width)

    def rows_at(j):
        return pl.ds(pl.multiple_of(rows * j, rows), rows)

    def in_mat(j):
        return wp[:, pl.ds(pl.multiple_of(64 + ROWS * j, ROWS), ROWS)].reshape(groups * ROWS, width)

    normed_mlp[...] = fed

    @pl.loop(0, 4)
    def _(j):
        pre = dot(normed_mlp[...], in_mat(j)) + bias[:, columns(j)]
        square = pre * pre
        t = jnp.tanh(GELU_A * pre * (1.0 + GELU_B * square))
        most = 0.5 + 0.5 * t
        activ[0:rows, columns(j)] = (pre * most).astype(bf16)
        slope = most + (0.5 * GELU_A) * pre * (1.0 - t * t) * (1.0 + (3.0 * GELU_B) * square)
        for q in range(tiles):
            spare[q, rows_at(j)] = slope[:, 128 * q : 128 * (q + 1)]

    gather.finish()
    gafter[...] = after[...]

    @pl.loop(0, 4)
    def _(j):
        gafter[...] += dot(activ[0:rows, columns(j)], out_mat(j))

    out = gafter[...]
    ro_ref[...] = out.astype(bf16)

    many = block // read

    def joining(b):
        at = slice(block * b, block * (b + 1))
        ro, ctr = ro_ref[at], ctr_ref[at].astype(f32)
        gs = [ctm[many * b + i] for i in range(many)]
        now = stat[many * b : many * (b + 1)]
        tab = table[0:mem]
        yield
        ro_f = ro.astype(f32)
        r = unit(ro_f)
        l = dot(ro, tab, 1, 1) * r
        d = jnp.concatenate(
            [dot(ro[read * i : read * (i + 1)], g, 1, 1) for i, g in enumerate(gs)], axis=0
        )
        yield
        l_c, d_c = l.reshape(many, read, mem), d.reshape(many, read, mem)
        top, total, moved = now[:, 0:1], now[:, 1:2], now[:, 2:3]
        new_top = jnp.maximum(top, jnp.max(l_c, axis=1, keepdims=True))
        old, e = jnp.exp(top - new_top), jnp.exp(l_c - new_top)
        total = total * old + jnp.sum(e, axis=1, keepdims=True)
        moved = moved * old + jnp.sum(e * d_c, axis=1, keepdims=True)
        inv = 1.0 / total
        a, mean = e * inv, moved * inv
        b_all = (a * (d_c - mean)).reshape(block, mem)
        k = jnp.sum(b_all * l, axis=1, keepdims=True) * (r * r * mean_of)
        a_low = a.reshape(block, mem).astype(bf16)
        h_low = (b_all * r).astype(bf16)
        yield
        made = dot(h_low, tab) + jnp.concatenate(
            [dot(a_low[read * i : read * (i + 1)], g) for i, g in enumerate(gs)], axis=0
        )
        yield
        gafter[at] = made - ro_f * k + ctr
        joined[at, 0:mem], joined[at, 128 : 128 + mem] = a_low, h_low
        stat[many * b : many * (b + 1), 0:1] = new_top + jnp.log(total)
        stat[many * b : many * (b + 1), 1:2] = mean

    lockstep([functools.partial(joining, b) for b in range(blocks)])

    gsum[...] = gafter[...].astype(bf16)
    d_fed_s[...] = jnp.zeros_like(d_fed_s)

    @pl.loop(0, 4)
    def _(j):
        gp[pl.ds(per * j, per), 128:192] = (
            dot(activ[0:rows, columns(j)], gsum[...], 0, 0).astype(bf16).reshape(per, 64, width)
        )

    sums.core(3)

    @pl.loop(0, 4)
    def _(j):
        g_out, fed = gsum[...], normed_mlp[...]
        slope = jnp.concatenate([spare[q, rows_at(j)] for q in range(tiles)], axis=1)
        d_low = (dot(g_out, out_mat(j), 1, 1) * slope).astype(bf16)
        bias[:, columns(j)] = jnp.sum(d_low.astype(f32), axis=0, keepdims=True)
        gp[:, pl.ds(pl.multiple_of(64 + ROWS * j, ROWS), ROWS)] = (
            dot(fed, d_low, 0, 0).astype(bf16).reshape(groups, ROWS, width)
        )
        d_fed_s[...] += dot(d_low, in_mat(j), 1, 1)

    sums.core(0)
    aft = after[...]
    unit_aft = unit(aft)
    flat_aft = aft * unit_aft
    d_fed = d_fed_s[...]
    d_gain_mlp = jnp.sum(d_fed * flat_aft, axis=0, keepdims=True)
    d_flat = d_fed * gain[2:3]
    g_mid = gafter[...] + unit_aft * (
        d_flat - flat_aft * jnp.mean(d_flat * flat_aft, axis=-1, keepdims=True)
    )
    gafter[...] = g_mid
    g_low = g_mid.astype(bf16)
    gp[:, 3 * ROWS : 4 * ROWS] = (
        dot(context[...], g_low, 0, 0).astype(bf16).reshape(groups, ROWS, width)
    )
    context[...] = dot(g_low, mat(3), 1, 1).astype(bf16)
    sums.diagonal(0)

    def attend_back(b, pair):
        at = pl.ds(pl.multiple_of(b * block, block), block)
        lanes = slice(pair * block, (pair + 1) * block)
        q, k, v, dc = queries[at, lanes], keys[at, lanes], values[at, lanes], context[at, lanes]
        lows = (probs[b, 2 * pair], probs[b, 2 * pair + 1])
        ps = [p.astype(f32) for p in lows]
        yield
        dps = [dot(half_of(dc, side), v, 1, 1) for side in range(2)]
        dvs = [dot(p, dc, 0, 0) for p in lows]
        yield
        means = [jnp.sum(dp * p, axis=1, keepdims=True) for dp, p in zip(dps, ps)]
        yield
        lows = [(scale * p * (dp - m)).astype(bf16) for p, dp, m in zip(ps, dps, means)]
        dqs = [dot(low, k) for low in lows]
        dks = [dot(low, q, 0, 0) for low in lows]
        yield
        queries[at, lanes] = jnp.where(low_lane, dqs[0], dqs[1]).astype(bf16)
        keys[at, lanes] = jnp.where(low_lane, dks[0], dks[1]).astype(bf16)
        values[at, lanes] = jnp.where(low_lane, dvs[0], dvs[1]).astype(bf16)

    @pl.loop(0, blocks)
    def _(b):
        lockstep([functools.partial(attend_back, b, pair) for pair in range(pairs)])

    hidden = normed[...]
    d_hid = jnp.zeros((rows, width), f32)
    for m, g in enumerate((queries, keys, values)):
        g_now = g[...]
        gp[:, ROWS * m : ROWS * (m + 1)] = (
            dot(hidden, g_now, 0, 0).astype(bf16).reshape(groups, ROWS, width)
        )
        d_hid = d_hid + dot(g_now, mat(m), 1, 1)
    sums.core(1)
    summ = summary[...]
    unit_sum = unit(summ)
    flat_sum = summ * unit_sum
    d_gain_attn = jnp.sum(d_hid * flat_sum, axis=0, keepdims=True)
    d_flat = d_hid * gain[1:2]
    gsum[...] = (
        gafter[...]
        + unit_sum * (d_flat - flat_sum * jnp.mean(d_flat * flat_sum, axis=-1, keepdims=True))
    ).astype(bf16)
    sums.sides(0)
    sums.diagonal(1)

    acc_w[...] = jnp.zeros_like(acc_w)
    acc_r[...] = jnp.zeros_like(acc_r)

    def closing(c):
        z_m, z_f, g, gr = zm[c], zf[c], ctm[c], gsum[rows_of(c)]
        ro, pair = ro_ref[rows_of(c)], joined[rows_of(c)]
        r_m, r_f, l_m, l_f = rm_s[c, 0:1], rf_s[c, 0:1], lw_m[c], lw_f[c]
        d_m, d_f = dw_m[c].astype(f32), dw_f[c].astype(f32)
        q_m, q_f, a_m, a_f = (v[c].astype(f32) for v in (lr_m, lr_f, ar_m, ar_f))
        now = stat[c].T
        lse, mean = now[:, 0:1], now[:, 1:2]
        tab = table[...]
        yield
        x_m, x_f = dot(gr, z_m, 1, 1), dot(gr, z_f, 1, 1)
        w_m, w_f = jnp.exp(l_m - lse), jnp.exp(l_f - lse)
        yield
        b_m, b_f = w_m * (d_m - mean), w_f * (d_f - mean)
        k_m = jnp.sum(b_m * l_m, axis=0, keepdims=True)
        k_f = jnp.sum(b_f * l_f, axis=0, keepdims=True)
        mean_r = jnp.sum(x_m * a_m, axis=1, keepdims=True) + jnp.sum(x_f * a_f, axis=1, keepdims=True)
        yield
        c_m, c_f = a_m * (x_m - mean_r), a_f * (x_f - mean_r)
        k_m = (k_m + jnp.sum(c_m * q_m, axis=0, keepdims=True)) * (r_m * r_m * mean_of)
        k_f = (k_f + jnp.sum(c_f * q_f, axis=0, keepdims=True)) * (r_f * r_f * mean_of)
        left_m = jnp.concatenate([w_m, b_m * r_m, a_m, c_m * r_m], axis=0).astype(bf16)
        left_f = jnp.concatenate([w_f, b_f * r_f, a_f, c_f * r_f], axis=0).astype(bf16)
        yield
        made = dot(left_m, z_m) + dot(left_f, z_f)
        joins = (dot(pair[:, 0:mem], ro, 0, 0), dot(pair[:, 128 : 128 + mem], ro, 0, 0))
        back = jnp.concatenate([g, tab[0:mem], gr, tab[mem:]], axis=0)
        t_m = jnp.broadcast_to(k_m, (8, mem)).T
        t_f = jnp.broadcast_to(k_f, (8, toks)).T
        yield
        dz_m = dot(left_m, back, 0, 0) - z_m.astype(f32) * t_m[:, 0:1]
        dz_f = dot(left_f, back, 0, 0) - z_f.astype(f32) * t_f[:, 0:1]
        yield
        ctm[c] = (made[0:mem] + joins[0]).astype(bf16)
        acc_w[...] += made[mem : 2 * mem] + joins[1]
        acc_r[...] += made[2 * mem + read :]
        zm[c], zf[c] = dz_m.astype(bf16), dz_f.astype(bf16)
        for copy in out_copies(c):
            copy.start()

    at_clips = [0, *(clips * part // 12 for part in (4, 7, 10, 12))]
    for turn in range(4):
        clip_loop(at_clips[turn], at_clips[turn + 1], 2, closing)
        sums.owners(0, [turn])
    sums.sides(1)

    zero_rows = jnp.zeros((1, width), f32)
    rest = jnp.concatenate(
        [zero_rows, d_gain_attn, d_gain_mlp, zero_rows, jnp.zeros((12, width), f32)], axis=0
    )
    stacked = jnp.concatenate([acc_w[...], acc_r[...], rest], axis=0)
    gp[:, SMALL:PACK] = jnp.zeros((groups, ROWS, width), bf16)
    gp[:, SMALL:PACK, 0:128] = stacked.T.astype(bf16).reshape(groups, ROWS, 128)
    for d in range(groups):
        gp[d, SMALL : SMALL + 1, 128 : 128 + piece] = bias[:, piece * d : piece * (d + 1)].astype(bf16)
    sums.small_core()
    sums.final(0)
    sums.small_send()
    frames_out()
    sums.owners(1)
    sums.final(1)
    sums.small_final()
    sums.early()
    sums.late()

    @pl.loop(0, clips)
    def _(c):
        for copy in out_copies(c):
            copy.wait()

    for i in range(max(0, len(chunks) - 2), len(chunks)):
        raw_copy(i, True).wait()
    sums.finish()


def step_scratch(clips, toks, mem, read, width):
    vm, sem = pltpu.VMEM, pltpu.SemaphoreType.DMA
    rows, wide = clips * read, mem + read
    return [
        vm((clips, mem, width), bf16),
        vm((clips, toks, width), bf16),
        vm((clips, mem, width), bf16),
        vm((wide, width), bf16),
        vm((8, width), f32),
        vm((1, 4 * width), f32),
        vm((clips, mem, mem), f32),
        vm((clips, mem, toks), f32),
        vm((clips, mem, mem), bf16),
        vm((clips, mem, toks), bf16),
        vm((clips, read, mem), bf16),
        vm((clips, read, toks), bf16),
        vm((clips, read, mem), bf16),
        vm((clips, read, toks), bf16),
        vm((clips, 8, mem), f32),
        vm((clips, 8, toks), f32),
        vm((clips, 8, mem), f32),
        vm((rows, width), f32),
        vm((rows, width), bf16),
        vm((rows, width), bf16),
        vm((rows, width), bf16),
        vm((rows // 128, HEADS, 128, 128), bf16),
        vm((rows, width), bf16),
        vm((rows, width), f32),
        vm((rows, width), bf16),
        vm((rows, width), bf16),
        vm((width // 128, 4 * max(rows, width), 128), f32),
        vm((max(rows, width), 4 * width), bf16),
        vm((rows, width), f32),
        vm((rows, width), f32),
        vm((rows, width), bf16),
        vm((mem, width), f32),
        vm((read, width), f32),
        vm((rows, 256), bf16),
        vm((2, 16 * clips, width), bf16),
        sem((2, clips)),
        sem((2, clips)),
        sem((-(-toks // 16),)),
    ]


def plain_kernel(clips, *refs):
    ins, wpack_h, outs, gp = refs[0:5], refs[5], refs[6:10], refs[10]
    wp, tiny, sems = refs[11:14]
    step(Load(wpack_h, wp, tiny, sems), NoSums(), clips, ins, outs, refs[14:], wp, tiny, gp)


def whole_kernel(clips, *refs):
    weights, ins, state = refs[0:7], refs[7:12], refs[12:18]
    outs, red, xrec = refs[18:22], refs[22], refs[23]
    refs = refs[24:]
    wp, tiny, gp = refs[0:3]
    gather_refs, refs = refs[3:21], refs[21:]
    sum_refs, refs = refs[0:21], refs[21:]
    muon_refs, refs = refs[0:8], refs[8:]
    gather = Gather(weights, wp, tiny, *gather_refs)
    muon = Muon(red, state, xrec, *muon_refs, refs[26], refs[27])
    step(gather, Sums(muon, gp, red, *sum_refs), clips, ins, outs, refs, wp, tiny, gp)
    muon.finish()


def run_step(frames, valid, memory, ct_memory, ct_read, wpack=None, weights=(), state=()):
    clips, toks, width = frames.shape
    mem, read = memory.shape[1], ct_read.shape[1]
    groups, rows = width // ROWS, clips * read
    vm, sem, made = pltpu.VMEM, pltpu.SemaphoreType.DMA, jax.ShapeDtypeStruct
    hbm = pl.BlockSpec(memory_space=pl.ANY)
    inside = pl.BlockSpec(memory_space=pltpu.VMEM)
    out_shape = [
        made(memory.shape, bf16), made((rows, width), bf16), made((toks * clips, width), bf16), made(memory.shape, bf16),
    ]
    out_specs = [hbm, inside, hbm, hbm]
    in_specs = [hbm, inside, hbm, hbm, inside]
    frames = frames.transpose(1, 0, 2).reshape(toks * clips, width)
    operands = [frames, valid, memory, ct_memory, ct_read.reshape(rows, width)]
    scratch = [vm((groups, SMALL, width), bf16), vm((groups, ROWS, TINY), bf16)]
    params = dict(vmem_limit_bytes=VMEM_LIMIT)
    if weights:
        n = lax.axis_size("sub")
        kernel = whole_kernel
        operands = [*weights, *operands, *state]
        in_specs = [inside] * len(weights) + in_specs + [inside] * len(state)
        out_shape += [made((PACK, width), f32), made((PACK, width), bf16)]
        out_specs += [inside, inside]
        scratch += [
            vm((groups, PACK, width), bf16),
            vm((SMALL, width), bf16), vm((ROWS, TINY), bf16), sem, sem, sem((len(GATHERED) + 1,)),
            *[sem((len(GATHERED), n))] * 2, *[sem((len(GATHERED),))] * 4, sem((len(GATHERED), 4)),
            *[sem((len(GATHERED), n))] * 3, *[sem((len(GATHERED),))] * 2, sem((len(GATHERED), 4)),
            vm((4, n, PACK, width), bf16),
            vm((n, 112, width), bf16),
            vm((n, 96, width), bf16),
            vm((n, PACK, width), bf16),
            vm((n, PACK, width), bf16),
            vm((n - 1, PACK, width), bf16),
            vm((4, n, ROWS, TINY), bf16),
            *[sem((4, 4))] * 2, *[sem((2, n))] * 8, *[sem((2, n - 1))] * 2, *[sem((4, n))] * 2,
            vm((PACK, width), bf16), vm((groups, 64, width), bf16), sem((len(OWNERS),)), sem((groups,)), sem,
            sem((groups,)), sem((len(OWNERS),)), sem,
        ]
        params.update(collective_id=1, has_side_effects=True)
    else:
        kernel = plain_kernel
        operands.append(wpack)
        in_specs.append(hbm)
        out_shape.append(made((groups, PACK, width), bf16))
        out_specs.append(inside)
        scratch.append(sem((2,)))
    outs = pl.pallas_call(
        functools.partial(kernel, clips),
        out_shape=tuple(out_shape),
        in_specs=in_specs,
        out_specs=tuple(out_specs),
        scratch_shapes=scratch + step_scratch(clips, toks, mem, read, width),
        compiler_params=pltpu.CompilerParams(**params),
        name="clip_step",
    )(*operands)
    return outs


def clip_outputs(outs, clips):
    new_memory, read_out, by_token, grad_memory = outs
    width = by_token.shape[1]
    frames = by_token.reshape(-1, clips, width).transpose(1, 0, 2)
    return new_memory, read_out.reshape(clips, ROWS, width), frames, grad_memory


OWNERS = ((2, 0), (4, 3), (2, 3), (4, 0), (0, 1), (6, 2), (0, 3))
PIECES = ((0, 16), (16, 16), (32, 16), (48, 16), (64, 64), (128, 64), (192, 16))


def is_owner(m):
    return (lax.axis_index("dp") == OWNERS[m][0]) & (lax.axis_index("sub") == OWNERS[m][1])


def small_grads(red, gains_t):
    return (
        red[SMALL:PACK, 0:96] * gains_t[:, 3:4],
        red[SMALL:PACK, 96:112] * gains_t[:, 0:1],
    )


def exact_dot(a, b, ca=1, cb=0):
    return lax.dot_general(a, b, (((ca,), (cb,)), ((), ())), preferred_element_type=f32, precision=highest)


def iterate_small(x, same):
    norm = jnp.sum(x * x, axis=1, keepdims=True)
    total = jnp.sum(jnp.where(same, norm.T, 0.0), axis=1, keepdims=True)
    x = x * (1.0 / (jnp.sqrt(total) + 1e-07))
    for _ in range(5):
        q = jnp.where(same, exact_dot(x, x, 1, 1), 0.0)
        mixed = NS[1] * q + NS[2] * exact_dot(q, q)
        x = NS[0] * x + exact_dot(mixed, x)
    return x


class Muon:
    def __init__(self, acc, state, xrec, pk, buf, gsend, grecv, gown, ssend, srecv, sown, x, low):
        self.__dict__.update(
            acc=acc, state=state, xrec=xrec, pk=pk, buf=buf, gsend=gsend, grecv=grecv, gown=gown,
            ssend=ssend, srecv=srecv, sown=sown, x=x, low=low,
        )
        self.count = lax.axis_size("sub")
        self.me = lax.axis_index("dp") * self.count + lax.axis_index("sub")
        self.groups = buf.shape[0]

    def piece(self, m):
        start, size = PIECES[m]
        return self.pk.at[pl.ds(start, size)], self.buf.at[self.me, pl.ds(0, size)]

    def away(self, m):
        return remote(*self.piece(m), self.gsend.at[m], self.grecv.at[self.me], OWNERS[m])

    def home(self, m):
        return pltpu.make_async_copy(*self.piece(m), self.gown)

    def send(self, part):
        attn_mom, w_in_mom, w_out_mom, s_read_mom, s_write_mom, gains = self.state
        acc, pk = self.acc, self.pk
        width = acc.shape[1]
        if part == 0:
            for m in range(4):
                at = slice(64 + ROWS * m, 64 + ROWS * (m + 1))
                pk[at] = (0.5 * w_in_mom[:, width * m : width * (m + 1)] + acc[at]).astype(bf16)
            pk[128:192] = (0.5 * w_out_mom[...] + acc[128:192]).astype(bf16)
        elif part == 1:
            for m in range(4):
                at = slice(ROWS * m, ROWS * (m + 1))
                pk[at] = (0.5 * attn_mom[m] + acc[at]).astype(bf16)
        else:
            g_write, g_read = small_grads(acc, turn_gains(gains[...]))
            pk[SMALL:PACK] = jnp.zeros((ROWS, width), bf16)
            pk[SMALL:PACK, 0:96] = (0.5 * s_write_mom[...] + g_write).astype(bf16)
            pk[SMALL:PACK, 96:112] = (0.5 * s_read_mom[...] + g_read).astype(bf16)
        for m in ((4, 5), (0, 1, 2, 3), (6,))[part]:

            @pl.when(jnp.logical_not(is_owner(m)))
            def _():
                self.away(m).start()

            @pl.when(is_owner(m))
            def _():
                self.home(m).start()

    def each_other(self, act):
        @pl.loop(0, self.groups)
        def _(d):
            @pl.when(d != self.me)
            def _():
                act(d)

    def whole(self, m):
        def take(d):
            got = self.buf.at[d, pl.ds(0, PIECES[m][1])]
            remote(got, got, self.grecv.at[d], self.grecv.at[d], OWNERS[m]).wait_recv()

        self.each_other(take)
        self.home(m).wait()

    def row_copy(self, m, d):
        start, size = PIECES[m]
        return remote(
            self.buf.at[d, pl.ds(0, size)], self.xrec.at[pl.ds(start, size)], self.ssend.at[d], self.srecv.at[m],
            (d // self.count, lax.rem(d, self.count)),
        )

    def row_home(self, m):
        start, size = PIECES[m]
        return pltpu.make_async_copy(
            self.buf.at[self.me, pl.ds(0, size)], self.xrec.at[pl.ds(start, size)], self.sown
        )

    def spread(self, m):
        self.each_other(lambda d: self.row_copy(m, d).start())
        self.row_home(m).start()

    def spread_wait(self, m):
        self.each_other(lambda d: self.row_copy(m, d).wait_send())
        self.row_home(m).wait()

    def put(self, j, value):
        n = value.shape[0]
        for q in range(value.shape[1] // 128):
            self.x[q, n * j : n * (j + 1)] = value[:, 128 * q : 128 * (q + 1)]

    def get(self, j, n):
        return jnp.concatenate([self.x[q, n * j : n * (j + 1)] for q in range(self.x.shape[0])], axis=1)

    def iterate(self, blocks, n):
        low = self.low
        total = jnp.zeros((1, 1), f32)
        for j in range(blocks):
            now = self.get(j, n)
            total = total + jnp.sum(now * now, keepdims=True)
        scale = 1.0 / (jnp.sqrt(total) + 1e-07)
        for j in range(blocks):
            now = self.get(j, n) * scale
            self.put(j, now)
            low[0:n, n * j : n * (j + 1)] = now.astype(bf16)

        self.sweep(blocks, n, 3)

    def sweep(self, blocks, n, times):
        low = self.low

        def block(j):
            return low[0:n, n * j : n * (j + 1)]

        @pl.loop(0, times)
        def _(_):
            q = dot(block(0), block(0), 1, 1)
            for j in range(1, blocks):
                q = q + dot(block(j), block(j), 1, 1)
            q_low = q.astype(bf16)
            mixed = (NS[1] * q + NS[2] * dot(q_low, q_low)).astype(bf16)
            for j in range(blocks):
                new = NS[0] * self.get(j, n) + dot(mixed, block(j))
                self.put(j, new)
                low[0:n, n * j : n * (j + 1)] = new.astype(bf16)

    def early(self):
        buf, groups = self.buf, self.groups
        width = buf.shape[2]
        per = groups // 4

        @pl.when(is_owner(4))
        def _():
            self.whole(4)
            for j in range(4):
                self.put(j, buf[:, ROWS * j : ROWS * (j + 1)].reshape(width, width).astype(f32))

        @pl.when(is_owner(5))
        def _():
            self.whole(5)
            for j in range(4):
                self.put(j, buf[per * j : per * (j + 1)].reshape(width, width).astype(f32).T)

        @pl.when(is_owner(4) | is_owner(5))
        def _():
            self.iterate(4, width)

    def late(self):
        buf, groups = self.buf, self.groups
        width = buf.shape[2]
        per = groups // 4

        @pl.when(is_owner(4) | is_owner(5))
        def _():
            self.sweep(4, width, 2)

        @pl.when(is_owner(4))
        def _():
            for j in range(4):
                buf[:, ROWS * j : ROWS * (j + 1)] = self.low[0:width, width * j : width * (j + 1)].reshape(
                    groups, ROWS, width
                )
            self.spread(4)

        @pl.when(is_owner(5))
        def _():
            for j in range(4):
                buf[per * j : per * (j + 1)] = self.get(j, width).T.astype(bf16).reshape(per, 64, width)
            self.spread(5)

    def work(self):
        buf, groups = self.buf, self.groups
        width = buf.shape[2]
        for m in range(4):

            @pl.when(is_owner(m))
            def _():
                self.whole(m)

        @pl.when(is_owner(0) | is_owner(1) | is_owner(2) | is_owner(3))
        def _():
            self.put(0, buf[:, 0:ROWS].reshape(width, width).astype(f32))
            self.iterate(1, width)
            self.sweep(1, width, 2)
            buf[:, 0:ROWS] = self.low[0:width, 0:width].reshape(groups, ROWS, width)

        for m in range(4):

            @pl.when(is_owner(m))
            def _():
                self.spread(m)

        @pl.when(is_owner(6))
        def _():
            self.whole(6)
            table = buf[:, 0:ROWS, 0:128].reshape(width, 128).astype(f32).T
            row = lax.broadcasted_iota(jnp.int32, (128, 128), 0)
            col = lax.broadcasted_iota(jnp.int32, (128, 128), 1)
            same = ((row < 96) & (col < 96)) | ((row >= 96) & (col >= 96))
            made = iterate_small(table, same)
            buf[:, 0:ROWS, 0:128] = made.T.astype(bf16).reshape(groups, ROWS, 128)
            self.spread(6)

    def finish(self):
        many = range(len(OWNERS))
        for m in many:

            @pl.when(jnp.logical_not(is_owner(m)))
            def _():
                self.away(m).wait_send()
                start, size = PIECES[m]
                got = self.xrec.at[pl.ds(start, size)]
                remote(got, got, self.srecv.at[m], self.srecv.at[m], OWNERS[m]).wait_recv()

            @pl.when(is_owner(m))
            def _():
                self.spread_wait(m)


def finish_kernel(
    red, xrec, attn, w_in, w_out, s_read, s_write, attn_mom, w_in_mom, w_out_mom, s_read_mom, s_write_mom,
    gains, gains_first, gains_second, bias, bias_first, bias_second, nm_in, ro_in, gf_in, gm_in,
    nm, ro, gf, gm, g_attn, g_in, g_out, g_read, g_write, g_gains, g_bias,
    n_attn, n_in, n_out, n_read, n_write, n_gains, n_bias, m_attn, m_in, m_out, m_read, m_write,
    n_gains_first, n_gains_second, n_bias_first, n_bias_second, sems, *stages,
):
    width = red.shape[1]
    ins, outs = [], []
    for src, stage, dst, cuts in zip((gf_in, nm_in, gm_in, ro_in), stages, (gf, nm, gm, ro), (3, 2, 2, 1)):
        size = src.shape[0] // cuts
        for i in range(cuts):
            at, k = pl.ds(size * i, size), len(ins)
            ins.append(pltpu.make_async_copy(src.at[at], stage.at[at], sems.at[0, k]))
            outs.append(pltpu.make_async_copy(stage.at[at], dst.at[at], sems.at[1, k]))
            ins[k].start()

    def pass_on(first, last):
        for k in range(first, last):
            ins[k].wait()
            outs[k].start()

    for m in range(4):
        lanes = slice(width * m, width * (m + 1))
        at = slice(ROWS * m, ROWS * (m + 1))
        g = red[at]
        g_attn[m] = g
        m_attn[m] = 0.5 * attn_mom[m] + g
        n_attn[m] = attn[m] - xrec[at].astype(f32)
        at = slice(64 + ROWS * m, 64 + ROWS * (m + 1))
        g = red[at]
        g_in[:, lanes] = g
        m_in[:, lanes] = 0.5 * w_in_mom[:, lanes] + g
        n_in[:, lanes] = w_in[:, lanes] - xrec[at].astype(f32)
        pass_on(m, m + 1)
    g = red[128:192]
    g_out[...] = g
    m_out[...] = 0.5 * w_out_mom[...] + g
    n_out[...] = w_out[...] - 2.0 * xrec[128:192].astype(f32)
    pass_on(4, len(ins))
    small = xrec[SMALL:PACK, 0:128].astype(f32)
    n_write[...] = s_write[...] - math.sqrt(512 / 96) * small[:, 0:96]
    n_read[...] = s_read[...] - math.sqrt(512 / 16) * small[:, 96:112]
    made_write, made_read = small_grads(red, turn_gains(gains[...]))
    g_write[...] = made_write
    g_read[...] = made_read
    m_write[...] = 0.5 * s_write_mom[...] + made_write
    m_read[...] = 0.5 * s_read_mom[...] + made_read
    low_write = s_write[...].astype(bf16).astype(f32)
    low_read = s_read[...].astype(bf16).astype(f32)
    to_read = jnp.sum(low_read * red[SMALL:PACK, 96:112], axis=1, keepdims=True)
    to_write = jnp.sum(low_write * red[SMALL:PACK, 0:96], axis=1, keepdims=True)
    column = lax.broadcasted_iota(jnp.int32, (ROWS, 128), 1)
    wide = jnp.where(
        column == 112, to_read, jnp.where(column == 115, to_write, red[SMALL:PACK, 0:128])
    )
    grad_gains = wide.T[112:116]
    g_gains[...] = grad_gains
    n_gains[...], n_gains_first[...], n_gains_second[...] = adam_step(
        gains[...], gains_first[...], gains_second[...], grad_gains
    )
    grad_bias = red[SMALL : SMALL + 1, 128:192]
    g_bias[...] = grad_bias
    n_bias[...], n_bias_first[...], n_bias_second[...] = adam_step(
        bias[...], bias_first[...], bias_second[...], grad_bias
    )
    for copy in outs:
        copy.wait()


highest = lax.Precision.HIGHEST
NS = (3.4445, -4.775, 2.0315)


def canonical(attn, w_in, w_out, s_read, s_write, gains, bias):
    width = attn.shape[2]
    groups = attn.shape[1] // ROWS
    a = attn.astype(bf16).reshape(4, groups, ROWS, width).transpose(1, 0, 2, 3)
    i = w_in.astype(bf16).reshape(groups, ROWS, 4, width).transpose(0, 2, 1, 3)
    o = w_out.astype(bf16).reshape(groups, 64, width)
    s = jnp.concatenate([s_write, s_read, gains.T], axis=1).astype(bf16)
    s = jnp.pad(s, ((0, 0), (0, 128 - s.shape[1]))).reshape(groups, ROWS, 128)
    b = bias.astype(bf16).reshape(groups, 1, 64)
    b = jnp.pad(b, ((0, 0), (0, ROWS - 1), (0, width - 128 - 64)))
    return jnp.concatenate(
        [
            a.reshape(groups, 64, width),
            i.reshape(groups, 64, width),
            o,
            jnp.concatenate([s, b], axis=2),
        ],
        axis=1,
    )


def natural(pack, mem, read):
    groups, _, width = pack.shape
    a = pack[:, 0:64].reshape(groups, 4, ROWS, width).transpose(1, 0, 2, 3)
    i = pack[:, 64:128].reshape(groups, 4, ROWS, width).transpose(0, 2, 1, 3)
    s = pack[:, SMALL:PACK, 0:128].reshape(groups * ROWS, 128)
    return (
        a.reshape(4, groups * ROWS, width),
        i.reshape(groups * ROWS, 4 * width),
        pack[:, 128:192].reshape(groups * 64, width),
        s[:, 0:mem],
        s[:, mem : mem + read],
        s[:, mem + read + 1 : mem + read + 3],
        pack[:, SMALL, 128:192].reshape(groups * 64),
    )


def adam_step(weight, first, second, grad):
    first_new = 0.5 * first + 0.5 * grad
    second_new = 0.5 * second + 0.5 * grad * grad
    part = 1.0 - 0.5**10
    moved = 0.25 * (first_new / part) / (jnp.sqrt(second_new / part) + 1e-08)
    return weight - moved, first_new, second_new


def orthogonalize(matrix):
    tall = matrix.shape[0] > matrix.shape[1]
    x = matrix.T if tall else matrix
    x = x / (jnp.sqrt(jnp.sum(x * x)) + 1e-07)
    for _ in range(5):
        q = jnp.dot(x, x.T, precision=highest)
        mixed = NS[1] * q + NS[2] * jnp.dot(q, q, precision=highest)
        x = NS[0] * x + jnp.dot(mixed, x, precision=highest)
    return x.T if tall else x


def any_slice(
    frames, valid, memory, ct_memory, ct_read,
    attn, w_in, w_out, s_read, s_write, gains, bias,
    attn_mom, w_in_mom, w_out_mom, s_read_mom, s_write_mom,
    gains_first, gains_second, bias_first, bias_second,
):
    axes = ("dp", "sub")
    mem, read = memory.shape[1], ct_read.shape[1]

    def gather(v, axis):
        return lax.all_gather(v.astype(bf16), axes, axis=axis, tiled=True)

    def scatter(v, axis):
        return lax.psum_scatter(v, axes, scatter_dimension=axis, tiled=True)

    wpack = canonical(
        gather(attn, 1), gather(w_in, 0), gather(w_out, 0), gather(s_read, 0),
        gather(s_write, 0), gather(gains, 1), gather(bias, 0),
    )
    *step_outs, gpack = run_step(frames, valid, memory, ct_memory, ct_read, wpack)
    new_memory, read_out, grad_frames, grad_memory = clip_outputs(step_outs, frames.shape[0])
    sums = natural(gpack.astype(f32), mem, read)
    g_attn, g_in, g_out, sum_w, sum_r, g_two, g_bias = (
        scatter(v, axis) for v, axis in zip(sums, (1, 0, 0, 0, 0, 0, 0))
    )
    low_gain = gains.astype(bf16).astype(f32)
    low_w, low_r = s_write.astype(bf16).astype(f32), s_read.astype(bf16).astype(f32)
    g_s_write = low_gain[3][:, None] * sum_w
    g_s_read = low_gain[0][:, None] * sum_r
    g_gains = jnp.stack(
        [jnp.sum(low_r * sum_r, axis=1), g_two[:, 0], g_two[:, 1], jnp.sum(low_w * sum_w, axis=1)]
    )
    moms = (
        0.5 * attn_mom + g_attn,
        0.5 * w_in_mom + g_in,
        0.5 * w_out_mom + g_out,
        0.5 * s_read_mom + g_s_read,
        0.5 * s_write_mom + g_s_write,
    )
    whole = [gather(v, axis).astype(f32) for v, axis in zip(moms, (1, 0, 0, 0, 0))]
    matrices = [whole[0][m] for m in range(4)] + whole[1:]
    rank, count = lax.axis_index(axes), lax.axis_size(axes)
    owned = [
        lax.cond(rank == m * count // 8, orthogonalize, jnp.zeros_like, matrix)
        for m, matrix in enumerate(matrices)
    ]
    ortho = (
        scatter(jnp.stack(owned[:4]), 1), *(scatter(v, 0) for v in owned[4:])
    )
    stepped = []
    for weight, part, full in zip((attn, w_in, w_out, s_read, s_write), ortho, whole):
        ratio = max(1.0, full.shape[-2] / full.shape[-1]) ** 0.5
        stepped.append(weight - ratio * part)
    n_gains = adam_step(gains, gains_first, gains_second, g_gains)
    n_bias = adam_step(bias, bias_first, bias_second, g_bias)
    return (
        new_memory, read_out, grad_frames, grad_memory,
        g_attn, g_in, g_out, g_s_read, g_s_write, g_gains, g_bias,
        *stepped, n_gains[0], n_bias[0], *moms, n_gains[1], n_gains[2], n_bias[1], n_bias[2],
    )


def this_slice(
    frames, valid, memory, ct_memory, ct_read,
    attn, w_in, w_out, s_read, s_write, gains, bias,
    attn_mom, w_in_mom, w_out_mom, s_read_mom, s_write_mom,
    gains_first, gains_second, bias_first, bias_second,
):
    inside, anywhere = pl.BlockSpec(memory_space=pltpu.VMEM), pl.BlockSpec(memory_space=pl.ANY)

    def like(*arrays):
        return tuple(jax.ShapeDtypeStruct(a.shape, f32) for a in arrays)

    def row(v):
        return v.reshape(1, -1)

    moms = (attn_mom, w_in_mom, w_out_mom, s_read_mom, s_write_mom)
    weights = (attn, w_in, w_out, s_read, s_write)
    *step_outs, red, xrec = run_step(
        frames, valid, memory, ct_memory, ct_read, None, (*weights, gains, row(bias)), (*moms, gains)
    )
    biases = (row(bias), row(bias_first), row(bias_second))
    made = pl.pallas_call(
        finish_kernel,
        out_shape=(
            *(jax.ShapeDtypeStruct(v.shape, bf16) for v in step_outs),
            *like(*weights, gains, biases[0]),
            *like(*weights, gains, biases[0]),
            *like(*moms, gains, gains, biases[0], biases[0]),
        ),
        in_specs=[inside] * 18 + [anywhere] * 4,
        out_specs=(anywhere,) * 4 + (inside,) * 23,
        scratch_shapes=[
            pltpu.SemaphoreType.DMA((2, 9)), *(pltpu.VMEM(step_outs[i].shape, bf16) for i in (2, 0, 3, 1)),
        ],
        compiler_params=pltpu.CompilerParams(vmem_limit_bytes=VMEM_LIMIT),
        name="finish",
    )(red, xrec, *weights, *moms, gains, gains_first, gains_second, *biases, *step_outs)
    flat = bias.shape
    return tuple(
        v.reshape(flat) if v.shape == biases[0].shape else v
        for v in (*clip_outputs(made[:4], frames.shape[0]), *made[4:])
    )


def solution(mesh):
    both = ("dp", "sub")
    rows3, rows2, rows1 = P(both, None, None), P(both, None), P(both)
    mid, last = P(None, both, None), P(None, both)
    weights = (mid, rows2, rows2, rows2, rows2)
    here = (mesh.shape["dp"], mesh.shape["sub"]) == (8, 4)
    return jax.shard_map(
        this_slice if here else any_slice,
        mesh=mesh,
        in_specs=(
            rows3, rows2, rows3, rows3, rows3, *weights, last, rows1, *weights, last, last, rows1, rows1,
        ),
        out_specs=(
            rows3, rows3, rows3, rows3, *weights, last, rows1, *weights, last, rows1, *weights,
            last, last, rows1, rows1,
        ),
        check_vma=False,
    )
```
